32 devices in a mesh: dp: 16 (over z, x, core), seq: 2 (over y).
Axes of the slice: x: 2, y: 2, z: 4, core: 2. Of those that a mesh axis runs over, the one named last changes fastest.
Arguments:
- tokens: bfloat16 [16, 16, 256, 512], P('dp', None, 'seq'), may hold values from -6 to 6
- lengths: int32 [16, 2, 3], P('dp'), may hold values from 1 to 5, 8 in all within a row
- cotangent: bfloat16 [16, 16, 256, 512], P('dp', None, 'seq'), may hold values from -8 to 8
- norm_gain: bfloat16 [2, 2, 512], P(None, None, ('dp', 'seq')), may hold values from 0.25 to 1.75
- norm_bias: bfloat16 [2, 2, 512], P(None, None, ('dp', 'seq')), may hold values from -3 to 3
- w_qkv: bfloat16 [2, 512, 1536], P(None, ('dp', 'seq')), may hold values from -0.25 to 0.25
- w_proj: bfloat16 [2, 512, 512], P(None, ('dp', 'seq')), may hold values from -0.75 to 0.75
- w_in: bfloat16 [2, 512, 2048], P(None, ('dp', 'seq')), may hold values from -0.25 to 0.25
- b_in: bfloat16 [2, 2048], P(None, ('dp', 'seq')), may hold values from -3 to 3
- w_out: bfloat16 [2, 2048, 512], P(None, ('dp', 'seq')), may hold values from -0.125 to 0.125
Outputs:
- activations: bfloat16 [16, 16, 256, 512], P('dp', None, 'seq')
- grad_tokens: bfloat16 [16, 16, 256, 512], P('dp', None, 'seq')
- grad_norm_gain: float32 [2, 2, 512], P(None, None, ('dp', 'seq'))
- grad_norm_bias: float32 [2, 2, 512], P(None, None, ('dp', 'seq'))
- grad_w_qkv: float32 [2, 512, 1536], P(None, ('dp', 'seq'))
- grad_w_proj: float32 [2, 512, 512], P(None, ('dp', 'seq'))
- grad_w_in: float32 [2, 512, 2048], P(None, ('dp', 'seq'))
- grad_b_in: float32 [2, 2048], P(None, ('dp', 'seq'))
- grad_w_out: float32 [2, 2048, 512], P(None, ('dp', 'seq'))
The draws below stay inside these ranges and needn't reach their ends.
Inputs may be any that keep to these rules, and one draw needn't show every extreme that they name: In each group, the 3 clip lengths of each of the 2 micro-batches sum to 8; in each micro-batch the longest clip has exactly 5 steps.
All inputs are finite; a program needn't handle non-finite values.
Results may differ from the reference program's by a relative error of at most 0.017.
Values may be sent and summed in bfloat16 or wider, within the bound.
No kernel may reach another device: no remote copies, remote signals or barrier semaphores. Data moves between devices by JAX's collectives and lax.ppermute only.
A program may use at most 320 MiB of HBM per device.

```python
import math
import jax
import jax.numpy as jnp
import numpy as np
from jax import lax

D = 512
HEADS = 8
FF = 2048
PATCHES = 256
BLOCKS = 2
MICRO = 2
STEPS_MB = 8
CLIPS = 3
MOST = 5
GROUPS = 16
STEPS = 16


def strengthened(values, own_key, source, target, parts, factor):
    owner, partner = [(jnp.arange(values.shape[position]) // (values.shape[position] // parts)).reshape([-1 if axis == position else 1 for axis in range(values.ndim)]) for position in (source, target)]
    chosen = jax.random.permutation(own_key, parts)[partner]
    strong = (owner == chosen) | (owner == (partner + parts // 2) % parts)
    return jnp.where(strong, factor * values, values)


def levels(own_key, shape, pieces, low, high):
    level, own = 1.0, jax.random.fold_in(own_key, 6)
    for position, parts in pieces:
        heights = jnp.exp(jax.random.uniform(jax.random.fold_in(own, position), (parts,), jnp.float32, low / len(pieces), high / len(pieces)))
        level = level * jnp.repeat(heights, shape[position] // parts).reshape([-1 if axis == position else 1 for axis in range(len(shape))])
    return level


def length_profile(amount, total, reach, slope):
    loads = [(1 << 20) // math.isqrt(standing ** slope) + 1 for standing in range(2, amount + 1)]
    surplus, counts = total - reach - (amount - 1), [1] * (amount - 1)
    while surplus > 0:
        free = [i for i in range(amount - 1) if counts[i] < reach]
        mass, left = sum([loads[i] for i in free]), surplus
        for i in free:
            extra = min(reach - counts[i], max(1, left * loads[i] // mass), surplus)
            counts[i] = counts[i] + extra
            surplus = surplus - extra
    return np.array([reach] + counts)


def ragged_sizes(own_key, count, total, reach, lean):
    if count == 2:
        one = jax.random.randint(own_key, (), max(1, total - reach), min(reach, total - 1) + 1)
        return jnp.stack([one, total - one])
    sizes = jnp.asarray(length_profile(count, total, reach, lean), jnp.int32)
    pairs = (count - 1) // 2
    giver, sink = sizes[1:1 + 2 * pairs:2], sizes[2:2 + 2 * pairs:2]
    margin = jnp.minimum(giver - 1, reach - sink)
    passed = jax.random.randint(jax.random.fold_in(own_key, 1), (pairs,), 0, 1 << 20) % (margin + 1)
    sizes = sizes.at[1:1 + 2 * pairs:2].set(giver - passed).at[2:2 + 2 * pairs:2].set(sink + passed)
    return sizes[jax.random.permutation(jax.random.fold_in(own_key, 2), count)]


def scatter_about(stream_key, dims, width, limit, shards=(), held_as=jnp.bfloat16):
    result = width * jax.random.normal(stream_key, dims, jnp.float32)
    if shards:
        result = result * levels(stream_key, dims, shards, -0.22, 0.18)
    return jnp.clip(result, -limit, limit).astype(held_as)


def bell_draw_with(stream_key, dims, scale, reach, split, heavy, held_as=jnp.bfloat16):
    array = scale * jax.random.normal(stream_key, dims, jnp.float32)
    if split:
        array = array * levels(stream_key, dims, split, -0.22, 0.18)
    return jnp.clip(strengthened(array, jax.random.fold_in(stream_key, 3), *heavy), -reach, reach).astype(held_as)


def setup_inputs(seed: int = 0) -> dict:
    key_list = jax.random.split(jax.random.key(seed), 11)
    tokens = scatter_about(key_list[0], (GROUPS, STEPS, PATCHES, D), 1.0, 6.0, ((0, 16), (2, 2)))
    lengths = jax.vmap(lambda own: ragged_sizes(own, CLIPS, STEPS_MB, MOST, 2))(jax.random.split(key_list[1], GROUPS * MICRO)).reshape((GROUPS, MICRO, CLIPS)).astype(jnp.int32)
    cotangent = bell_draw_with(key_list[2], (GROUPS, STEPS, PATCHES, D), 1.0, 8.0, ((0, 16), (2, 2)), (0, 3, 16, 2.0))
    norm_gain = jnp.clip(1.0 + 0.15 * jax.random.normal(key_list[3], (BLOCKS, 2, D), jnp.float32), 0.25, 1.75).astype(jnp.bfloat16)
    norm_bias = scatter_about(key_list[4], (BLOCKS, 2, D), 0.5, 3.0, ((2, 32),))
    w_qkv = scatter_about(key_list[5], (BLOCKS, D, 3 * D), D ** -0.5, 0.25, ((1, 32),))
    w_proj = scatter_about(key_list[6], (BLOCKS, D, D), (D // 8) ** -0.5, 0.75, ((1, 32),))
    w_in = scatter_about(key_list[7], (BLOCKS, D, FF), D ** -0.5, 0.25, ((1, 32),))
    b_in = scatter_about(key_list[8], (BLOCKS, FF), 0.5, 3.0, ((1, 32),))
    w_out = scatter_about(key_list[9], (BLOCKS, FF, D), FF ** -0.5, 0.125, ((1, 32),))
    return dict(tokens=tokens, lengths=lengths, cotangent=cotangent, norm_gain=norm_gain, norm_bias=norm_bias, w_qkv=w_qkv, w_proj=w_proj, w_in=w_in, b_in=b_in, w_out=w_out)


@jax.custom_vjp
def low(v):
    return lax.optimization_barrier(v.astype(jnp.bfloat16)).astype(jnp.float32)

@jax.custom_vjp
def low_back(v):
    return v

def low_keep(v):
    return (low(v), None)

def low_pass(kept, grad):
    return (grad,)

def back_keep(v):
    return (v, None)

def back_low(kept, grad):
    return (low(grad),)
low.defvjp(low_keep, low_pass)
low_back.defvjp(back_keep, back_low)
highest = lax.Precision.HIGHEST

def matmul_high(left_rows, matrix):
    return jnp.einsum('...k,kn->...n', left_rows, matrix, precision=highest, preferred_element_type=jnp.float32)

def layer_norm(values, gain_row, shift_row):
    centre = values - lax.optimization_barrier(jnp.mean(values, -1, keepdims=True))
    variance = lax.optimization_barrier(jnp.mean(centre * centre, -1, keepdims=True))
    return centre * lax.rsqrt(variance + 1e-05) * gain_row + shift_row

def gelu_smooth(values):
    return 0.5 * values * (1.0 + lax.erf(values * 0.7071067811865476))

def softmax_rows(scores):
    shifted = scores - lax.optimization_barrier(jnp.max(scores, -1, keepdims=True))
    exponent = jnp.exp(shifted)
    return exponent / lax.optimization_barrier(jnp.sum(exponent, -1, keepdims=True))

def attend(queries, key_rows, values, spatial, allowed):
    scale_factor = queries.shape[-1] ** (-0.5)
    if spatial:
        scores = jnp.einsum('tphe,tqhe->thpq', queries, key_rows, precision=highest) * scale_factor
        scores = low_back(scores)
        attn_prob = low(softmax_rows(scores))
        return jnp.einsum('thpq,tqhe->tphe', attn_prob, values, precision=highest)
    scores = jnp.einsum('tphe,sphe->phts', queries, key_rows, precision=highest) * scale_factor
    scores = low_back(scores)
    scores = jnp.where(allowed, scores, -1000000000.0)
    attn_prob = low(softmax_rows(scores))
    return jnp.einsum('phts,sphe->tphe', attn_prob, values, precision=highest)

def block_pass(values, block_params, spatial, allowed):
    gain_pair, shift_pair, qkv_matrix, proj_matrix, in_matrix, in_bias, out_matrix = block_params
    steps_n, patches_n, model_width = values.shape
    normed = low(layer_norm(values, gain_pair[0], shift_pair[0]))
    mixed_qkv = low(low_back(matmul_high(normed, qkv_matrix)))
    parts_qkv = mixed_qkv.reshape(steps_n, patches_n, 3, HEADS, model_width // HEADS)
    attended = attend(parts_qkv[:, :, 0], parts_qkv[:, :, 1], parts_qkv[:, :, 2], spatial, allowed)
    attended = low(low_back(attended)).reshape(steps_n, patches_n, model_width)
    middle = values + low_back(matmul_high(attended, proj_matrix))
    normed_two = low(layer_norm(middle, gain_pair[1], shift_pair[1]))
    pre_act = low_back(matmul_high(normed_two, in_matrix) + in_bias)
    hidden = low(gelu_smooth(pre_act))
    return middle + low_back(matmul_high(hidden, out_matrix))

def clip_mask(lengths_group):
    step_ids = jnp.arange(STEPS, dtype=jnp.int32)
    micro_ids = step_ids // STEPS_MB
    within = step_ids % STEPS_MB
    clip_ends = jnp.cumsum(lengths_group, -1).astype(jnp.int32)
    clip_ids = lax.optimization_barrier(jnp.sum((within[:, None] >= clip_ends[micro_ids]).astype(jnp.int32), -1))
    segment = micro_ids * CLIPS + clip_ids
    same_clip = segment[:, None] == segment[None, :]
    return same_clip & (step_ids[None, :] <= step_ids[:, None])

def forward(values, params, allowed):
    for block_idx in range(BLOCKS):
        block_params = tuple((array_item[block_idx] for array_item in params))
        values = block_pass(values, block_params, block_idx % 2 == 0, allowed)
    return values

def reference(tokens, lengths, cotangent, norm_gain, norm_bias, w_qkv, w_proj, w_in, b_in, w_out):
    params = tuple((array_item.astype(jnp.float32) for array_item in (norm_gain, norm_bias, w_qkv, w_proj, w_in, b_in, w_out)))
    zero_sums = tuple((jnp.zeros(array_item.shape, jnp.float32) for array_item in params))

    def one_group(totals, group_data):
        tokens_group, lengths_group, cotangent_group = group_data
        allowed = clip_mask(lengths_group)

        def group_forward(values, weights):
            return forward(values, weights, allowed)
        output, pullback = jax.vjp(group_forward, tokens_group.astype(jnp.float32), params)
        grad_values, grad_params = pullback(cotangent_group.astype(jnp.float32))
        totals = tuple((left_sum + right_sum for left_sum, right_sum in zip(totals, grad_params)))
        return (totals, (output.astype(jnp.bfloat16), grad_values.astype(jnp.bfloat16)))
    totals, results = lax.scan(one_group, zero_sums, (tokens, lengths, cotangent))
    return (results[0], results[1], totals[0], totals[1], totals[2], totals[3], totals[4], totals[5], totals[6])
```

```python
import functools

import jax
import jax.numpy as jnp
from jax import lax
from jax.experimental import pallas as pl
from jax.experimental.pallas import tpu as pltpu
from jax.sharding import PartitionSpec as P

HEADS = 8
MICRO = 2
LANES = 128
AXES = ("dp", "seq")
BF = jnp.bfloat16
F32 = jnp.float32
MIB = 1 << 20
FROM_A, FROM_B, TO_A, TO_B = range(4)


def dot(left, right, left_dim, right_dim):
    return lax.dot_general(
        left, right, (((left_dim,), (right_dim,)), ((), ())), preferred_element_type=F32
    )


def norm_stats(values):
    centre = values - jnp.mean(values, -1, keepdims=True)
    variance = jnp.mean(centre * centre, -1, keepdims=True)
    inverse = lax.rsqrt(variance + 1e-05)
    return centre * inverse, inverse


def norm_back(grad_scaled, unit_rows, inverse):
    mean_grad = jnp.mean(grad_scaled, -1, keepdims=True)
    mean_cross = jnp.mean(grad_scaled * unit_rows, -1, keepdims=True)
    return inverse * (grad_scaled - mean_grad - unit_rows * mean_cross)


def fold_rows(values):
    return jnp.sum(values.reshape(-1, 8, values.shape[-1]), 0)


def gelu_pair(values):
    cumulative = 0.5 * (1.0 + lax.erf(values * 0.7071067811865476))
    slope = cumulative + values * jnp.exp(-0.5 * values * values) * 0.3989422804014327
    return values * cumulative, slope


def start_weight(pieces, table_ref, which, held, sem):
    slab = 0
    for piece in pieces:
        rows = piece.shape[1]
        for idx in range(piece.shape[0]):
            first = pl.multiple_of(table_ref[which, slab] * rows, rows)
            pltpu.make_async_copy(piece.at[idx], held.at[pl.ds(first, rows)], sem).start()
            slab += 1


def wait_weight(held, sem):
    pltpu.make_async_copy(held, held, sem).wait()


def start_slabs(staged, table_ref, which, out, sem):
    rows = out.shape[1]
    for idx in range(out.shape[0]):
        first = pl.multiple_of(table_ref[which, idx] * rows, rows)
        pltpu.make_async_copy(staged.at[pl.ds(first, rows)], out.at[idx], sem).start()


def wait_slabs(out, sem):
    pltpu.make_async_copy(out, out, sem).wait()


def head_rows(head, width, value):
    lane = lax.broadcasted_iota(jnp.int32, (1, LANES), 1)
    inside = (lane >= head * width) & (lane < (head + 1) * width)
    return jnp.where(inside, value, 0.0).astype(BF)


def merge_heads(parts, width):
    lane = lax.broadcasted_iota(jnp.int32, (1, LANES), 1)
    merged = parts[-1]
    for head in range(len(parts) - 2, -1, -1):
        merged = jnp.where(lane < (head + 1) * width, parts[head], merged)
    return merged


def attend_forward(load, model, store, keep, bias):
    width = model // HEADS
    each = LANES // width
    scale = width ** (-0.5)
    for pair in range(model // LANES):
        first = pair * LANES
        queries = load(first)
        key_rows = load(model + first)
        values = load(2 * model + first)
        parts = []
        for sub in range(each):
            scores = dot(key_rows, queries * head_rows(sub, width, scale), 1, 1)
            if bias is not None:
                scores = scores + bias
            exponent = jnp.exp(scores - jnp.max(scores, 0, keepdims=True))
            prob = (exponent * (1.0 / jnp.sum(exponent, 0, keepdims=True))).astype(BF)
            keep(pair * each + sub, prob)
            parts.append(dot(prob, values, 0, 0))
        store(first, merge_heads(parts, width).astype(BF))


def attend_backward(load, load_grad, load_prob, model, store):
    width = model // HEADS
    each = LANES // width
    scale = width ** (-0.5)
    for pair in range(model // LANES):
        first = pair * LANES
        queries = load(first)
        key_rows = load(model + first)
        values = load(2 * model + first)
        grad_out = load_grad(first)
        scaled_q = queries * jnp.asarray(scale, BF)
        scaled_k = key_rows * jnp.asarray(scale, BF)
        grad_q, grad_k, grad_v = [], [], []
        for sub in range(each):
            prob = load_prob(pair * each + sub)
            grad_prob = dot(values, grad_out * head_rows(sub, width, 1.0), 1, 1)
            prob_wide = prob.astype(F32)
            total = jnp.sum(prob_wide * grad_prob, 0, keepdims=True)
            grad_scores = (prob_wide * (grad_prob - total)).astype(BF)
            grad_v.append(dot(prob, grad_out, 1, 0))
            grad_k.append(dot(grad_scores, scaled_q, 1, 0))
            grad_q.append(dot(grad_scores, scaled_k, 0, 0))
        store(first, merge_heads(grad_q, width).astype(BF))
        store(model + first, merge_heads(grad_k, width).astype(BF))
        store(2 * model + first, merge_heads(grad_v, width).astype(BF))


def spatial_forward_kernel(counts, table_ref, *refs):
    n_qkv, n_proj = counts
    qkv_pieces, refs = refs[:n_qkv], refs[n_qkv:]
    proj_pieces, refs = refs[:n_proj], refs[n_proj:]
    (
        own_ref,
        other_ref,
        vec_ref,
        middle_ref,
        qkv_ref,
        attended_ref,
        prob_ref,
        w_qkv,
        w_proj,
        sems,
    ) = refs
    frames, half, model = own_ref.shape

    @pl.when(pl.program_id(0) == 0)
    def _():
        start_weight(qkv_pieces, table_ref, FROM_A, w_qkv, sems.at[0])
        start_weight(proj_pieces, table_ref, FROM_A, w_proj, sems.at[1])
        wait_weight(w_qkv, sems.at[0])
        wait_weight(w_proj, sems.at[1])

    rows = jnp.concatenate([own_ref[...], other_ref[...]], 1).astype(F32)
    rows = rows.reshape(frames * 2 * half, model)
    unit, _ = norm_stats(rows)
    normed = (unit * vec_ref[0:1] + vec_ref[1:2]).astype(BF)
    qkv_ref[...] = dot(normed, w_qkv[...], 1, 0).astype(BF).reshape(qkv_ref.shape)
    for frame in range(frames):

        def load(first):
            return qkv_ref[frame, :, first : first + LANES]

        def store(first, value):
            attended_ref[frame, :, first : first + LANES] = value

        def keep(head, value):
            prob_ref[frame, head] = value

        attend_forward(load, model, store, keep, None)
    attended = attended_ref[...].reshape(rows.shape)
    middle = rows + dot(attended, w_proj[...], 1, 0)
    middle_ref[...] = middle.reshape(middle_ref.shape)


def feed_forward_kernel(counts, table_ref, *refs):
    n_in, n_out = counts
    in_pieces, refs = refs[:n_in], refs[n_in:]
    out_pieces, refs = refs[:n_out], refs[n_out:]
    (
        middle_ref,
        vec_ref,
        b_in_ref,
        result_ref,
        hidden_ref,
        slope_ref,
        w_in,
        w_out,
        sems,
    ) = refs

    @pl.when(pl.program_id(0) == 0)
    def _():
        start_weight(in_pieces, table_ref, FROM_A, w_in, sems.at[0])
        start_weight(out_pieces, table_ref, FROM_B, w_out, sems.at[1])
        wait_weight(w_in, sems.at[0])
        wait_weight(w_out, sems.at[1])

    middle = middle_ref[...]
    unit, _ = norm_stats(middle)
    normed = (unit * vec_ref[2:3] + vec_ref[3:4]).astype(BF)
    result_ref[...] = middle + ff_through(normed, b_in_ref, w_in, w_out, hidden_ref, slope_ref)


def ff_through(normed, b_in_ref, w_in, w_out, hidden_ref, slope_ref):
    width = w_in.shape[1]
    chunk = min(512, width)
    total = None
    for first in range(0, width, chunk):
        cols = slice(first, first + chunk)
        pre_act = dot(normed, w_in[:, cols], 1, 0) + b_in_ref[:, cols]
        hidden, slope = gelu_pair(pre_act)
        hidden = hidden.astype(BF)
        hidden_ref[:, cols] = hidden
        slope_ref[:, cols] = slope.astype(BF)
        term = dot(hidden, w_out[cols, :], 1, 0)
        total = term if total is None else total + term
    return total


def ff_back(grad_out, normed, unit, inverse, gain, w_in, w_out, hidden_ref, slope_ref, sums):
    acc_in, acc_out, small_ref = sums
    model, width = w_in.shape
    chunk = min(512, width)
    branch = grad_out.astype(BF)
    grad_second = None
    for first in range(0, width, chunk):
        cols = slice(first, first + chunk)
        grad_hidden = dot(branch, w_out[cols, :], 1, 1)
        grad_pre = (grad_hidden * slope_ref[:, cols].astype(F32)).astype(BF)
        small_ref[:, 2 * model + first : 2 * model + first + chunk] += fold_rows(
            grad_pre.astype(F32)
        )
        acc_out[cols, :] += dot(hidden_ref[:, cols], branch, 0, 0)
        acc_in[:, cols] += dot(normed, grad_pre, 0, 0)
        term = dot(grad_pre, w_in[:, cols], 1, 1)
        grad_second = term if grad_second is None else grad_second + term
    small_ref[:, :model] += fold_rows(grad_second * unit)
    small_ref[:, model : 2 * model] += fold_rows(grad_second)
    return grad_out + norm_back(grad_second * gain, unit, inverse)


def feed_backward_kernel(counts, table_ref, *refs):
    n_in, n_out = counts
    in_pieces, refs = refs[:n_in], refs[n_in:]
    out_pieces, refs = refs[:n_out], refs[n_out:]
    (
        grad_ref,
        middle_ref,
        hidden_ref,
        slope_ref,
        vec_ref,
        grad_middle_ref,
        small_ref,
        grad_in_out,
        grad_out_out,
        w_in,
        w_out,
        acc_in,
        acc_out,
        sems,
    ) = refs

    @pl.when(pl.program_id(0) == 0)
    def _():
        start_weight(in_pieces, table_ref, FROM_A, w_in, sems.at[0])
        start_weight(out_pieces, table_ref, FROM_B, w_out, sems.at[1])
        acc_in[...] = jnp.zeros_like(acc_in)
        acc_out[...] = jnp.zeros_like(acc_out)
        small_ref[...] = jnp.zeros_like(small_ref)
        wait_weight(w_in, sems.at[0])
        wait_weight(w_out, sems.at[1])

    unit, inverse = norm_stats(middle_ref[...])
    normed = (unit * vec_ref[2:3] + vec_ref[3:4]).astype(BF)
    grad_middle_ref[...] = ff_back(
        grad_ref[...],
        normed,
        unit,
        inverse,
        vec_ref[2:3],
        w_in,
        w_out,
        hidden_ref,
        slope_ref,
        (acc_in, acc_out, small_ref),
    )

    @pl.when(pl.program_id(0) == pl.num_programs(0) - 1)
    def _():
        w_out[...] = acc_out[...].astype(BF)
        start_slabs(w_out, table_ref, TO_B, grad_out_out, sems.at[1])
        w_in[...] = acc_in[...].astype(BF)
        start_slabs(w_in, table_ref, TO_A, grad_in_out, sems.at[0])
        wait_slabs(grad_out_out, sems.at[1])
        wait_slabs(grad_in_out, sems.at[0])


def spatial_backward_kernel(counts, table_ref, *refs):
    n_qkv, n_proj = counts
    qkv_pieces, refs = refs[:n_qkv], refs[n_qkv:]
    proj_pieces, refs = refs[:n_proj], refs[n_proj:]
    (
        grad_ref,
        own_ref,
        other_ref,
        qkv_ref,
        attended_ref,
        prob_ref,
        vec_ref,
        grad_own_ref,
        grad_other_ref,
        small_ref,
        grad_qkv_out,
        grad_proj_out,
        w_qkv,
        w_proj,
        acc_qkv,
        acc_proj,
        grad_att,
        grad_mixed,
        sems,
    ) = refs
    frames, half, model = own_ref.shape

    @pl.when(pl.program_id(0) == 0)
    def _():
        start_weight(qkv_pieces, table_ref, FROM_A, w_qkv, sems.at[0])
        start_weight(proj_pieces, table_ref, FROM_A, w_proj, sems.at[1])
        acc_qkv[...] = jnp.zeros_like(acc_qkv)
        acc_proj[...] = jnp.zeros_like(acc_proj)
        small_ref[...] = jnp.zeros_like(small_ref)
        wait_weight(w_qkv, sems.at[0])
        wait_weight(w_proj, sems.at[1])

    rows = jnp.concatenate([own_ref[...], other_ref[...]], 1).astype(F32)
    rows = rows.reshape(frames * 2 * half, model)
    unit, inverse = norm_stats(rows)
    normed = (unit * vec_ref[0:1] + vec_ref[1:2]).astype(BF)
    grad_middle = grad_ref[...].reshape(rows.shape)
    proj_in = grad_middle.astype(BF)
    acc_proj[...] += dot(attended_ref[...].reshape(rows.shape), proj_in, 0, 0)
    grad_att[...] = dot(proj_in, w_proj[...], 1, 1).astype(BF)
    for frame in range(frames):
        frame_rows = slice(frame * 2 * half, (frame + 1) * 2 * half)

        def load(first):
            return qkv_ref[frame, :, first : first + LANES]

        def load_grad(first):
            return grad_att[frame_rows, first : first + LANES]

        def load_prob(head):
            return prob_ref[frame, head]

        def store(first, value):
            grad_mixed[frame_rows, first : first + LANES] = value

        attend_backward(load, load_grad, load_prob, model, store)
    acc_qkv[...] += dot(normed, grad_mixed[...], 0, 0)
    grad_first = dot(grad_mixed[...], w_qkv[...], 1, 1)
    small_ref[:, :model] += fold_rows(grad_first * unit)
    small_ref[:, model : 2 * model] += fold_rows(grad_first)
    grad_rows = grad_middle + norm_back(grad_first * vec_ref[0:1], unit, inverse)
    grad_rows = grad_rows.astype(BF).reshape(frames, 2 * half, model)
    grad_own_ref[...] = grad_rows[:, :half]
    grad_other_ref[...] = grad_rows[:, half:]

    @pl.when(pl.program_id(0) == pl.num_programs(0) - 1)
    def _():
        w_qkv[...] = acc_qkv[...].astype(BF)
        start_slabs(w_qkv, table_ref, TO_A, grad_qkv_out, sems.at[0])
        w_proj[...] = acc_proj[...].astype(BF)
        start_slabs(w_proj, table_ref, TO_A, grad_proj_out, sems.at[1])
        wait_slabs(grad_qkv_out, sems.at[0])
        wait_slabs(grad_proj_out, sems.at[1])


def temporal_kernel(counts, tile, table_ref, *refs):
    groups = []
    for count in counts:
        groups.append(refs[:count])
        refs = refs[count:]
    (
        rows_ref,
        own_ref,
        other_ref,
        vec_ref,
        b_in_ref,
        bias_ref,
        active_ref,
        grad_ref,
        small_ref,
        grad_qkv_out,
        grad_proj_out,
        grad_in_out,
        grad_out_out,
        w_qkv,
        w_proj,
        w_in,
        w_out,
        acc_qkv,
        acc_proj,
        acc_in,
        acc_out,
        mixed,
        attended,
        probs,
        hidden,
        slope,
        grad_att,
        grad_mixed,
        sems,
    ) = refs
    steps, patches, model = rows_ref.shape
    tiles = patches // tile
    held = (w_qkv, w_proj, w_in, w_out)
    totals = (acc_qkv, acc_proj, acc_in, acc_out)

    @pl.when(pl.program_id(0) == 0)
    def _():
        for idx in range(4):
            start_weight(groups[idx], table_ref, FROM_A, held[idx], sems.at[idx])
        for total in totals:
            total[...] = jnp.zeros_like(total)
        small_ref[...] = jnp.zeros_like(small_ref)
        for idx in range(4):
            wait_weight(held[idx], sems.at[idx])

    def gather_rows(ref):
        parts = [
            ref[:, idx * tile : (idx + 1) * tile, :].reshape(steps * tile, model)
            for idx in range(tiles)
        ]
        return jnp.concatenate(parts, 0)

    def spread_rows(ref, values):
        for idx in range(tiles):
            part = values[idx * steps * tile : (idx + 1) * steps * tile]
            ref[:, idx * tile : (idx + 1) * tile, :] = part.reshape(steps, tile, model).astype(
                ref.dtype
            )

    rows = gather_rows(rows_ref)
    unit_one, inverse_one = norm_stats(rows)
    normed_one = (unit_one * vec_ref[0:1] + vec_ref[1:2]).astype(BF)
    mixed[...] = dot(normed_one, w_qkv[...], 1, 0).astype(BF)
    span = steps * tile
    bias = bias_ref[...]
    for idx in range(tiles):
        tile_rows = slice(idx * span, (idx + 1) * span)

        def load(first):
            return mixed[tile_rows, first : first + LANES]

        def store(first, value):
            attended[tile_rows, first : first + LANES] = value

        def keep(head, value):
            probs[idx, head] = value

        attend_forward(load, model, store, keep, bias)
    middle = rows + dot(attended[...], w_proj[...], 1, 0)
    unit_two, inverse_two = norm_stats(middle)
    normed_two = (unit_two * vec_ref[2:3] + vec_ref[3:4]).astype(BF)
    result = middle + ff_through(normed_two, b_in_ref, w_in, w_out, hidden, slope)
    spread_rows(active_ref, result)

    from_own = pl.program_id(0) < pl.num_programs(0) // 2
    cotangent = jnp.where(from_own, own_ref[...], other_ref[...])
    grad_out = gather_rows(cotangent).astype(F32)
    grad_middle = ff_back(
        grad_out,
        normed_two,
        unit_two,
        inverse_two,
        vec_ref[2:3],
        w_in,
        w_out,
        hidden,
        slope,
        (acc_in, acc_out, small_ref),
    )
    proj_in = grad_middle.astype(BF)
    acc_proj[...] += dot(attended[...], proj_in, 0, 0)
    grad_att[...] = dot(proj_in, w_proj[...], 1, 1).astype(BF)
    for idx in range(tiles):
        tile_rows = slice(idx * span, (idx + 1) * span)

        def load(first):
            return mixed[tile_rows, first : first + LANES]

        def load_grad(first):
            return grad_att[tile_rows, first : first + LANES]

        def load_prob(head):
            return probs[idx, head]

        def store(first, value):
            grad_mixed[tile_rows, first : first + LANES] = value

        attend_backward(load, load_grad, load_prob, model, store)
    acc_qkv[...] += dot(normed_one, grad_mixed[...], 0, 0)
    grad_first = dot(grad_mixed[...], w_qkv[...], 1, 1)
    offset = 2 * model + w_in.shape[1]
    small_ref[:, offset : offset + model] += fold_rows(grad_first * unit_one)
    small_ref[:, offset + model : offset + 2 * model] += fold_rows(grad_first)
    spread_rows(
        grad_ref, grad_middle + norm_back(grad_first * vec_ref[0:1], unit_one, inverse_one)
    )

    @pl.when(pl.program_id(0) == pl.num_programs(0) - 1)
    def _():
        outs = (grad_qkv_out, grad_proj_out, grad_in_out, grad_out_out)
        places = (TO_B, TO_B, TO_A, TO_B)
        for idx in range(4):
            held[idx][...] = totals[idx][...].astype(BF)
            start_slabs(held[idx], table_ref, places[idx], outs[idx], sems.at[idx])
        for idx in range(4):
            wait_slabs(outs[idx], sems.at[idx])


ANY = pl.BlockSpec(memory_space=pl.ANY)
SMEM = pl.BlockSpec(memory_space=pltpu.SMEM)


def whole(shape):
    return pl.BlockSpec(shape, lambda idx: (0,) * len(shape))


def leading(shape):
    return pl.BlockSpec(shape, lambda idx: (idx,) + (0,) * (len(shape) - 1))


def limits(megabytes):
    return pltpu.CompilerParams(vmem_limit_bytes=megabytes * MIB)


def cost(flops, bytes_accessed):
    return pl.CostEstimate(flops=flops, bytes_accessed=bytes_accessed, transcendentals=0)


def spatial_forward(table, qkv_pieces, proj_pieces, own, other, vec):
    frames, half, model = own.shape
    patches = 2 * half
    each = min(2, frames)
    shape = jax.ShapeDtypeStruct
    return pl.pallas_call(
        functools.partial(spatial_forward_kernel, (len(qkv_pieces), len(proj_pieces))),
        grid=(frames // each,),
        in_specs=[SMEM]
        + [ANY] * (len(qkv_pieces) + len(proj_pieces))
        + [leading((each, half, model))] * 2
        + [whole(vec.shape)],
        out_specs=[
            leading((each, patches, model)),
            leading((each, patches, 3 * model)),
            leading((each, patches, model)),
            leading((each, HEADS, patches, patches)),
        ],
        out_shape=[
            shape((frames, patches, model), F32),
            shape((frames, patches, 3 * model), BF),
            shape((frames, patches, model), BF),
            shape((frames, HEADS, patches, patches), BF),
        ],
        scratch_shapes=[
            pltpu.VMEM((model, 3 * model), BF),
            pltpu.VMEM((model, model), BF),
            pltpu.SemaphoreType.DMA((2,)),
        ],
        compiler_params=limits(48),
        cost_estimate=cost(
            2 * frames * patches * model * (4 * model + 2 * patches), frames * patches * model * 24
        ),
        name="spatial_forward",
    )(table, *qkv_pieces, *proj_pieces, own, other, vec)


def feed_forward(table, in_pieces, out_pieces, middle, vec, b_in):
    tokens, model = middle.shape
    width = b_in.shape[1]
    block = min(512, tokens)
    shape = jax.ShapeDtypeStruct
    return pl.pallas_call(
        functools.partial(feed_forward_kernel, (len(in_pieces), len(out_pieces))),
        grid=(tokens // block,),
        in_specs=[SMEM]
        + [ANY] * (len(in_pieces) + len(out_pieces))
        + [leading((block, model)), whole(vec.shape), whole(b_in.shape)],
        out_specs=[leading((block, model)), leading((block, width)), leading((block, width))],
        out_shape=[
            shape((tokens, model), F32),
            shape((tokens, width), BF),
            shape((tokens, width), BF),
        ],
        scratch_shapes=[
            pltpu.VMEM((model, width), BF),
            pltpu.VMEM((width, model), BF),
            pltpu.SemaphoreType.DMA((2,)),
        ],
        compiler_params=limits(48),
        cost_estimate=cost(4 * tokens * model * width, tokens * (8 * model + 4 * width)),
        name="feed_forward",
    )(table, *in_pieces, *out_pieces, middle, vec, b_in)


def feed_backward(table, in_pieces, out_pieces, grad, middle, hidden, slope, vec, slabs):
    tokens, model = middle.shape
    width = hidden.shape[1]
    block = min(512, tokens)
    shape = jax.ShapeDtypeStruct
    small_width = 2 * model + width
    return pl.pallas_call(
        functools.partial(feed_backward_kernel, (len(in_pieces), len(out_pieces))),
        grid=(tokens // block,),
        in_specs=[SMEM]
        + [ANY] * (len(in_pieces) + len(out_pieces))
        + [leading((block, model))] * 2
        + [leading((block, width))] * 2
        + [whole(vec.shape)],
        out_specs=[leading((block, model)), whole((8, small_width)), ANY, ANY],
        out_shape=[
            shape((tokens, model), F32),
            shape((8, small_width), F32),
            shape((slabs, model // slabs, width), BF),
            shape((slabs, width // slabs, model), BF),
        ],
        scratch_shapes=[
            pltpu.VMEM((model, width), BF),
            pltpu.VMEM((width, model), BF),
            pltpu.VMEM((model, width), F32),
            pltpu.VMEM((width, model), F32),
            pltpu.SemaphoreType.DMA((2,)),
        ],
        compiler_params=limits(56),
        cost_estimate=cost(8 * tokens * model * width, tokens * (12 * model + 4 * width)),
        name="feed_backward",
    )(table, *in_pieces, *out_pieces, grad, middle, hidden, slope, vec)


def spatial_backward(table, qkv_pieces, proj_pieces, grad, own, other, mixed, attended, prob, vec, slabs):
    frames, half, model = own.shape
    patches = 2 * half
    each = min(2, frames)
    shape = jax.ShapeDtypeStruct
    return pl.pallas_call(
        functools.partial(spatial_backward_kernel, (len(qkv_pieces), len(proj_pieces))),
        grid=(frames // each,),
        in_specs=[SMEM]
        + [ANY] * (len(qkv_pieces) + len(proj_pieces))
        + [
            leading((each, patches, model)),
            leading((each, half, model)),
            leading((each, half, model)),
            leading((each, patches, 3 * model)),
            leading((each, patches, model)),
            leading((each, HEADS, patches, patches)),
            whole(vec.shape),
        ],
        out_specs=[
            leading((each, half, model)),
            leading((each, half, model)),
            whole((8, 2 * model)),
            ANY,
            ANY,
        ],
        out_shape=[
            shape((frames, half, model), BF),
            shape((frames, half, model), BF),
            shape((8, 2 * model), F32),
            shape((slabs, model // slabs, 3 * model), BF),
            shape((slabs, model // slabs, model), BF),
        ],
        scratch_shapes=[
            pltpu.VMEM((model, 3 * model), BF),
            pltpu.VMEM((model, model), BF),
            pltpu.VMEM((model, 3 * model), F32),
            pltpu.VMEM((model, model), F32),
            pltpu.VMEM((each * patches, model), BF),
            pltpu.VMEM((each * patches, 3 * model), BF),
            pltpu.SemaphoreType.DMA((2,)),
        ],
        compiler_params=limits(56),
        cost_estimate=cost(
            2 * frames * patches * model * (8 * model + 4 * patches), frames * patches * model * 30
        ),
        name="spatial_backward",
    )(table, *qkv_pieces, *proj_pieces, grad, own, other, mixed, attended, prob, vec)


def temporal_block(table, pieces, rows, own, other, vec, b_in, allowed, slabs):
    steps, patches, model = rows.shape
    width = b_in.shape[1]
    half = own.shape[1]
    each = min(64, half)
    tile = min(16, each)
    halves = half // each
    last = halves - 1
    count = steps * each
    same = jnp.eye(tile, dtype=jnp.bool_)
    bias = jnp.where(
        allowed.T[:, None, :, None] & same[None, :, None, :], 0.0, -1000000000.0
    ).astype(F32)
    bias = bias.reshape(steps * tile, steps * tile)
    shape = jax.ShapeDtypeStruct
    small_width = 4 * model + width
    block = (steps, each, model)
    return pl.pallas_call(
        functools.partial(temporal_kernel, tuple(len(piece) for piece in pieces), tile),
        grid=(2 * halves,),
        in_specs=[SMEM]
        + [ANY] * sum(len(piece) for piece in pieces)
        + [
            pl.BlockSpec(block, lambda idx: (0, idx, 0)),
            pl.BlockSpec(block, lambda idx: (0, jnp.minimum(idx, last), 0)),
            pl.BlockSpec(block, lambda idx: (0, jnp.maximum(idx - halves, 0), 0)),
            whole(vec.shape),
            whole(b_in.shape),
            whole(bias.shape),
        ],
        out_specs=[
            pl.BlockSpec(block, lambda idx: (0, idx, 0)),
            pl.BlockSpec(block, lambda idx: (0, idx, 0)),
            whole((8, small_width)),
            ANY,
            ANY,
            ANY,
            ANY,
        ],
        out_shape=[
            shape((steps, patches, model), BF),
            shape((steps, patches, model), F32),
            shape((8, small_width), F32),
            shape((slabs, model // slabs, 3 * model), BF),
            shape((slabs, model // slabs, model), BF),
            shape((slabs, model // slabs, width), BF),
            shape((slabs, width // slabs, model), BF),
        ],
        scratch_shapes=[
            pltpu.VMEM((model, 3 * model), BF),
            pltpu.VMEM((model, model), BF),
            pltpu.VMEM((model, width), BF),
            pltpu.VMEM((width, model), BF),
            pltpu.VMEM((model, 3 * model), F32),
            pltpu.VMEM((model, model), F32),
            pltpu.VMEM((model, width), F32),
            pltpu.VMEM((width, model), F32),
            pltpu.VMEM((count, 3 * model), BF),
            pltpu.VMEM((count, model), BF),
            pltpu.VMEM((each // tile, HEADS, steps * tile, steps * tile), BF),
            pltpu.VMEM((count, width), BF),
            pltpu.VMEM((count, width), BF),
            pltpu.VMEM((count, model), BF),
            pltpu.VMEM((count, 3 * model), BF),
            pltpu.SemaphoreType.DMA((4,)),
        ],
        compiler_params=limits(60),
        cost_estimate=cost(
            6 * steps * patches * model * (4 * model + 2 * width), steps * patches * model * 16
        ),
        name="temporal_block",
    )(
        table,
        *[item for piece in pieces for item in piece],
        rows,
        own,
        other,
        vec,
        b_in,
        bias,
    )


class Plan:
    def __init__(self, mesh):
        self.dp = mesh.shape["dp"]
        self.seq = mesh.shape["seq"]
        self.count = self.dp * self.seq
        self.cube = self.dp == 16 and self.seq == 2

    def swap(self, value, mask):
        pairs = [(idx, idx ^ mask) for idx in range(self.count)]
        return lax.ppermute(value, AXES, pairs)

    def me(self):
        return lax.axis_index("dp") * self.seq + lax.axis_index("seq")


ROW, CORE, COLUMN, Z_LOW, Z_HIGH = 1, 2, 4, 8, 16


def gather_masks(order):
    masks = [0]
    for stage in order:
        masks = masks + [mask ^ bit for bit in stage for mask in masks]
    return masks


STAGE_Z = (Z_LOW, Z_HIGH, Z_LOW | Z_HIGH)
GATHER_A = (STAGE_Z, (COLUMN,), (ROW,), (CORE,))
GATHER_B = (STAGE_Z, (ROW,), (COLUMN,), (CORE,))


def gather_pieces(plan, shards, order):
    if not plan.cube:
        return [
            [lax.all_gather(shard, AXES, axis=0, tiled=True)[None]] for shard in shards
        ]
    have = [shard[None] for shard in shards]
    for stage in order[:-1]:
        come = [[item] + [plan.swap(item, bit) for bit in stage] for item in have]
        have = [jnp.concatenate(parts, 0) for parts in come]
    return [[item, plan.swap(item, order[-1][0])] for item in have]


SUM_A = (CORE, COLUMN, ROW, Z_HIGH, Z_LOW)
SUM_B = (CORE, ROW, COLUMN, Z_HIGH, Z_LOW)


def sum_masks(order):
    masks = [0]
    for bit in reversed(order):
        masks = masks + [mask ^ bit for mask in masks]
    return masks


def add_up(*values):
    total = values[0].astype(F32)
    for value in values[1:]:
        total = total + value.astype(F32)
    return total


def scatter_sum(plan, slabs, order):
    if not plan.cube:
        return lax.psum_scatter(
            slabs[0].astype(F32), AXES, scatter_dimension=0, tiled=True
        )
    value = slabs
    for bit in order[:-2]:
        half = value.shape[0] // 2
        come = plan.swap(value[half:], bit)
        value = add_up(value[:half], come).astype(slabs.dtype)
    high, low = order[-2], order[-1]
    parts = [
        plan.swap(value[1], low),
        plan.swap(value[2], high),
        plan.swap(value[3], high ^ low),
    ]
    return add_up(value[0], *parts)


def to_frames(plan, values):
    steps, here, model = values.shape
    if plan.seq == 2:
        row = lax.axis_index("seq")
        count = steps // 2
        own = lax.dynamic_slice_in_dim(values, row * count, count, 0)
        away = lax.dynamic_slice_in_dim(values, (1 - row) * count, count, 0)
        return own, lax.ppermute(away, "seq", [(0, 1), (1, 0)])
    full = lax.all_to_all(values, "seq", split_axis=0, concat_axis=1, tiled=True)
    half = full.shape[1] // 2
    return full[:, :half], full[:, half:]


def from_frames(plan, own, other):
    if plan.seq == 2:
        row = lax.axis_index("seq")
        count = own.shape[0]
        come = lax.ppermute(other, "seq", [(0, 1), (1, 0)])
        first = jnp.where(row == 0, own, come)
        second = jnp.where(row == 0, come, own)
        return jnp.concatenate([first, second], 0)
    full = jnp.concatenate([own, other], 1)
    return lax.all_to_all(full, "seq", split_axis=1, concat_axis=0, tiled=True)


def regroup(plan, values, split_axis, concat_axis):
    members = plan.seq // MICRO
    if members == 1:
        return values
    row = lax.axis_index("seq")
    rank = row % members
    size = values.shape[split_axis] // members
    span = values.shape[concat_axis]
    shape = list(values.shape)
    shape[split_axis] = size
    shape[concat_axis] = span * members
    result = jnp.zeros(shape, values.dtype)
    for shift in range(members):
        target = (rank + shift) % members
        part = lax.dynamic_slice_in_dim(values, target * size, size, split_axis)
        if shift:
            pairs = [
                (idx, idx - idx % members + (idx + shift) % members) for idx in range(plan.seq)
            ]
            part = lax.ppermute(part, "seq", pairs)
        source = (rank - shift) % members
        result = lax.dynamic_update_slice_in_dim(result, part, source * span, concat_axis)
    return result


def clip_mask(lengths, steps):
    ends = jnp.cumsum(lengths, -1)
    positions = jnp.arange(steps, dtype=jnp.int32)
    clips = jnp.sum((positions[:, None] >= ends[None, :]).astype(jnp.int32), -1)
    return (clips[:, None] == clips[None, :]) & (positions[None, :] <= positions[:, None])


def on_device(plan, tokens, lengths, cotangent, norm_gain, norm_bias, w_qkv, w_proj, w_in, b_in, w_out):
    steps_all, here, model = tokens.shape[1:]
    steps = steps_all // MICRO
    width = b_in.shape[1] * plan.count
    row = lax.axis_index("seq")
    micro = row * MICRO // plan.seq
    allowed = clip_mask(lax.dynamic_index_in_dim(lengths[0], micro, 0, keepdims=False), steps)

    own, other = to_frames(plan, tokens[0])

    small = jnp.concatenate([norm_gain.reshape(-1), norm_bias.reshape(-1), b_in.reshape(-1)])
    if plan.cube:
        me = plan.me()
        orders = [gather_masks(GATHER_A), gather_masks(GATHER_B), sum_masks(SUM_A), sum_masks(SUM_B)]
        table = me ^ jnp.array(orders, jnp.int32)
        slabs = plan.count
        small = jnp.pad(small, (0, LANES * 16 - small.shape[0])).reshape(16, LANES)
        (small_pieces,) = gather_pieces(plan, [small], GATHER_A)
        small_all = jnp.concatenate(small_pieces, 0)[:, :2].reshape(plan.count, -1)
        pick = (table[FROM_A][None, :] == jnp.arange(plan.count)[:, None]).astype(BF)
        small_all = jnp.einsum("ij,jk->ik", pick, small_all, preferred_element_type=F32)
    else:
        table = jnp.zeros((4, 1), jnp.int32)
        slabs = 1
        small_all = lax.all_gather(small, AXES, axis=0).astype(F32)
    wide = model // plan.count
    cut = 4 * wide
    gains = small_all[:, :cut].reshape(plan.count, 2, 2, wide)
    shifts = small_all[:, cut : 2 * cut].reshape(plan.count, 2, 2, wide)
    gains = gains.transpose(1, 2, 0, 3).reshape(2, 2, model)
    shifts = shifts.transpose(1, 2, 0, 3).reshape(2, 2, model)
    vecs = jnp.stack([gains, shifts], 2).reshape(2, 4, model)
    biases = small_all[:, 2 * cut : 2 * cut + 2 * (width // plan.count)]
    biases = biases.reshape(plan.count, 2, -1).transpose(1, 0, 2).reshape(2, 1, width)

    qkv_0, proj_0 = gather_pieces(plan, [w_qkv[0], w_proj[0]], GATHER_A)
    (in_0,) = gather_pieces(plan, [w_in[0]], GATHER_A)
    (out_0,) = gather_pieces(plan, [w_out[0]], GATHER_B)
    qkv_1, proj_1, in_1, out_1 = gather_pieces(
        plan, [w_qkv[1], w_proj[1], w_in[1], w_out[1]], GATHER_A
    )

    middle, mixed, attended, prob = spatial_forward(table, qkv_0, proj_0, own, other, vecs[0])
    frames, patches = middle.shape[:2]
    count = frames * patches
    middle = middle.reshape(count, model)
    result, hidden, slope = feed_forward(table, in_0, out_0, middle, vecs[0], biases[0])

    ct_own, ct_other = to_frames(plan, cotangent[0])
    rows = regroup(plan, result.reshape(frames, patches, model), 1, 0)
    if plan.seq != 2:
        full = regroup(plan, jnp.concatenate([ct_own, ct_other], 1), 1, 0)
        cut_at = full.shape[1] // 2
        ct_own, ct_other = full[:, :cut_at], full[:, cut_at:]
    active, grad, small_1, g_qkv_1, g_proj_1, g_in_1, g_out_1 = temporal_block(
        table,
        (qkv_1, proj_1, in_1, out_1),
        rows,
        ct_own,
        ct_other,
        vecs[1],
        biases[1],
        allowed,
        slabs,
    )
    active = regroup(plan, active, 0, 1)
    half = active.shape[1] // 2
    activations = from_frames(plan, active[:, :half], active[:, half:])
    grad = regroup(plan, grad, 0, 1).reshape(count, model)

    s_in_1 = scatter_sum(plan, g_in_1, SUM_A)
    s_out_1 = scatter_sum(plan, g_out_1, SUM_B)
    s_qkv_1 = scatter_sum(plan, g_qkv_1, SUM_B)
    s_proj_1 = scatter_sum(plan, g_proj_1, SUM_B)

    grad_middle, small_0, g_in_0, g_out_0 = feed_backward(
        table, in_0, out_0, grad, middle, hidden, slope, vecs[0], slabs
    )
    s_in_0 = scatter_sum(plan, g_in_0, SUM_A)
    s_out_0 = scatter_sum(plan, g_out_0, SUM_B)
    grad_own, grad_other, tiny_0, g_qkv_0, g_proj_0 = spatial_backward(
        table,
        qkv_0,
        proj_0,
        grad_middle.reshape(frames, patches, model),
        own,
        other,
        mixed,
        attended,
        prob,
        vecs[0],
        slabs,
    )
    grad_tokens = from_frames(plan, grad_own, grad_other)
    s_qkv_0 = scatter_sum(plan, g_qkv_0, SUM_A)
    s_proj_0 = scatter_sum(plan, g_proj_0, SUM_A)

    small_0 = jnp.sum(small_0, 0)
    small_1 = jnp.sum(small_1, 0)
    tiny_0 = jnp.sum(tiny_0, 0)
    far = 2 * model + width

    def cut_up(values):
        return values.reshape(plan.count, -1)

    columns = [
        tiny_0[:model],
        small_0[:model],
        small_1[far : far + model],
        small_1[:model],
        tiny_0[model:],
        small_0[model : 2 * model],
        small_1[far + model :],
        small_1[model : 2 * model],
        small_0[2 * model :],
        small_1[2 * model : far],
    ]
    smalls = jnp.concatenate([cut_up(item) for item in columns], 1)
    if plan.cube:
        pick = (table[TO_A][:, None] == jnp.arange(plan.count)[None, :]).astype(F32)
        smalls = jnp.einsum(
            "ij,jk->ik", pick, smalls, preferred_element_type=F32, precision=lax.Precision.HIGHEST
        )
        mine = scatter_sum(plan, smalls.reshape(plan.count, 2, -1), SUM_A).reshape(-1)
    else:
        mine = lax.psum_scatter(smalls, AXES, scatter_dimension=0, tiled=True).reshape(-1)
    grad_gain = mine[:cut].reshape(2, 2, wide)
    grad_shift = mine[cut : 2 * cut].reshape(2, 2, wide)
    grad_b_in = mine[2 * cut :].reshape(2, -1)
    return (
        activations[None],
        grad_tokens[None],
        grad_gain,
        grad_shift,
        jnp.stack([s_qkv_0, s_qkv_1]),
        jnp.stack([s_proj_0, s_proj_1]),
        jnp.stack([s_in_0, s_in_1]),
        grad_b_in,
        jnp.stack([s_out_0, s_out_1]),
    )


def solution(mesh):
    in_specs = (
        P("dp", None, "seq", None),
        P("dp", None, None),
        P("dp", None, "seq", None),
        P(None, None, AXES),
        P(None, None, AXES),
        P(None, AXES, None),
        P(None, AXES, None),
        P(None, AXES, None),
        P(None, AXES),
        P(None, AXES, None),
    )
    out_specs = (
        P("dp", None, "seq", None),
        P("dp", None, "seq", None),
        P(None, None, AXES),
        P(None, None, AXES),
        P(None, AXES, None),
        P(None, AXES, None),
        P(None, AXES, None),
        P(None, AXES),
        P(None, AXES, None),
    )
    return jax.shard_map(
        functools.partial(on_device, Plan(mesh)),
        mesh=mesh,
        in_specs=in_specs,
        out_specs=out_specs,
        check_vma=False,
    )
```

```python
import functools

import jax
import jax.numpy as jnp
from jax import lax
from jax.experimental import pallas as pl
from jax.experimental.pallas import tpu as pltpu
from jax.sharding import PartitionSpec as P

HEADS = 8
MICRO = 2
LANES = 128
JOINED = 256
AXES = ("dp", "seq")
BF = jnp.bfloat16
F32 = jnp.float32
MIB = 1 << 20
FROM_A, FROM_B, FROM_C, TO_A, AS_IS, HERE = range(6)


def dot(left, right, left_dim, right_dim):
    return lax.dot_general(
        left, right, (((left_dim,), (right_dim,)), ((), ())), preferred_element_type=F32
    )


def norm_stats(values):
    centre = values - jnp.mean(values, -1, keepdims=True)
    variance = jnp.mean(centre * centre, -1, keepdims=True)
    inverse = lax.rsqrt(variance + 1e-05)
    return centre * inverse, inverse


def norm_back(grad_scaled, unit_rows, inverse):
    mean_grad = jnp.mean(grad_scaled, -1, keepdims=True)
    mean_cross = jnp.mean(grad_scaled * unit_rows, -1, keepdims=True)
    return inverse * (grad_scaled - mean_grad - unit_rows * mean_cross)


def fold_rows(values):
    return jnp.sum(values.reshape(-1, 8, values.shape[-1]), 0)


def gelu_pair(values):
    cumulative = 0.5 * (1.0 + lax.erf(values * 0.7071067811865476))
    slope = cumulative + values * jnp.exp(-0.5 * values * values) * 0.3989422804014327
    return values * cumulative, slope


def start_weight(segments, groups, table_ref, held, sem):
    for group, which, first_col, cols, block, blocks, to_col in segments:
        slab = 0
        for piece in groups[group]:
            rows = piece.shape[1]
            for idx in range(piece.shape[0]):
                first = table_ref[which, slab] * (rows * blocks) + block * rows
                pltpu.make_async_copy(
                    piece.at[idx, :, pl.ds(first_col, cols)],
                    held.at[pl.ds(pl.multiple_of(first, rows), rows), pl.ds(to_col, cols)],
                    sem,
                ).start()
                slab += 1


def wait_weight(held, sem):
    pltpu.make_async_copy(held, held, sem).wait()


def split_refs(refs, counts):
    groups = []
    for count in counts:
        groups.append(refs[:count])
        refs = refs[count:]
    return groups, refs


def spread_heads(values, width, scale):
    lane = lax.broadcasted_iota(jnp.int32, (1, values.shape[-1]), 1)
    parts = []
    for head in range(values.shape[-1] // width):
        inside = (lane >= head * width) & (lane < (head + 1) * width)
        parts.append(values * jnp.where(inside, scale, 0.0).astype(BF))
    return jnp.concatenate(parts, 0)


def merge_heads(values, width):
    lane = lax.broadcasted_iota(jnp.int32, (1, values.shape[-1]), 1)
    count = values.shape[-1] // width
    rows = values.shape[0] // count
    merged = values[(count - 1) * rows :]
    for head in range(count - 2, -1, -1):
        merged = jnp.where(
            lane < (head + 1) * width, values[head * rows : (head + 1) * rows], merged
        )
    return merged


def attend_forward(load, model, store, keep, bias):
    width = model // HEADS
    scale = width ** (-0.5)
    for part in range(model // JOINED):
        first = part * JOINED
        scores = dot(load(model + first), spread_heads(load(first), width, scale), 1, 1)
        if bias is not None:
            scores = scores + bias
        exponent = jnp.exp(scores - jnp.max(scores, 0, keepdims=True))
        prob = (exponent * (1.0 / jnp.sum(exponent, 0, keepdims=True))).astype(BF)
        keep(part, prob)
        store(first, merge_heads(dot(prob, load(2 * model + first), 0, 0), width).astype(BF))


def attend_backward(load, load_grad, load_prob, model, store):
    width = model // HEADS
    scale = width ** (-0.5)
    for part in range(model // JOINED):
        first = part * JOINED
        spread_grad = spread_heads(load_grad(first), width, 1.0)
        spread_query = spread_heads(load(first), width, scale)
        prob = load_prob(part)
        grad_prob = dot(load(2 * model + first), spread_grad, 1, 1)
        prob_wide = prob.astype(F32)
        total = jnp.sum(prob_wide * grad_prob, 0, keepdims=True)
        grad_scores = (prob_wide * (grad_prob - total)).astype(BF)
        store(2 * model + first, dot(prob, spread_grad, 1, 0).astype(BF))
        store(model + first, dot(grad_scores, spread_query, 1, 0).astype(BF))
        scaled_key = load(model + first) * jnp.asarray(scale, BF)
        store(first, merge_heads(dot(grad_scores, scaled_key, 0, 0), width).astype(BF))


def spatial_forward_kernel(specs, counts, table_ref, *refs):
    groups, refs = split_refs(refs, counts)
    (
        own_ref,
        other_ref,
        vec_ref,
        middle_ref,
        normed_ref,
        qkv_ref,
        attended_ref,
        prob_ref,
        w_qkv,
        w_proj,
        sems,
    ) = refs
    frames, half, model = own_ref.shape

    @pl.when(pl.program_id(0) == 0)
    def _():
        start_weight(specs[0], groups, table_ref, w_qkv, sems.at[0])
        start_weight(specs[1], groups, table_ref, w_proj, sems.at[1])
        wait_weight(w_qkv, sems.at[0])
        wait_weight(w_proj, sems.at[1])

    rows = jnp.concatenate([own_ref[...], other_ref[...]], 1).astype(F32)
    rows = rows.reshape(frames * 2 * half, model)
    unit, _ = norm_stats(rows)
    normed = (unit * vec_ref[0:1] + vec_ref[1:2]).astype(BF)
    normed_ref[...] = normed.reshape(normed_ref.shape)
    qkv_ref[...] = dot(normed, w_qkv[...], 1, 0).astype(BF).reshape(qkv_ref.shape)
    for frame in range(frames):

        def load(first):
            return qkv_ref[frame, :, first : first + JOINED]

        def store(first, value):
            attended_ref[frame, :, first : first + JOINED] = value

        def keep(part, value):
            prob_ref[frame, part] = value

        attend_forward(load, model, store, keep, None)
    attended = attended_ref[...].reshape(rows.shape)
    middle = rows + dot(attended, w_proj[...], 1, 0)
    middle_ref[...] = middle.reshape(middle_ref.shape)


def feed_forward_kernel(specs, counts, table_ref, *refs):
    groups, refs = split_refs(refs, counts)
    (
        middle_ref,
        vec_ref,
        b_in_ref,
        result_ref,
        normed_ref,
        hidden_ref,
        slope_ref,
        w_in,
        w_out,
        sems,
    ) = refs

    @pl.when(pl.program_id(0) == 0)
    def _():
        start_weight(specs[0], groups, table_ref, w_in, sems.at[0])
        start_weight(specs[1], groups, table_ref, w_out, sems.at[1])
        wait_weight(w_in, sems.at[0])
        wait_weight(w_out, sems.at[1])

    middle = middle_ref[...]
    unit, _ = norm_stats(middle)
    normed = (unit * vec_ref[2:3] + vec_ref[3:4]).astype(BF)
    normed_ref[...] = normed
    result_ref[...] = middle + ff_through(normed, b_in_ref, w_in, w_out, hidden_ref, slope_ref)


def ff_through(normed, b_in_ref, w_in, w_out, hidden_ref, slope_ref):
    width = w_in.shape[1]
    chunk = min(512, width)
    total = None
    for first in range(0, width, chunk):
        cols = slice(first, first + chunk)
        pre_act = dot(normed, w_in[:, cols], 1, 0) + b_in_ref[:, cols]
        hidden, slope = gelu_pair(pre_act)
        hidden = hidden.astype(BF)
        hidden_ref[:, cols] = hidden
        slope_ref[:, cols] = slope.astype(BF)
        term = dot(hidden, w_out[cols, :], 1, 0)
        total = term if total is None else total + term
    return total


def ff_back(grad_out, branch, unit, inverse, gain, w_in, w_out, slope_ref, grad_pre_ref, small_ref):
    model, width = w_in.shape
    chunk = min(512, width)
    grad_second = None
    for first in range(0, width, chunk):
        cols = slice(first, first + chunk)
        grad_hidden = dot(branch, w_out[cols, :], 1, 1)
        grad_pre = (grad_hidden * slope_ref[:, cols].astype(F32)).astype(BF)
        grad_pre_ref[:, cols] = grad_pre
        small_ref[:, 2 * model + first : 2 * model + first + chunk] += fold_rows(
            grad_pre.astype(F32)
        )
        term = dot(grad_pre, w_in[:, cols], 1, 1)
        grad_second = term if grad_second is None else grad_second + term
    small_ref[:, :model] += fold_rows(grad_second * unit)
    small_ref[:, model : 2 * model] += fold_rows(grad_second)
    return grad_out + norm_back(grad_second * gain, unit, inverse)


def feed_backward_kernel(specs, counts, table_ref, *refs):
    groups, refs = split_refs(refs, counts)
    (
        grad_ref,
        middle_ref,
        slope_ref,
        vec_ref,
        grad_middle_ref,
        branch_ref,
        grad_pre_ref,
        small_ref,
        w_in,
        w_out,
        sems,
    ) = refs

    @pl.when(pl.program_id(0) == 0)
    def _():
        start_weight(specs[0], groups, table_ref, w_in, sems.at[0])
        start_weight(specs[1], groups, table_ref, w_out, sems.at[1])
        small_ref[...] = jnp.zeros_like(small_ref)
        wait_weight(w_in, sems.at[0])
        wait_weight(w_out, sems.at[1])

    unit, inverse = norm_stats(middle_ref[...])
    branch = grad_ref[...].astype(BF)
    branch_ref[...] = branch
    grad_middle_ref[...] = ff_back(
        grad_ref[...],
        branch,
        unit,
        inverse,
        vec_ref[2:3],
        w_in,
        w_out,
        slope_ref,
        grad_pre_ref,
        small_ref,
    )


def spatial_backward_kernel(specs, counts, table_ref, *refs):
    groups, refs = split_refs(refs, counts)
    (
        grad_ref,
        own_ref,
        other_ref,
        qkv_ref,
        prob_ref,
        vec_ref,
        grad_own_ref,
        grad_other_ref,
        proj_in_ref,
        grad_mixed_ref,
        small_ref,
        w_qkv,
        w_proj,
        grad_att,
        sems,
    ) = refs
    frames, half, model = own_ref.shape

    @pl.when(pl.program_id(0) == 0)
    def _():
        start_weight(specs[0], groups, table_ref, w_qkv, sems.at[0])
        start_weight(specs[1], groups, table_ref, w_proj, sems.at[1])
        small_ref[...] = jnp.zeros_like(small_ref)
        wait_weight(w_qkv, sems.at[0])
        wait_weight(w_proj, sems.at[1])

    rows = jnp.concatenate([own_ref[...], other_ref[...]], 1).astype(F32)
    rows = rows.reshape(frames * 2 * half, model)
    unit, inverse = norm_stats(rows)
    grad_middle = grad_ref[...].reshape(rows.shape)
    proj_in = grad_middle.astype(BF)
    proj_in_ref[...] = proj_in.reshape(proj_in_ref.shape)
    grad_att[...] = dot(proj_in, w_proj[...], 1, 1).astype(BF)
    for frame in range(frames):
        frame_rows = slice(frame * 2 * half, (frame + 1) * 2 * half)

        def load(first):
            return qkv_ref[frame, :, first : first + JOINED]

        def load_grad(first):
            return grad_att[frame_rows, first : first + JOINED]

        def load_prob(part):
            return prob_ref[frame, part]

        def store(first, value):
            grad_mixed_ref[frame, :, first : first + JOINED] = value

        attend_backward(load, load_grad, load_prob, model, store)
    grad_mixed = grad_mixed_ref[...].reshape(rows.shape[0], 3 * model)
    grad_first = dot(grad_mixed, w_qkv[...], 1, 1)
    small_ref[:, :model] += fold_rows(grad_first * unit)
    small_ref[:, model : 2 * model] += fold_rows(grad_first)
    grad_rows = grad_middle + norm_back(grad_first * vec_ref[0:1], unit, inverse)
    grad_rows = grad_rows.astype(BF).reshape(frames, 2 * half, model)
    grad_own_ref[...] = grad_rows[:, :half]
    grad_other_ref[...] = grad_rows[:, half:]


def temporal_kernel(specs, counts, tile, table_ref, *refs):
    groups, refs = split_refs(refs, counts)
    (
        rows_ref,
        own_ref,
        other_ref,
        vec_ref,
        b_in_ref,
        bias_ref,
        active_own_ref,
        active_other_ref,
        grad_ref,
        small_ref,
        normed_one_ref,
        attended_ref,
        normed_two_ref,
        hidden_ref,
        branch_ref,
        grad_pre_ref,
        proj_in_ref,
        grad_mixed_ref,
        w_qkv,
        w_proj,
        w_in,
        w_out,
        mixed,
        probs,
        slope,
        grad_att,
        sems,
    ) = refs
    steps, patches, model = rows_ref.shape
    tiles = patches // tile
    held = (w_qkv, w_proj, w_in, w_out)

    @pl.when(pl.program_id(0) == 0)
    def _():
        for idx in range(4):
            start_weight(specs[idx], groups, table_ref, held[idx], sems.at[idx])
        small_ref[...] = jnp.zeros_like(small_ref)
        for idx in range(4):
            wait_weight(held[idx], sems.at[idx])

    def gather_rows(ref):
        parts = [
            ref[:, idx * tile : (idx + 1) * tile, :].reshape(steps * tile, model)
            for idx in range(tiles)
        ]
        return jnp.concatenate(parts, 0)

    def spread_rows(ref, values):
        for idx in range(tiles):
            part = values[idx * steps * tile : (idx + 1) * steps * tile]
            ref[:, idx * tile : (idx + 1) * tile, :] = part.reshape(steps, tile, model).astype(
                ref.dtype
            )

    rows = gather_rows(rows_ref)
    unit_one, inverse_one = norm_stats(rows)
    normed_one = (unit_one * vec_ref[0:1] + vec_ref[1:2]).astype(BF)
    normed_one_ref[...] = normed_one
    mixed[...] = dot(normed_one, w_qkv[...], 1, 0).astype(BF)
    span = steps * tile
    bias = jnp.concatenate([bias_ref[...]] * (JOINED // (model // HEADS)), 1)
    for idx in range(tiles):
        tile_rows = slice(idx * span, (idx + 1) * span)

        def load(first):
            return mixed[tile_rows, first : first + JOINED]

        def store(first, value):
            attended_ref[tile_rows, first : first + JOINED] = value

        def keep(part, value):
            probs[idx, part] = value

        attend_forward(load, model, store, keep, bias)
    middle = rows + dot(attended_ref[...], w_proj[...], 1, 0)
    unit_two, inverse_two = norm_stats(middle)
    normed_two = (unit_two * vec_ref[2:3] + vec_ref[3:4]).astype(BF)
    normed_two_ref[...] = normed_two
    result = middle + ff_through(normed_two, b_in_ref, w_in, w_out, hidden_ref, slope)
    from_own = pl.program_id(0) < pl.num_programs(0) // 2

    @pl.when(from_own)
    def _():
        spread_rows(active_own_ref, result)

    @pl.when(jnp.logical_not(from_own))
    def _():
        spread_rows(active_other_ref, result)

    branch = gather_rows(jnp.where(from_own, own_ref[...], other_ref[...]))
    branch_ref[...] = branch
    grad_middle = ff_back(
        branch.astype(F32),
        branch,
        unit_two,
        inverse_two,
        vec_ref[2:3],
        w_in,
        w_out,
        slope,
        grad_pre_ref,
        small_ref,
    )
    proj_in = grad_middle.astype(BF)
    proj_in_ref[...] = proj_in
    grad_att[...] = dot(proj_in, w_proj[...], 1, 1).astype(BF)
    for idx in range(tiles):
        tile_rows = slice(idx * span, (idx + 1) * span)

        def load(first):
            return mixed[tile_rows, first : first + JOINED]

        def load_grad(first):
            return grad_att[tile_rows, first : first + JOINED]

        def load_prob(part):
            return probs[idx, part]

        def store(first, value):
            grad_mixed_ref[tile_rows, first : first + JOINED] = value

        attend_backward(load, load_grad, load_prob, model, store)
    grad_first = dot(grad_mixed_ref[...], w_qkv[...], 1, 1)
    offset = 2 * model + w_in.shape[1]
    small_ref[:, offset : offset + model] += fold_rows(grad_first * unit_one)
    small_ref[:, offset + model : offset + 2 * model] += fold_rows(grad_first)
    spread_rows(
        grad_ref, grad_middle + norm_back(grad_first * vec_ref[0:1], unit_one, inverse_one)
    )


def weight_grad_kernel(jobs, which, rows, n_in, n_out, has_small, table_ref, *refs):
    ins, refs = refs[:n_in], refs[n_in:]
    outs = refs[len(refs) - n_out - 3 - has_small : len(refs) - 3 - has_small]
    over, staged, sem = refs[len(refs) - 3 - has_small :][:3]
    step = pl.program_id(0)
    each = outs[0].shape[0]
    slabs = each * n_out
    first_step = 0
    for left, right, by_rows, first_col, tiles in jobs:
        begin = first_step
        first_step += tiles

        def work():
            staged[step] = dot(ins[left][...], ins[right][...], 0, 0).astype(BF)
            tile = step - begin
            for idx in range(slabs):
                out = outs[idx // each].at[idx % each]
                place = table_ref[which, idx]
                if by_rows:
                    fold = ins[left].shape[1] * tiles // (slabs * rows)
                    here = slabs // tiles

                    @pl.when(place // here == tile)
                    def _():
                        for item in range(fold):
                            first = (place % here) * (fold * rows) + item * rows
                            cols = staged.shape[2]
                            pltpu.make_async_copy(
                                staged.at[step, pl.ds(pl.multiple_of(first, rows), rows)],
                                out.at[:, pl.ds(first_col + item * cols, cols)],
                                sem,
                            ).start()

                else:
                    cols = staged.shape[2]
                    to_col = first_col + tile * cols
                    pltpu.make_async_copy(
                        staged.at[step, pl.ds(pl.multiple_of(place * rows, rows), rows)],
                        out.at[:, pl.ds(pl.multiple_of(to_col, LANES), cols)],
                        sem,
                    ).start()

        pl.when((step >= begin) & (step < first_step))(work)

    @pl.when(step == pl.num_programs(0) - 1)
    def _():
        if has_small:
            small = refs[-1]
            small[...] = small_slabs(refs[0], refs[1:4])
            width = outs[0].shape[2] - LANES
            for half in range(n_out):
                pltpu.make_async_copy(
                    small.at[pl.ds(half * each, each)],
                    outs[half].at[:, :, pl.ds(width, LANES)],
                    sem,
                ).start()
        for out in outs:
            pltpu.make_async_copy(out, out, sem).wait()
        over[...] = jnp.zeros_like(over)


def small_slabs(place_ref, sums):
    tiny_0, small_0, small_1 = [jnp.sum(ref[...], 0, keepdims=True) for ref in sums]
    model = tiny_0.shape[1] // 2
    width = small_0.shape[1] - 2 * model
    far = 2 * model + width
    place = place_ref[...][:, :1]
    slabs = place.shape[0]

    def table(items):
        total = jnp.zeros((slabs, LANES), F32)
        offset = 0
        for values in items:
            length = values.shape[1]
            each = length // slabs
            lane = lax.broadcasted_iota(jnp.int32, (1, length), 1)
            mine = jnp.where(lane // each == place, values, 0.0).astype(BF)
            source = lax.broadcasted_iota(jnp.int32, (length, LANES), 0)
            target = lax.broadcasted_iota(jnp.int32, (length, LANES), 1)
            choose = jnp.where(source % each + offset == target, 1.0, 0.0).astype(BF)
            total = total + dot(mine, choose, 1, 0)
            offset += each
        return total

    norms = table(
        [
            tiny_0[:, :model],
            small_0[:, :model],
            small_1[:, far : far + model],
            small_1[:, :model],
            tiny_0[:, model:],
            small_0[:, model : 2 * model],
            small_1[:, far + model :],
            small_1[:, model : 2 * model],
        ]
    )
    biases = table([small_0[:, 2 * model :], small_1[:, 2 * model : far]])
    row = lax.broadcasted_iota(jnp.int32, (slabs, 16, LANES), 1)
    both = jnp.where(row == 0, norms[:, None, :], jnp.where(row == 1, biases[:, None, :], 0.0))
    return both.astype(BF)


def pack_kernel(copies, n_in, n_small, row_ref, *refs):
    ins, refs = refs[:n_in], refs[n_in:]
    smalls, refs = refs[:n_small], refs[n_small:]
    outs, wide = refs[:-1], refs[-1]
    for source, source_index, target, target_index in copies:
        index = tuple(item(row_ref[0]) if callable(item) else item for item in source_index)
        outs[target][target_index] = ins[source][index]
    if n_small:
        gain_ref, shift_ref, bias_ref = smalls
        wide[...] = jnp.zeros_like(wide)
        for block in range(2):
            wide[2 * block : 2 * block + 2, : gain_ref.shape[2]] = gain_ref[block].astype(F32)
            wide[4 + 2 * block : 6 + 2 * block, : gain_ref.shape[2]] = shift_ref[block].astype(F32)
        wide[8:10, : bias_ref.shape[1]] = bias_ref[...].astype(F32)
        width = outs[0].shape[1] - LANES
        outs[0][:, width:] = wide[...].astype(BF)


def unpack_kernel(place_ref, *refs):
    pieces, (vecs_ref, biases_ref, held, sem) = refs[:-4], refs[-4:]
    first = 0
    for piece in pieces:
        count = piece.shape[0]
        width = piece.shape[2] - LANES
        pltpu.make_async_copy(
            piece.at[:, :, pl.ds(width, LANES)], held.at[pl.ds(first, count)], sem
        ).start()
        first += count
    pltpu.make_async_copy(held, held, sem).wait()
    values = held[...].astype(F32)
    place = place_ref[...][:, :1]
    slabs = place.shape[0]

    def row(idx, length):
        each = length // slabs
        lane = lax.broadcasted_iota(jnp.int32, (LANES, length), 1)
        source = lax.broadcasted_iota(jnp.int32, (LANES, length), 0)
        choose = jnp.where(lane % each == source, 1.0, 0.0).astype(BF)
        wide = dot(values[:, idx, :].astype(BF), choose, 1, 0)
        mine = lax.broadcasted_iota(jnp.int32, (1, length), 1) // each == place
        return jnp.sum(jnp.where(mine, wide, 0.0), 0, keepdims=True)

    model, width = vecs_ref.shape[2], biases_ref.shape[2]
    for block in range(2):
        for norm in range(2):
            vecs_ref[block, 2 * norm : 2 * norm + 1] = row(2 * block + norm, model)
            vecs_ref[block, 2 * norm + 1 : 2 * norm + 2] = row(4 + 2 * block + norm, model)
        biases_ref[block] = row(8 + block, width)


def finish_kernel(*refs):
    parts = [refs[4 * idx : 4 * idx + 4] for idx in range(3)]
    gain_ref, shift_ref, qkv_ref, proj_ref, in_ref, b_in_ref, out_ref = refs[12:]

    def total(idx, first, cols):
        return add_up(*[ref[0, :, first : first + cols] for ref in parts[idx]])

    model, width = proj_ref.shape[2], in_ref.shape[2]
    triple, rows = 3 * model, proj_ref.shape[1]
    start = triple + model
    qkv_ref[0] = total(0, 0, triple)
    qkv_ref[1] = total(2, 0, triple)
    proj_ref[0] = total(0, triple, model)
    proj_ref[1] = total(2, triple, model)
    in_ref[0] = total(1, 0, width)
    in_ref[1] = total(2, start, width)
    for idx in range(width // model):
        out_ref[0, idx * rows : (idx + 1) * rows] = total(1, width + idx * model, model)
        out_ref[1, idx * rows : (idx + 1) * rows] = total(2, start + width + idx * model, model)
    small = total(0, start, LANES)
    wide = gain_ref.shape[2]
    for block in range(2):
        for norm in range(2):
            first = (2 * block + norm) * wide
            gain_ref[block, norm : norm + 1] = small[0:1, first : first + wide]
            first += 4 * wide
            shift_ref[block, norm : norm + 1] = small[0:1, first : first + wide]
        cols = b_in_ref.shape[1]
        b_in_ref[block : block + 1] = small[1:2, block * cols : (block + 1) * cols]


def add_kernel(count, plans, *refs):
    outs = refs[2 * count :]
    for out, parts in zip(outs, plans):
        for pair, index, first, cols, to_col in parts:
            place = index + (slice(first, first + cols),)
            value = add_up(refs[2 * pair][place], refs[2 * pair + 1][place])
            out[..., to_col : to_col + cols] = value.astype(out.dtype)


def place_kernel(table_ref, _, come_ref, out_ref):
    out_ref[...] = come_ref[...]


ANY = pl.BlockSpec(memory_space=pl.ANY)
SMEM = pl.BlockSpec(memory_space=pltpu.SMEM)
Shape = jax.ShapeDtypeStruct


def whole(shape):
    return pl.BlockSpec(shape, lambda idx, *_: (0,) * len(shape))


def leading(shape):
    return pl.BlockSpec(shape, lambda idx, *_: (idx,) + (0,) * (len(shape) - 1))


def mine(shape, blocks):
    rest = (0,) * (len(shape) - 1)
    return pl.BlockSpec(shape, lambda idx, table: (table[HERE, 0] * blocks + idx,) + rest)


def limits(megabytes):
    return pltpu.CompilerParams(vmem_limit_bytes=megabytes * MIB)


def cost(flops, bytes_accessed):
    return pl.CostEstimate(flops=flops, bytes_accessed=bytes_accessed, transcendentals=0)


def pack(row, sources, targets, copies, smalls, name):
    vmem = pl.BlockSpec(memory_space=pltpu.VMEM)
    return pl.pallas_call(
        functools.partial(pack_kernel, copies, len(sources), len(smalls)),
        in_specs=[SMEM] + [vmem] * (len(sources) + len(smalls)),
        out_specs=[vmem] * len(targets),
        out_shape=[Shape(shape, BF) for shape in targets],
        scratch_shapes=[pltpu.VMEM((16, LANES), F32)],
        compiler_params=limits(60),
        name=name,
    )(row, *sources, *smalls)


def finish(parts, shapes):
    vmem = pl.BlockSpec(memory_space=pltpu.VMEM)
    return pl.pallas_call(
        finish_kernel,
        in_specs=[vmem] * 12,
        out_specs=[vmem] * 7,
        out_shape=[Shape(shape, F32) for shape in shapes],
        compiler_params=limits(60),
        name="finish",
    )(*parts)


def add_pairs(pairs, outs, name):
    vmem = pl.BlockSpec(memory_space=pltpu.VMEM)
    return pl.pallas_call(
        functools.partial(add_kernel, len(pairs), tuple(parts for _, parts in outs)),
        in_specs=[vmem] * (2 * len(pairs)),
        out_specs=[vmem] * len(outs),
        out_shape=[Shape(shape, BF) for shape, _ in outs],
        compiler_params=limits(60),
        name=name,
    )(*[item for pair in pairs for item in pair])


def put_back(table, full, come):
    frames = come.shape[0]
    each = frames // 2
    block = (each,) + come.shape[1:]

    def target(idx, table):
        return ((1 - table[HERE, 0]) * 2 + idx, 0, 0)

    return pl.pallas_call(
        place_kernel,
        grid_spec=pltpu.PrefetchScalarGridSpec(
            num_scalar_prefetch=1,
            grid=(2,),
            in_specs=[ANY, leading(block)],
            out_specs=pl.BlockSpec(block, target),
        ),
        out_shape=Shape(full.shape, BF),
        input_output_aliases={1: 0},
        compiler_params=limits(60),
        name="put_back",
    )(table, full, come)


def unpack(place, pieces, model, width):
    slabs, rows = place.shape[0], pieces[0].shape[1]
    vmem = pl.BlockSpec(memory_space=pltpu.VMEM)
    return pl.pallas_call(
        unpack_kernel,
        in_specs=[vmem] + [ANY] * len(pieces),
        out_specs=[vmem] * 2,
        out_shape=[Shape((2, 4, model), F32), Shape((2, 1, width), F32)],
        scratch_shapes=[pltpu.VMEM((slabs, rows, LANES), BF), pltpu.SemaphoreType.DMA],
        compiler_params=limits(60),
        name="unpack",
    )(place, *pieces)


class Weight:
    def __init__(self, shape, segments):
        self.shape = shape
        self.segments = segments


def call(kernel, name, table, groups, weights, static, inputs, outputs, scratch, grid, flops, traffic, first):
    names = []
    for weight in weights:
        for segment in weight.segments:
            if segment[0] not in names:
                names.append(segment[0])
    specs = tuple(
        tuple((names.index(segment[0]),) + tuple(segment[1:]) for segment in weight.segments)
        for weight in weights
    )
    pieces = [tuple(groups[item]) for item in names] + [tuple(first)]
    counts = tuple(len(item) for item in pieces)
    pieces = [item for group in pieces for item in group]
    return pl.pallas_call(
        functools.partial(kernel, specs, counts, *static),
        grid_spec=pltpu.PrefetchScalarGridSpec(
            num_scalar_prefetch=1,
            grid=(grid,),
            in_specs=[ANY] * len(pieces) + [spec for _, spec in inputs],
            out_specs=[spec for _, spec in outputs],
            scratch_shapes=[pltpu.VMEM(weight.shape, BF) for weight in weights]
            + scratch
            + [pltpu.SemaphoreType.DMA((len(weights),))],
        ),
        out_shape=[shape for shape, _ in outputs],
        compiler_params=limits(60),
        cost_estimate=cost(flops, traffic),
        name=name,
    )(table, *pieces, *[value for value, _ in inputs])


def spatial_forward(table, groups, weights, own, other, vec, first=()):
    frames, half, model = other.shape
    patches = 2 * half
    each = min(2, frames)
    parts = model // JOINED
    spread = patches * (JOINED * HEADS // model)
    return call(
        spatial_forward_kernel,
        "spatial_forward",
        table,
        groups,
        weights,
        (),
        [
            (own, mine((each, half, model), frames // each)),
            (other, leading((each, half, model))),
            (vec, whole(vec.shape)),
        ],
        [
            (Shape((frames, patches, model), F32), leading((each, patches, model))),
            (Shape((frames, patches, model), BF), leading((each, patches, model))),
            (Shape((frames, patches, 3 * model), BF), leading((each, patches, 3 * model))),
            (Shape((frames, patches, model), BF), leading((each, patches, model))),
            (
                Shape((frames, parts, patches, spread), BF),
                leading((each, parts, patches, spread)),
            ),
        ],
        [],
        frames // each,
        2 * frames * patches * model * (4 * model + 2 * patches),
        frames * patches * model * 24,
        first,
    )


def feed_forward(table, groups, weights, middle, vec, b_in, first=()):
    tokens, model = middle.shape
    width = b_in.shape[1]
    block = min(512, tokens)
    return call(
        feed_forward_kernel,
        "feed_forward",
        table,
        groups,
        weights,
        (),
        [
            (middle, leading((block, model))),
            (vec, whole(vec.shape)),
            (b_in, whole(b_in.shape)),
        ],
        [
            (Shape((tokens, model), F32), leading((block, model))),
            (Shape((tokens, model), BF), leading((block, model))),
            (Shape((tokens, width), BF), leading((block, width))),
            (Shape((tokens, width), BF), leading((block, width))),
        ],
        [],
        tokens // block,
        4 * tokens * model * width,
        tokens * (8 * model + 4 * width),
        first,
    )


def feed_backward(table, groups, weights, grad, middle, slope, vec, first=()):
    tokens, model = middle.shape
    width = slope.shape[1]
    block = min(512, tokens)
    small = (8, 2 * model + width)
    return call(
        feed_backward_kernel,
        "feed_backward",
        table,
        groups,
        weights,
        (),
        [
            (grad, leading((block, model))),
            (middle, leading((block, model))),
            (slope, leading((block, width))),
            (vec, whole(vec.shape)),
        ],
        [
            (Shape((tokens, model), F32), leading((block, model))),
            (Shape((tokens, model), BF), leading((block, model))),
            (Shape((tokens, width), BF), leading((block, width))),
            (Shape(small, F32), whole(small)),
        ],
        [],
        tokens // block,
        4 * tokens * model * width,
        tokens * (14 * model + 4 * width),
        first,
    )


def spatial_backward(table, groups, weights, grad, own, other, mixed, prob, vec, first=()):
    frames, half, model = other.shape
    patches = 2 * half
    each = min(2, frames)
    small = (8, 2 * model)
    return call(
        spatial_backward_kernel,
        "spatial_backward",
        table,
        groups,
        weights,
        (),
        [
            (grad, leading((each, patches, model))),
            (own, mine((each, half, model), frames // each)),
            (other, leading((each, half, model))),
            (mixed, leading((each, patches, 3 * model))),
            (prob, leading((each,) + prob.shape[1:])),
            (vec, whole(vec.shape)),
        ],
        [
            (Shape(own.shape, BF), mine((each, half, model), frames // each)),
            (Shape((frames, half, model), BF), leading((each, half, model))),
            (Shape((frames, patches, model), BF), leading((each, patches, model))),
            (Shape((frames, patches, 3 * model), BF), leading((each, patches, 3 * model))),
            (Shape(small, F32), whole(small)),
        ],
        [pltpu.VMEM((each * patches, model), BF)],
        frames // each,
        2 * frames * patches * model * (4 * model + 4 * patches),
        frames * patches * model * 30,
        first,
    )


def temporal_block(table, groups, weights, rows, own, other, vec, b_in, allowed, first=()):
    steps, patches, model = rows.shape
    width = b_in.shape[1]
    half = other.shape[1]
    each = min(64, half)
    tile = min(16, each)
    halves = half // each
    last = halves - 1
    count = steps * each
    total = steps * patches
    same = jnp.eye(tile, dtype=jnp.bool_)
    bias = jnp.where(
        allowed.T[:, None, :, None] & same[None, :, None, :], 0.0, -1000000000.0
    ).astype(F32)
    bias = bias.reshape(steps * tile, steps * tile)
    small = (8, 4 * model + width)
    block = (steps, each, model)
    spread = steps * tile * (JOINED * HEADS // model)
    mine_part = pl.BlockSpec(
        block, lambda idx, table: (table[HERE, 0], jnp.minimum(idx, last), 0)
    )
    other_part = pl.BlockSpec(block, lambda idx, _: (0, jnp.maximum(idx - halves, 0), 0))
    return call(
        temporal_kernel,
        "temporal_block",
        table,
        groups,
        weights,
        (tile,),
        [
            (rows, pl.BlockSpec(block, lambda idx, _: (0, idx, 0))),
            (own, mine_part),
            (other, other_part),
            (vec, whole(vec.shape)),
            (b_in, whole(b_in.shape)),
            (bias, whole(bias.shape)),
        ],
        [
            (Shape(own.shape, BF), mine_part),
            (Shape((steps, half, model), BF), other_part),
            (Shape((steps, patches, model), F32), pl.BlockSpec(block, lambda idx, _: (0, idx, 0))),
            (Shape(small, F32), whole(small)),
            (Shape((total, model), BF), leading((count, model))),
            (Shape((total, model), BF), leading((count, model))),
            (Shape((total, model), BF), leading((count, model))),
            (Shape((total, width), BF), leading((count, width))),
            (Shape((total, model), BF), leading((count, model))),
            (Shape((total, width), BF), leading((count, width))),
            (Shape((total, model), BF), leading((count, model))),
            (Shape((total, 3 * model), BF), leading((count, 3 * model))),
        ],
        [
            pltpu.VMEM((count, 3 * model), BF),
            pltpu.VMEM((each // tile, model // JOINED, steps * tile, spread), BF),
            pltpu.VMEM((count, width), BF),
            pltpu.VMEM((count, model), BF),
        ],
        2 * halves,
        4 * total * model * (4 * model + 2 * width),
        total * (40 * model + 4 * width),
        first,
    )


def weight_grads(table, which, n_out, slabs, jobs, name, small=None, first=()):
    tile = 512
    tokens = jobs[0][0].shape[0]
    plans, operands, in_specs = [], [], []
    col, begin, flops = 0, 0, 0
    rows = None
    for left, right, by_rows in jobs:
        tiles = (left if by_rows else right).shape[1] // tile

        def moving(idx, begin=begin, tiles=tiles):
            return 0, jnp.clip(idx - begin, 0, tiles - 1)

        def still(idx):
            return 0, 0

        plans.append((len(operands), len(operands) + 1, by_rows, col, tiles))
        operands += [left, right]
        left_cols = tile if by_rows else left.shape[1]
        right_cols = right.shape[1] if by_rows else tile
        in_specs += [
            pl.BlockSpec((tokens, left_cols), moving if by_rows else still),
            pl.BlockSpec((tokens, right_cols), still if by_rows else moving),
        ]
        if not by_rows:
            rows = left.shape[1] // slabs
        begin += tiles
        col += left.shape[1] * right.shape[1] // (tile if by_rows else left.shape[1])
        flops += 2 * tokens * left.shape[1] * right.shape[1]
    n_in = len(operands)
    extra = []
    if small is not None:
        place = jnp.broadcast_to(table[which][:, None], (slabs, LANES))
        extra = [place, *small]
        col += LANES
    return pl.pallas_call(
        functools.partial(
            weight_grad_kernel, tuple(plans), which, rows, n_in, n_out, int(small is not None)
        ),
        grid=(begin,),
        in_specs=[SMEM]
        + in_specs
        + [whole(item.shape) for item in extra]
        + [ANY] * len(first),
        out_specs=[ANY] * n_out + [whole((8, LANES))],
        out_shape=[Shape((slabs // n_out, rows, col), BF)] * n_out + [Shape((8, LANES), F32)],
        scratch_shapes=[pltpu.VMEM((begin, tile, tile), BF), pltpu.SemaphoreType.DMA]
        + ([pltpu.VMEM((slabs, rows, LANES), BF)] if small is not None else []),
        compiler_params=limits(60),
        cost_estimate=cost(flops, flops // 512),
        name=name,
    )(table, *operands, *extra, *first)


def plain_grad(left, right):
    grad = dot(left, right, 0, 0)
    return lax.psum_scatter(grad, AXES, scatter_dimension=0, tiled=True)


class Plan:
    def __init__(self, mesh):
        self.dp = mesh.shape["dp"]
        self.seq = mesh.shape["seq"]
        self.count = self.dp * self.seq
        self.cube = self.dp == 16 and self.seq == 2

    def swap(self, value, mask):
        pairs = [(idx, idx ^ mask) for idx in range(self.count)]
        return lax.ppermute(value, AXES, pairs)

    def me(self):
        return lax.axis_index("dp") * self.seq + lax.axis_index("seq")


ROW, CORE, COLUMN, Z_LOW, Z_HIGH = 1, 2, 4, 8, 16


def gather_masks(order):
    masks = [0]
    for stage in order:
        masks = masks + [mask ^ bit for bit in stage for mask in masks]
    return masks


STAGE_Z = (Z_LOW, Z_HIGH, Z_LOW | Z_HIGH)
GATHER_A = (STAGE_Z, (COLUMN,), (ROW,), (CORE,))
GATHER_B = (STAGE_Z, (ROW,), (COLUMN,), (CORE,))
GATHER_C = ((ROW,), STAGE_Z, (COLUMN,), (CORE,))


def join(*values, axis=0):
    total = sum(value.shape[axis] for value in values)
    low = jnp.array(-jnp.inf, values[0].dtype)
    joined, first = None, 0
    for value in values:
        count = value.shape[axis]
        sides = [(0, 0, 0)] * value.ndim
        sides[axis] = (first, total - first - count, 0)
        padded = lax.pad(value, low, sides)
        joined = padded if joined is None else jnp.maximum(joined, padded)
        first += count
    return joined


SUM_A = (CORE, COLUMN, ROW, Z_HIGH, Z_LOW)


def sum_masks(order):
    masks = [0]
    for bit in reversed(order):
        masks = masks + [mask ^ bit for mask in masks]
    return masks


def add_up(*values):
    total = values[0].astype(F32)
    for value in values[1:]:
        total = total + value.astype(F32)
    return total


class Sum:
    def __init__(self, plan, keep, send, cut):
        self.plan = plan
        self.keep, self.away = keep, send
        self.cut = cut

    def send_core(self):
        return self.plan.swap(self.away, CORE)

    def add_core(self, come):
        rows, cols = self.keep.shape[1:]
        shape = (2, 2, 4, rows, cols)
        cut, every = self.cut, slice(None)
        outs = []
        for first, size, index in ((0, cut, 0), (cut, cols - cut, 1)):
            for half in range(2):
                lead = (half, every) if index == 0 else (every, half)
                part = (0, lead + (every, every), first, size, 0)
                outs.append(((2, 4, rows, size), (part,)))
        sums = add_pairs([(self.keep.reshape(shape), come.reshape(shape))], outs, "add_core")
        self.keep, self.away = [sums[0], sums[2]], [sums[1], sums[3]]

    def send_first(self):
        return [self.plan.swap(item, bit) for item, bit in zip(self.away, (COLUMN, ROW))]

    def add_first(self, come):
        pairs = list(zip(self.keep, come))
        every = slice(None)
        outs = []
        for pair, (keep, _) in enumerate(pairs):
            for half in range(2):
                part = (pair, (half, every, every), 0, keep.shape[3], 0)
                outs.append((keep.shape[1:], (part,)))
        sums = add_pairs(pairs, outs, "add_first")
        self.keep, self.away = [sums[0], sums[2]], [sums[1], sums[3]]

    def send_second(self):
        return [self.plan.swap(item, bit) for item, bit in zip(self.away, (ROW, COLUMN))]

    def add_second(self, come):
        pairs = list(zip(self.keep, come))
        every = slice(None)
        _, rows, cols = self.keep[0].shape
        total = cols + self.keep[1].shape[2]
        outs = []
        for idx in range(4):
            lead = (slice(idx, idx + 1), every)
            parts = ((0, lead, 0, cols, 0), (1, lead, 0, total - cols, cols))
            outs.append(((1, rows, total), parts))
        sums = add_pairs(pairs, outs, "add_second")
        self.keep, self.away = sums[0], sums[1:]

    def send_last(self):
        one, two, both = self.away
        swap = self.plan.swap
        return [swap(one, Z_LOW), swap(two, Z_HIGH), swap(both, Z_LOW | Z_HIGH)]


def together(*values):
    return lax.optimization_barrier(values)


def to_frames(plan, values):
    full = lax.all_to_all(values, "seq", split_axis=0, concat_axis=1, tiled=True)
    half = full.shape[1] // 2
    return full[:, :half], full[:, half:]


def from_frames(plan, own, other):
    full = jnp.concatenate([own, other], 1)
    return lax.all_to_all(full, "seq", split_axis=1, concat_axis=0, tiled=True)


def regroup(plan, values, split_axis, concat_axis):
    members = plan.seq // MICRO
    if members == 1:
        return values
    row = lax.axis_index("seq")
    rank = row % members
    size = values.shape[split_axis] // members
    span = values.shape[concat_axis]
    shape = list(values.shape)
    shape[split_axis] = size
    shape[concat_axis] = span * members
    result = jnp.zeros(shape, values.dtype)
    for shift in range(members):
        target = (rank + shift) % members
        part = lax.dynamic_slice_in_dim(values, target * size, size, split_axis)
        if shift:
            pairs = [
                (idx, idx - idx % members + (idx + shift) % members) for idx in range(plan.seq)
            ]
            part = lax.ppermute(part, "seq", pairs)
        source = (rank - shift) % members
        result = lax.dynamic_update_slice_in_dim(result, part, source * span, concat_axis)
    return result


def clip_mask(lengths, steps):
    ends = jnp.cumsum(lengths, -1)
    positions = jnp.arange(steps, dtype=jnp.int32)
    clips = jnp.sum((positions[:, None] >= ends[None, :]).astype(jnp.int32), -1)
    return (clips[:, None] == clips[None, :]) & (positions[None, :] <= positions[:, None])


def plain_weights(plan, weights, small):
    groups, blocks = {}, []
    for idx in range(2):
        block = []
        for name, value in zip(("qkv", "proj", "in", "out"), weights):
            key = name + str(idx)
            whole_value = lax.all_gather(value[idx], AXES, axis=0, tiled=True)
            groups[key] = [whole_value[None]]
            block.append(Weight(whole_value.shape, ((key, AS_IS, 0, value.shape[2], 0, 1, 0),)))
        blocks.append(block)
    return groups, blocks, lax.all_gather(small, AXES, axis=0).astype(F32)


def cube_weights(shapes, fold):
    (model, triple), _, (_, width), _ = shapes
    start = triple + model + width
    first = [
        Weight(shapes[0], (("att0", FROM_C, 0, triple, 0, 1, 0),)),
        Weight(shapes[1], (("att0", FROM_C, triple, model, 0, 1, 0),)),
        Weight(shapes[2], (("in0", FROM_A, 0, width, 0, 1, 0),)),
        Weight(
            shapes[3],
            tuple(("out0", FROM_B, idx * model, model, idx, fold, 0) for idx in range(fold)),
        ),
    ]
    last = [
        Weight(shapes[0], (("last", AS_IS, 0, triple, 0, 1, 0),)),
        Weight(shapes[1], (("last", AS_IS, triple, model, 0, 1, 0),)),
        Weight(shapes[2], (("last", AS_IS, triple + model, width, 0, 1, 0),)),
        Weight(
            shapes[3],
            tuple(("last", AS_IS, start + idx * model, model, idx, fold, 0) for idx in range(fold)),
        ),
    ]
    return [first, last]


def cube_packs(plan, row, tokens, weights, smalls):
    w_qkv, w_proj, w_in, w_out = weights
    rows, triple = w_qkv.shape[1:]
    model, width = w_proj.shape[2], w_in.shape[2]
    fold = w_out.shape[1] // rows
    start = triple + model + width
    steps, here = tokens.shape[1:3]
    count = steps // 2

    def cols(first, size):
        return (slice(None), pl.ds(first, size))

    copies = [
        (0, (0,), 0, cols(0, triple)),
        (1, (0,), 0, cols(triple, model)),
        (4, (0, lambda me: pl.ds((1 - me) * count, count)), 3, (slice(None),)),
        (2, (0,), 1, cols(0, width)),
        (0, (1,), 2, cols(0, triple)),
        (1, (1,), 2, cols(triple, model)),
        (2, (1,), 2, cols(triple + model, width)),
    ]
    for idx in range(fold):
        part = pl.ds(idx * rows, rows)
        copies.append((3, (0, part), 1, cols(width + idx * model, model)))
        copies.append((3, (1, part), 2, cols(start + idx * model, model)))
    targets = [
        (rows, triple + model + LANES),
        (rows, width + fold * model),
        (rows, start + fold * model),
        (count, here, model),
    ]
    return pack(row, [*weights, tokens], targets, copies, smalls, "pack")


def on_device(plan, tokens, lengths, cotangent, norm_gain, norm_bias, w_qkv, w_proj, w_in, b_in, w_out):
    steps_all, here, model = tokens.shape[1:]
    steps = steps_all // MICRO
    width = b_in.shape[1] * plan.count
    row = lax.axis_index("seq")
    micro = row * MICRO // plan.seq
    allowed = clip_mask(lax.dynamic_index_in_dim(lengths[0], micro, 0, keepdims=False), steps)

    weights = (w_qkv, w_proj, w_in, w_out)
    shapes = ((model, 3 * model), (model, model), (model, width), (width, model))
    wide = model // plan.count
    cut = 4 * wide
    slabs = plan.count
    waits = ()
    if plan.cube:
        me = plan.me()
        orders = [gather_masks(GATHER_A), gather_masks(GATHER_B), gather_masks(GATHER_C), sum_masks(SUM_A)]
        table = jnp.concatenate(
            [
                me ^ jnp.array(orders, jnp.int32),
                jnp.arange(plan.count, dtype=jnp.int32)[None],
                jnp.broadcast_to(row, (1, plan.count)).astype(jnp.int32),
            ]
        )
        row_index = jnp.reshape(row, (1,)).astype(jnp.int32)
        own = tokens[0]
        att, feed_0, last, away = cube_packs(
            plan, row_index, tokens, weights, (norm_gain, norm_bias, b_in)
        )
        last = lax.all_gather(last, AXES, axis=0, tiled=True)
        groups = {"last": [last.reshape(plan.count, -1, last.shape[1])]}
        att, feed_0 = att[None], feed_0[None]
        att = join(att, plan.swap(att, ROW))
        *come, feed_0, cotangent = together(
            *[plan.swap(att, bit) for bit in STAGE_Z], feed_0, cotangent
        )
        att = join(att, *come)
        ct_own = cotangent[0]
        (ct_away,) = pack(
            row_index,
            [cotangent],
            [away.shape],
            [(0, (0, lambda me: pl.ds((1 - me) * steps, steps)), 0, (slice(None),))],
            (),
            "pack_cotangent",
        )
        come, other, *feed_come, ct_away = together(
            plan.swap(att, COLUMN),
            plan.swap(away, ROW),
            *[plan.swap(feed_0, bit) for bit in STAGE_Z],
            ct_away,
        )
        ct_other = plan.swap(ct_away, ROW)
        att = join(att, come)
        parts = [feed_0] + feed_come
        part_a = join(*[item[:, :, :width] for item in parts])
        part_b = join(*[item[:, :, width:] for item in parts])
        att_come, *come = together(
            plan.swap(att, CORE), plan.swap(part_a, COLUMN), plan.swap(part_b, ROW)
        )
        groups["att0"] = [att, att_come]
        part_a, part_b = join(part_a, come[0]), join(part_b, come[1])
        moving = [plan.swap(part_a, ROW), plan.swap(part_b, COLUMN)]
        waits = (part_a, part_b)
        place = jnp.broadcast_to(table[FROM_C][:, None], (slabs, LANES))
        vecs, biases = unpack(place, groups["att0"], model, width)
        blocks = cube_weights(shapes, w_out.shape[1] // w_in.shape[1])
    else:
        own, other = to_frames(plan, tokens[0])
        table = jnp.zeros((6, 1), jnp.int32)
        small = jnp.concatenate([norm_gain.reshape(-1), norm_bias.reshape(-1), b_in.reshape(-1)])
        groups, blocks, small_all = plain_weights(plan, weights, small)
        gains = small_all[:, :cut].reshape(plan.count, 2, 2, wide)
        shifts = small_all[:, cut : 2 * cut].reshape(plan.count, 2, 2, wide)
        gains = gains.transpose(1, 2, 0, 3).reshape(2, 2, model)
        shifts = shifts.transpose(1, 2, 0, 3).reshape(2, 2, model)
        vecs = jnp.stack([gains, shifts], 2).reshape(2, 4, model)
        biases = small_all[:, 2 * cut :]
        biases = biases.reshape(plan.count, 2, -1).transpose(1, 0, 2).reshape(2, 1, width)

    middle, normed_0, mixed, attended, prob = spatial_forward(
        table, groups, blocks[0][:2], own, other, vecs[0], waits
    )
    frames, patches = middle.shape[:2]
    count = frames * patches
    middle = middle.reshape(count, model)
    if plan.cube:
        *moving, middle = together(*moving, middle)
        part_a, part_b = join(part_a, moving[0]), join(part_b, moving[1])
        groups["in0"] = [part_a, plan.swap(part_a, CORE)]
        groups["out0"] = [part_b, plan.swap(part_b, CORE)]
    result, second_0, hidden, slope = feed_forward(
        table, groups, blocks[0][2:], middle, vecs[0], biases[0]
    )
    if plan.cube:
        ct_other, result = together(ct_other, result)
    else:
        ct_own, ct_other = to_frames(plan, cotangent[0])
    rows = regroup(plan, result.reshape(frames, patches, model), 1, 0)
    if plan.seq != 2:
        full = regroup(plan, jnp.concatenate([ct_own, ct_other], 1), 1, 0)
        cut_at = full.shape[1] // 2
        ct_own, ct_other = full[:, :cut_at], full[:, cut_at:]
    (
        active_own,
        active_other,
        grad,
        small_1,
        normed_1,
        attended_1,
        second_1,
        hidden_1,
        branch_1,
        grad_pre_1,
        proj_in_1,
        grad_mixed_1,
    ) = temporal_block(
        table, groups, blocks[1], rows, ct_own, ct_other, vecs[1], biases[1], allowed
    )
    grad = regroup(plan, grad, 0, 1).reshape(count, model)

    def flat(values):
        return values.reshape(count, values.shape[-1])

    pairs_1 = [
        (normed_1, grad_mixed_1, False),
        (attended_1, proj_in_1, False),
        (second_1, grad_pre_1, False),
        (hidden_1, branch_1, True),
    ]
    waits = ()
    if plan.cube:
        keep, send, over = weight_grads(table, TO_A, 2, slabs, pairs_1, "grads_last")
        active_come, send = together(plan.swap(active_other, ROW), send)
        s_last = Sum(plan, keep, send, keep.shape[2] // 2)
        last_come = s_last.send_core()
        waits = (over,)

    grad_middle, branch_0, grad_pre_0, small_0 = feed_backward(
        table, groups, blocks[0][2:], grad, middle, slope, vecs[0], waits
    )
    pairs_0 = [(second_0, grad_pre_0, False), (hidden, branch_0, True)]
    waits = ()
    if plan.cube:
        last_come, branch_0 = together(last_come, branch_0)
        pairs_0[1] = (hidden, branch_0, True)
        s_last.add_core(last_come)
        last_come = s_last.send_first()
        keep, send, over = weight_grads(
            table, TO_A, 2, slabs, pairs_0, "grads_feed", None, s_last.keep
        )
        *last_come, send = together(*last_come, send)
        s_feed = Sum(plan, keep, send, keep.shape[2] // 2)
        s_last.add_first(last_come)
        s_feed.add_core(s_feed.send_core())
        last_come, feed_come = s_last.send_second(), s_feed.send_first()
        waits = (*s_last.keep, *s_feed.keep)
    grad_own, grad_other, proj_in_0, grad_mixed_0, tiny_0 = spatial_backward(
        table,
        groups,
        blocks[0][:2],
        grad_middle.reshape(frames, patches, model),
        own,
        other,
        mixed,
        prob,
        vecs[0],
        waits,
    )
    pairs_2 = [
        (flat(normed_0), flat(grad_mixed_0), False),
        (flat(attended), flat(proj_in_0), False),
    ]
    if plan.cube:
        *come, grad_other = together(*feed_come, *last_come, grad_other)
        cut_at = grad_other.shape[0] // 2
        tokens_come = [plan.swap(grad_other[:cut_at], ROW)]
        s_feed.add_first(come[:2])
        s_last.add_second(come[2:])
        feed_come, last_come = s_feed.send_second(), s_last.send_last()
        waits = (*s_feed.keep, s_last.keep)
        keep, send, _ = weight_grads(
            table, TO_A, 2, slabs, pairs_2, "grads_attention", (tiny_0, small_0, small_1), waits
        )
        *feed_come, tokens_come[0], grad_other, send = together(
            *feed_come, *tokens_come, grad_other, send
        )
        *last_come, send = together(*last_come, send)
        s_att = Sum(plan, keep, send, 2 * model)
        tokens_come.append(plan.swap(grad_other[cut_at:], ROW))
        s_att.add_core(s_att.send_core())
        att_come = s_att.send_first()
        s_feed.add_second(feed_come)
        feed_come = s_feed.send_last()
        s_att.add_first(together(*att_come))
        att_come = s_att.send_second()
        *come, att_come[0], att_come[1] = together(*feed_come, *last_come, *att_come)
        s_att.add_second(att_come)
        *att_come, tokens_come[1] = together(*s_att.send_last(), tokens_come[1])
        outs = finish(
            [
                s_att.keep,
                *att_come,
                s_feed.keep,
                *come[:3],
                s_last.keep,
                *come[3:],
            ],
            [
                norm_gain.shape,
                norm_bias.shape,
                w_qkv.shape,
                w_proj.shape,
                w_in.shape,
                b_in.shape,
                w_out.shape,
            ],
        )
        activations = put_back(table, active_own, active_come)
        grad_tokens = put_back(table, grad_own, join(*tokens_come))
        return (activations[None], grad_tokens[None], *outs)

    active = regroup(plan, jnp.concatenate([active_own[:steps], active_other], 1), 0, 1)
    half = active.shape[1] // 2
    activations = from_frames(plan, active[:, :half], active[:, half:])
    grad_tokens = from_frames(plan, grad_own, grad_other)
    each = [(pairs_2 + pairs_0), pairs_1]
    sums = [
        tuple(plain_grad(*each[block][item][:2]) for block in range(2)) for item in range(4)
    ]
    tiny_0, small_0, small_1 = [jnp.sum(item, 0) for item in (tiny_0, small_0, small_1)]
    far = 2 * model + width
    columns = [
        tiny_0[:model],
        small_0[:model],
        small_1[far : far + model],
        small_1[:model],
        tiny_0[model:],
        small_0[model : 2 * model],
        small_1[far + model :],
        small_1[model : 2 * model],
        small_0[2 * model :],
        small_1[2 * model : far],
    ]
    smalls = jnp.concatenate([item.reshape(plan.count, -1) for item in columns], 1)
    mine = lax.psum_scatter(smalls, AXES, scatter_dimension=0, tiled=True).reshape(-1)
    grad_gain = mine[:cut].reshape(2, 2, wide)
    grad_shift = mine[cut : 2 * cut].reshape(2, 2, wide)
    grad_b_in = mine[2 * cut :].reshape(2, -1)
    return (
        activations[None],
        grad_tokens[None],
        grad_gain,
        grad_shift,
        jnp.stack(sums[0]),
        jnp.stack(sums[1]),
        jnp.stack(sums[2]),
        grad_b_in,
        jnp.stack(sums[3]),
    )


def solution(mesh):
    in_specs = (
        P("dp", None, "seq", None),
        P("dp", None, None),
        P("dp", None, "seq", None),
        P(None, None, AXES),
        P(None, None, AXES),
        P(None, AXES, None),
        P(None, AXES, None),
        P(None, AXES, None),
        P(None, AXES),
        P(None, AXES, None),
    )
    out_specs = (
        P("dp", None, "seq", None),
        P("dp", None, "seq", None),
        P(None, None, AXES),
        P(None, None, AXES),
        P(None, AXES, None),
        P(None, AXES, None),
        P(None, AXES, None),
        P(None, AXES),
        P(None, AXES, None),
    )
    return jax.shard_map(
        functools.partial(on_device, Plan(mesh)),
        mesh=mesh,
        in_specs=in_specs,
        out_specs=out_specs,
        check_vma=False,
    )
```

```python
import functools

import jax
import jax.numpy as jnp
from jax import lax
from jax.experimental import pallas as pl
from jax.experimental.pallas import tpu as pltpu
from jax.sharding import PartitionSpec as P

HEADS = 8
MICRO = 2
LANES = 128
JOINED = 256
AXES = ("dp", "seq")
BF = jnp.bfloat16
F32 = jnp.float32
MIB = 1 << 20
SHRINK = 1000
FROM_A, FROM_B, FROM_C, TO_A, PLACE, AS_IS, HERE, CLIP_LENGTHS = range(8)


def dot(left, right, left_dim, right_dim):
    return lax.dot_general(
        left, right, (((left_dim,), (right_dim,)), ((), ())), preferred_element_type=F32
    )


def norm_stats(values):
    centre = values - jnp.mean(values, -1, keepdims=True)
    variance = jnp.mean(centre * centre, -1, keepdims=True)
    inverse = lax.rsqrt(variance + 1e-05)
    return centre * inverse, inverse


def norm_back(grad_scaled, unit_rows, inverse):
    mean_grad = jnp.mean(grad_scaled, -1, keepdims=True)
    mean_cross = jnp.mean(grad_scaled * unit_rows, -1, keepdims=True)
    return inverse * (grad_scaled - mean_grad - unit_rows * mean_cross)


def fold_rows(values):
    return jnp.sum(values.reshape(-1, 8, values.shape[-1]), 0)


def gelu_pair(values):
    cumulative = 0.5 * (1.0 + lax.erf(values * 0.7071067811865476))
    slope = cumulative + values * jnp.exp(-0.5 * values * values) * 0.3989422804014327
    return values * cumulative, slope


def start_weight(segments, groups, table_ref, held, sem):
    for group, which, first_col, cols, block, blocks, to_col in segments:
        slab = 0
        for piece in groups[group]:
            rows = piece.shape[1]
            for idx in range(piece.shape[0]):
                first = table_ref[which, slab] * (rows * blocks) + block * rows
                pltpu.make_async_copy(
                    piece.at[idx, :, pl.ds(first_col, cols)],
                    held.at[pl.ds(pl.multiple_of(first, rows), rows), pl.ds(to_col, cols)],
                    sem,
                ).start()
                slab += 1


def wait_weight(held, sem):
    pltpu.make_async_copy(held, held, sem).wait()


def split_refs(refs, counts):
    groups = []
    for count in counts:
        groups.append(refs[:count])
        refs = refs[count:]
    return groups, refs


def spread_heads(values, width, scale):
    lane = lax.broadcasted_iota(jnp.int32, (1, values.shape[-1]), 1)
    parts = []
    for head in range(values.shape[-1] // width):
        inside = (lane >= head * width) & (lane < (head + 1) * width)
        parts.append(values * jnp.where(inside, scale, 0.0).astype(BF))
    return jnp.concatenate(parts, 0)


def merge_heads(values, width):
    lane = lax.broadcasted_iota(jnp.int32, (1, values.shape[-1]), 1)
    count = values.shape[-1] // width
    rows = values.shape[0] // count
    merged = values[(count - 1) * rows :]
    for head in range(count - 2, -1, -1):
        merged = jnp.where(
            lane < (head + 1) * width, values[head * rows : (head + 1) * rows], merged
        )
    return merged


def attend_forward(sets, model, load, store, keep, bias):
    width = model // HEADS
    scale = width ** (-0.5)
    units = [(item, part) for item in range(sets) for part in range(model // JOINED)]

    def before(item, part):
        first = part * JOINED
        queries = spread_heads(load(item, first), width, scale)
        scores = dot(load(item, model + first), queries, 1, 1)
        return scores if bias is None else scores + bias

    scores = before(*units[0])
    for number, (item, part) in enumerate(units):
        following = before(*units[number + 1]) if number + 1 < len(units) else None
        first = part * JOINED
        exponent = jnp.exp(scores - jnp.max(scores, 0, keepdims=True))
        prob = (exponent * (1.0 / jnp.sum(exponent, 0, keepdims=True))).astype(BF)
        keep(item, part, prob)
        result = merge_heads(dot(prob, load(item, 2 * model + first), 0, 0), width)
        store(item, first, result.astype(BF))
        scores = following


def attend_backward(sets, model, load, load_grad, load_prob, store, late):
    width = model // HEADS
    scale = width ** (-0.5)
    units = [(item, part) for item in range(sets) for part in range(model // JOINED)]

    def before(item, part):
        first = part * JOINED
        spread_grad = spread_heads(load_grad(item, first), width, 1.0)
        return spread_grad, dot(load(item, 2 * model + first), spread_grad, 1, 1)

    def finish(item, part, spread_grad, grad_scores):
        first = part * JOINED
        spread_query = spread_heads(load(item, first), width, scale)
        prob = load_prob(item, part)
        store(item, 2 * model + first, dot(prob, spread_grad, 1, 0).astype(BF))
        store(item, model + first, dot(grad_scores, spread_query, 1, 0).astype(BF))
        scaled_key = load(item, model + first) * jnp.asarray(scale, BF)
        result = merge_heads(dot(grad_scores, scaled_key, 0, 0), width)
        store(item, first, result.astype(BF))

    started = before(*units[0]) if late else None
    waiting = None
    for number, (item, part) in enumerate(units):
        following = None
        if late and number + 1 < len(units):
            following = before(*units[number + 1])
        spread_grad, grad_prob = started if late else before(item, part)
        prob = load_prob(item, part).astype(F32)
        total = jnp.sum(prob * grad_prob, 0, keepdims=True)
        grad_scores = (prob * (grad_prob - total)).astype(BF)
        if late:
            if waiting is not None:
                finish(*waiting)
            waiting = (item, part, spread_grad, grad_scores)
            started = following
        else:
            finish(item, part, spread_grad, grad_scores)
    if late:
        finish(*waiting)


def spatial_forward_kernel(specs, counts, table_ref, *refs):
    groups, refs = split_refs(refs, counts)
    (
        own_ref,
        other_ref,
        vec_ref,
        middle_ref,
        normed_ref,
        qkv_ref,
        attended_ref,
        prob_ref,
        w_qkv,
        w_proj,
        sems,
    ) = refs
    frames, half, model = own_ref.shape

    @pl.when(pl.program_id(0) == 0)
    def _():
        start_weight(specs[0], groups, table_ref, w_qkv, sems.at[0])
        start_weight(specs[1], groups, table_ref, w_proj, sems.at[1])
        wait_weight(w_qkv, sems.at[0])
        wait_weight(w_proj, sems.at[1])

    rows = jnp.concatenate([own_ref[...], other_ref[...]], 1).astype(F32)
    rows = rows.reshape(frames * 2 * half, model)
    unit, _ = norm_stats(rows)
    normed = (unit * vec_ref[0:1] + vec_ref[1:2]).astype(BF)
    normed_ref[...] = normed.reshape(normed_ref.shape)
    qkv_ref[...] = dot(normed, w_qkv[...], 1, 0).astype(BF).reshape(qkv_ref.shape)

    def load(frame, first):
        return qkv_ref[frame, :, first : first + JOINED]

    def store(frame, first, value):
        attended_ref[frame, :, first : first + JOINED] = value

    def keep(frame, part, value):
        prob_ref[frame, part] = value

    attend_forward(frames, model, load, store, keep, None)
    attended = attended_ref[...].reshape(rows.shape)
    middle = rows + dot(attended, w_proj[...], 1, 0)
    middle_ref[...] = middle.reshape(middle_ref.shape)


def feed_forward_kernel(specs, counts, table_ref, *refs):
    groups, refs = split_refs(refs, counts)
    (
        middle_ref,
        vec_ref,
        b_in_ref,
        result_ref,
        normed_ref,
        hidden_ref,
        slope_ref,
        w_in,
        w_out,
        sems,
    ) = refs

    @pl.when(pl.program_id(0) == 0)
    def _():
        start_weight(specs[0], groups, table_ref, w_in, sems.at[0])
        start_weight(specs[1], groups, table_ref, w_out, sems.at[1])
        wait_weight(w_in, sems.at[0])
        wait_weight(w_out, sems.at[1])

    middle = middle_ref[...]
    unit, _ = norm_stats(middle)
    normed = (unit * vec_ref[2:3] + vec_ref[3:4]).astype(BF)
    normed_ref[...] = normed
    result_ref[...] = middle + ff_through(normed, b_in_ref, w_in, w_out, hidden_ref, slope_ref)


def ff_through(normed, b_in_ref, w_in, w_out, hidden_ref, slope_ref):
    width = w_in.shape[1]
    chunk = min(512, width)
    starts = range(0, width, chunk)

    def before(first):
        cols = slice(first, first + chunk)
        return dot(normed, w_in[:, cols], 1, 0) + b_in_ref[:, cols]

    total, waiting, pre_act = None, None, before(0)
    for first in starts:
        following = before(first + chunk) if first + chunk < width else None
        cols = slice(first, first + chunk)
        hidden, slope = gelu_pair(pre_act)
        hidden = hidden.astype(BF)
        hidden_ref[:, cols] = hidden
        slope_ref[:, cols] = slope.astype(BF)
        if waiting is not None:
            term = dot(waiting, w_out[first - chunk : first, :], 1, 0)
            total = term if total is None else total + term
        waiting, pre_act = hidden, following
    term = dot(waiting, w_out[width - chunk :, :], 1, 0)
    return term if total is None else total + term


def ff_back(grad_out, branch, unit, inverse, gain, w_in, w_out, slope_ref, grad_pre_ref, small_ref):
    model, width = w_in.shape
    chunk = min(512, width)

    def before(first):
        return dot(branch, w_out[first : first + chunk, :], 1, 1)

    grad_second, waiting, grad_hidden = None, None, before(0)
    for first in range(0, width, chunk):
        following = before(first + chunk) if first + chunk < width else None
        cols = slice(first, first + chunk)
        grad_pre = (grad_hidden * slope_ref[:, cols].astype(F32)).astype(BF)
        grad_pre_ref[:, cols] = grad_pre
        small_ref[:, 2 * model + first : 2 * model + first + chunk] += fold_rows(
            grad_pre.astype(F32)
        )
        if waiting is not None:
            term = dot(waiting, w_in[:, first - chunk : first], 1, 1)
            grad_second = term if grad_second is None else grad_second + term
        waiting, grad_hidden = grad_pre, following
    term = dot(waiting, w_in[:, width - chunk :], 1, 1)
    grad_second = term if grad_second is None else grad_second + term
    small_ref[:, :model] += fold_rows(grad_second * unit)
    small_ref[:, model : 2 * model] += fold_rows(grad_second)
    return grad_out + norm_back(grad_second * gain, unit, inverse)


def feed_backward_kernel(specs, counts, table_ref, *refs):
    groups, refs = split_refs(refs, counts)
    (
        grad_ref,
        middle_ref,
        slope_ref,
        vec_ref,
        grad_middle_ref,
        proj_in_ref,
        branch_ref,
        grad_pre_ref,
        small_ref,
        w_in,
        w_out,
        sems,
    ) = refs

    @pl.when(pl.program_id(0) == 0)
    def _():
        start_weight(specs[0], groups, table_ref, w_in, sems.at[0])
        start_weight(specs[1], groups, table_ref, w_out, sems.at[1])
        small_ref[...] = jnp.zeros_like(small_ref)
        wait_weight(w_in, sems.at[0])
        wait_weight(w_out, sems.at[1])

    unit, inverse = norm_stats(middle_ref[...])
    branch = grad_ref[...].astype(BF)
    branch_ref[...] = branch
    grad_middle = ff_back(
        grad_ref[...],
        branch,
        unit,
        inverse,
        vec_ref[2:3],
        w_in,
        w_out,
        slope_ref,
        grad_pre_ref,
        small_ref,
    )
    grad_middle_ref[...] = grad_middle
    proj_in_ref[...] = grad_middle.astype(BF)


def spatial_backward_kernel(specs, counts, table_ref, *refs):
    groups, refs = split_refs(refs, counts)
    (
        grad_ref,
        own_ref,
        other_ref,
        qkv_ref,
        prob_ref,
        vec_ref,
        grad_own_ref,
        grad_early_ref,
        grad_late_ref,
        grad_mixed_ref,
        small_ref,
        w_qkv,
        w_proj,
        grad_att,
        sems,
    ) = refs
    frames, half, model = own_ref.shape

    @pl.when(pl.program_id(0) == 0)
    def _():
        start_weight(specs[0], groups, table_ref, w_qkv, sems.at[0])
        start_weight(specs[1], groups, table_ref, w_proj, sems.at[1])
        small_ref[...] = jnp.zeros_like(small_ref)
        wait_weight(w_qkv, sems.at[0])
        wait_weight(w_proj, sems.at[1])

    rows = jnp.concatenate([own_ref[...], other_ref[...]], 1).astype(F32)
    rows = rows.reshape(frames * 2 * half, model)
    unit, inverse = norm_stats(rows)
    grad_middle = grad_ref[...].reshape(rows.shape)
    grad_att[...] = dot(grad_middle.astype(BF), w_proj[...], 1, 1).astype(BF)

    def load(frame, first):
        return qkv_ref[frame, :, first : first + JOINED]

    def load_grad(frame, first):
        return grad_att[frame * 2 * half : (frame + 1) * 2 * half, first : first + JOINED]

    def load_prob(frame, part):
        return prob_ref[frame, part]

    def store(frame, first, value):
        grad_mixed_ref[frame, :, first : first + JOINED] = value

    attend_backward(frames, model, load, load_grad, load_prob, store, 0)
    grad_mixed = grad_mixed_ref[...].reshape(rows.shape[0], 3 * model)
    grad_first = dot(grad_mixed, w_qkv[...], 1, 1)
    small_ref[:, :model] += fold_rows(grad_first * unit)
    small_ref[:, model : 2 * model] += fold_rows(grad_first)
    grad_rows = grad_middle + norm_back(grad_first * vec_ref[0:1], unit, inverse)
    grad_rows = grad_rows.astype(BF).reshape(frames, 2 * half, model)
    grad_own_ref[...] = grad_rows[:, :half]
    early = pl.program_id(0) < (pl.num_programs(0) + 1) // 2

    @pl.when(early)
    def _():
        grad_early_ref[...] = grad_rows[:, half:]

    @pl.when(jnp.logical_not(early))
    def _():
        grad_late_ref[...] = grad_rows[:, half:]


def temporal_kernel(specs, counts, tile, clips, halves, table_ref, *refs):
    groups, refs = split_refs(refs, counts)
    (
        rows_ref,
        own_ref,
        other_ref,
        vec_ref,
        b_in_ref,
        active_own_ref,
        *refs,
    ) = refs
    active_other_refs, refs = refs[:halves], refs[halves:]
    (
        grad_ref,
        small_ref,
        normed_one_ref,
        attended_ref,
        normed_two_ref,
        hidden_ref,
        branch_ref,
        grad_pre_ref,
        proj_in_ref,
        grad_mixed_ref,
        w_qkv,
        w_proj,
        w_in,
        w_out,
        mixed,
        probs,
        slope,
        grad_att,
        sems,
    ) = refs
    steps, patches, model = rows_ref.shape
    tiles = patches // tile
    held = (w_qkv, w_proj, w_in, w_out)

    @pl.when(pl.program_id(0) == 0)
    def _():
        for idx in range(4):
            start_weight(specs[idx], groups, table_ref, held[idx], sems.at[idx])
        small_ref[...] = jnp.zeros_like(small_ref)
        for idx in range(4):
            wait_weight(held[idx], sems.at[idx])

    def gather_rows(ref):
        parts = [
            ref[:, idx * tile : (idx + 1) * tile, :].reshape(steps * tile, model)
            for idx in range(tiles)
        ]
        return jnp.concatenate(parts, 0)

    def spread_rows(ref, values):
        for idx in range(tiles):
            part = values[idx * steps * tile : (idx + 1) * steps * tile]
            ref[:, idx * tile : (idx + 1) * tile, :] = part.reshape(steps, tile, model).astype(
                ref.dtype
            )

    rows = gather_rows(rows_ref)
    unit_one, inverse_one = norm_stats(rows)
    normed_one = (unit_one * vec_ref[0:1] + vec_ref[1:2]).astype(BF)
    normed_one_ref[...] = normed_one
    mixed[...] = dot(normed_one, w_qkv[...], 1, 0).astype(BF)
    span = steps * tile
    key_row = lax.broadcasted_iota(jnp.int32, (span, span), 0)
    query_row = lax.broadcasted_iota(jnp.int32, (span, span), 1)
    key_step, query_step = key_row // tile, query_row // tile
    key_clip, query_clip, end = jnp.zeros_like(key_row), jnp.zeros_like(key_row), 0
    for clip in range(clips):
        end = end + table_ref[CLIP_LENGTHS, clip]
        key_clip = key_clip + jnp.where(key_step >= end, 1, 0)
        query_clip = query_clip + jnp.where(query_step >= end, 1, 0)
    seen = (key_clip == query_clip) & (key_step <= query_step) & (key_row % tile == query_row % tile)
    bias = jnp.where(seen, 0.0, -1000000000.0)
    bias = jnp.concatenate([bias] * (JOINED // (model // HEADS)), 1)

    def load(idx, first):
        return mixed[idx * span : (idx + 1) * span, first : first + JOINED]

    def store(idx, first, value):
        attended_ref[idx * span : (idx + 1) * span, first : first + JOINED] = value

    def keep(idx, part, value):
        probs[idx, part] = value

    attend_forward(tiles, model, load, store, keep, bias)
    middle = rows + dot(attended_ref[...], w_proj[...], 1, 0)
    unit_two, inverse_two = norm_stats(middle)
    normed_two = (unit_two * vec_ref[2:3] + vec_ref[3:4]).astype(BF)
    normed_two_ref[...] = normed_two
    result = middle + ff_through(normed_two, b_in_ref, w_in, w_out, hidden_ref, slope)
    from_own = pl.program_id(0) < halves

    @pl.when(from_own)
    def _():
        spread_rows(active_own_ref, result)

    for idx, active_other_ref in enumerate(active_other_refs):

        @pl.when(pl.program_id(0) == halves + idx)
        def _():
            spread_rows(active_other_ref, result)

    branch = gather_rows(jnp.where(from_own, own_ref[...], other_ref[...]))
    branch_ref[...] = branch
    grad_middle = ff_back(
        branch.astype(F32),
        branch,
        unit_two,
        inverse_two,
        vec_ref[2:3],
        w_in,
        w_out,
        slope,
        grad_pre_ref,
        small_ref,
    )
    proj_in = grad_middle.astype(BF)
    proj_in_ref[...] = proj_in
    grad_att[...] = dot(proj_in, w_proj[...], 1, 1).astype(BF)

    def load_grad(idx, first):
        return grad_att[idx * span : (idx + 1) * span, first : first + JOINED]

    def load_prob(idx, part):
        return probs[idx, part]

    def store_grad(idx, first, value):
        grad_mixed_ref[idx * span : (idx + 1) * span, first : first + JOINED] = value

    attend_backward(tiles, model, load, load_grad, load_prob, store_grad, 1)
    grad_first = dot(grad_mixed_ref[...], w_qkv[...], 1, 1)
    offset = 2 * model + w_in.shape[1]
    small_ref[:, offset : offset + model] += fold_rows(grad_first * unit_one)
    small_ref[:, offset + model : offset + 2 * model] += fold_rows(grad_first)
    spread_rows(
        grad_ref, grad_middle + norm_back(grad_first * vec_ref[0:1], unit_one, inverse_one)
    )


def weight_grad_kernel(jobs, which, slabs, n_in, n_out, has_small, table_ref, *refs):
    ins, refs = refs[:n_in], refs[n_in:]
    over, fixed, moving, staged, in_sems, sem = refs[-6:]
    outs = refs[-6 - n_out : -6]
    each = slabs // n_out
    rows = staged.shape[1]
    steps, loads = [], []
    for number, (left, right, by_rows, first_col, tiles) in enumerate(jobs):
        begin = 0
        for item, size in enumerate(tiles):
            needs = []
            if item == 0:
                still = right if by_rows else left
                needs.append((still, 0, ins[still].shape[1], fixed, number % 2, 0))
            slot = len(steps) % 2
            needs.append((left if by_rows else right, begin, size, moving, slot, 1))
            loads.append(needs)
            steps.append((by_rows, number % 2, slot, begin, size, first_col))
            begin += size

    def copies(step):
        return [
            pltpu.make_async_copy(
                ins[array].at[:, pl.ds(first, size)],
                buffer.at[slot, :, pl.ds(0, size)],
                in_sems.at[kind, slot],
            )
            for array, first, size, buffer, slot, kind in loads[step]
        ]

    def send_out(first_col, cols):
        for half, out in enumerate(outs):
            pltpu.make_async_copy(
                staged.at[pl.ds(half * each, each), :, pl.ds(first_col, cols)],
                out.at[:, :, pl.ds(first_col, cols)],
                sem,
            ).start()

    for copy in copies(0):
        copy.start()
    for step, (by_rows, still, slot, begin, size, first_col) in enumerate(steps):
        if step + 1 < len(steps):
            for copy in copies(step + 1):
                copy.start()
        for copy in copies(step):
            copy.wait()
        if by_rows:
            cols = fixed.shape[2]
            value = dot(moving[slot, :, :size], fixed[still], 0, 0).astype(BF)
            fold = ins[jobs[-1][0]].shape[1] // (slabs * rows)
            for idx in range(size // (fold * rows)):
                place = table_ref[which, begin // (fold * rows) + idx]
                for part in range(fold):
                    source = (idx * fold + part) * rows
                    to_col = first_col + part * cols
                    staged[place, :, to_col : to_col + cols] = value[source : source + rows]
            if step + 1 == len(steps):
                send_out(first_col, fold * cols)
        else:
            value = dot(fixed[still], moving[slot, :, :size], 0, 0).astype(BF)
            to_col = first_col + begin
            for idx in range(slabs):
                place = table_ref[which, idx]
                staged[place, :, to_col : to_col + size] = value[idx * rows : (idx + 1) * rows]
            send_out(to_col, size)
    if has_small:
        width = staged.shape[2] - LANES
        staged[:, :, width:] = small_slabs(refs[0], refs[1:4])
        send_out(width, LANES)
    for out in outs:
        pltpu.make_async_copy(out, out, sem).wait()
    over[...] = jnp.zeros_like(over)


def small_slabs(place_ref, sums):
    tiny_0, small_0, small_1 = [jnp.sum(ref[...], 0, keepdims=True) for ref in sums]
    model = tiny_0.shape[1] // 2
    width = small_0.shape[1] - 2 * model
    far = 2 * model + width
    place = place_ref[...][:, :1]
    slabs = place.shape[0]

    def table(items):
        total = jnp.zeros((slabs, LANES), F32)
        offset = 0
        for values in items:
            length = values.shape[1]
            each = length // slabs
            lane = lax.broadcasted_iota(jnp.int32, (1, length), 1)
            mine = jnp.where(lane // each == place, values, 0.0).astype(BF)
            source = lax.broadcasted_iota(jnp.int32, (length, LANES), 0)
            target = lax.broadcasted_iota(jnp.int32, (length, LANES), 1)
            choose = jnp.where(source % each + offset == target, 1.0, 0.0).astype(BF)
            total = total + dot(mine, choose, 1, 0)
            offset += each
        return total

    norms = table(
        [
            tiny_0[:, :model],
            small_0[:, :model],
            small_1[:, far : far + model],
            small_1[:, :model],
            tiny_0[:, model:],
            small_0[:, model : 2 * model],
            small_1[:, far + model :],
            small_1[:, model : 2 * model],
        ]
    )
    biases = table([small_0[:, 2 * model :], small_1[:, 2 * model : far]])
    row = lax.broadcasted_iota(jnp.int32, (slabs, 16, LANES), 1)
    both = jnp.where(row == 0, norms[:, None, :], jnp.where(row == 1, biases[:, None, :], 0.0))
    return both.astype(BF)


def pack_kernel(copies, n_in, n_small, row_ref, *refs):
    ins, refs = refs[:n_in], refs[n_in:]
    smalls, refs = refs[:n_small], refs[n_small:]
    outs, wide = refs[:-1], refs[-1]
    for source, source_index, target, target_index in copies:
        index = tuple(item(row_ref[0]) if callable(item) else item for item in source_index)
        outs[target][target_index] = ins[source][index]
    if n_small:
        gain_ref, shift_ref, bias_ref = smalls
        wide[...] = jnp.zeros_like(wide)
        for block in range(2):
            wide[2 * block : 2 * block + 2, : gain_ref.shape[2]] = gain_ref[block].astype(F32)
            wide[4 + 2 * block : 6 + 2 * block, : gain_ref.shape[2]] = shift_ref[block].astype(F32)
        wide[8:10, : bias_ref.shape[1]] = bias_ref[...].astype(F32)
        width = outs[0].shape[1] - LANES
        outs[0][:, width:] = wide[...].astype(BF)


def unpack_kernel(place_ref, *refs):
    pieces, vec_refs, bias_refs, (held, sem) = refs[:-6], refs[-6:-4], refs[-4:-2], refs[-2:]
    first = 0
    for piece in pieces:
        count = piece.shape[0]
        width = piece.shape[2] - LANES
        pltpu.make_async_copy(
            piece.at[:, :, pl.ds(width, LANES)], held.at[pl.ds(first, count)], sem
        ).start()
        first += count
    pltpu.make_async_copy(held, held, sem).wait()
    values = held[...].astype(F32)
    place = place_ref[...][:, :1]
    slabs = place.shape[0]

    def row(idx, length):
        each = length // slabs
        lane = lax.broadcasted_iota(jnp.int32, (LANES, length), 1)
        source = lax.broadcasted_iota(jnp.int32, (LANES, length), 0)
        choose = jnp.where(lane % each == source, 1.0, 0.0).astype(BF)
        wide = dot(values[:, idx, :].astype(BF), choose, 1, 0)
        mine = lax.broadcasted_iota(jnp.int32, (1, length), 1) // each == place
        return jnp.sum(jnp.where(mine, wide, 0.0), 0, keepdims=True)

    model, width = vec_refs[0].shape[1], bias_refs[0].shape[1]
    for block in range(2):
        for norm in range(2):
            vec_refs[block][2 * norm : 2 * norm + 1] = row(2 * block + norm, model)
            vec_refs[block][2 * norm + 1 : 2 * norm + 2] = row(4 + 2 * block + norm, model)
        bias_refs[block][...] = row(8 + block, width)


def finish_kernel(*refs):
    parts = [refs[:4], refs[4:8]]
    last_ref = refs[8]
    gain_ref, shift_ref, qkv_ref, proj_ref, in_ref, b_in_ref, out_ref = refs[9:]

    def total(idx, first, cols):
        if idx == 2:
            return last_ref[:, first : first + cols].astype(F32)
        return add_up(*[ref[0, :, first : first + cols] for ref in parts[idx]])

    model, width = proj_ref.shape[2], in_ref.shape[2]
    triple, rows = 3 * model, proj_ref.shape[1]
    start = triple + model
    qkv_ref[0] = total(0, 0, triple)
    qkv_ref[1] = total(2, 0, triple)
    proj_ref[0] = total(1, 0, model)
    proj_ref[1] = total(2, triple, model)
    in_ref[0] = total(1, model, width)
    in_ref[1] = total(2, start, width)
    for idx in range(width // model):
        to_rows = slice(idx * rows, (idx + 1) * rows)
        out_ref[0, to_rows] = total(1, model + width + idx * model, model)
        out_ref[1, to_rows] = total(2, start + width + idx * model, model)
    small = total(0, triple, LANES)
    wide = gain_ref.shape[2]
    for block in range(2):
        for norm in range(2):
            first = (2 * block + norm) * wide
            gain_ref[block, norm : norm + 1] = small[0:1, first : first + wide]
            first += 4 * wide
            shift_ref[block, norm : norm + 1] = small[0:1, first : first + wide]
        cols = b_in_ref.shape[1]
        b_in_ref[block : block + 1] = small[1:2, block * cols : (block + 1) * cols]


def add_kernel(count, plans, *refs):
    outs = refs[2 * count :]
    for out, parts in zip(outs, plans):
        for pair, index, first, cols, to_col in parts:
            place = index + (slice(first, first + cols),)
            value = add_up(refs[2 * pair][place], refs[2 * pair + 1][place])
            out[..., to_col : to_col + cols] = value.astype(out.dtype)


def place_kernel(table_ref, _, come_ref, out_ref):
    out_ref[...] = come_ref[...]


ANY = pl.BlockSpec(memory_space=pl.ANY)
SMEM = pl.BlockSpec(memory_space=pltpu.SMEM)
Shape = jax.ShapeDtypeStruct


def whole(shape):
    return pl.BlockSpec(shape, lambda idx, *_: (0,) * len(shape))


def leading(shape):
    return pl.BlockSpec(shape, lambda idx, *_: (idx,) + (0,) * (len(shape) - 1))


def mine(shape, blocks):
    rest = (0,) * (len(shape) - 1)
    return pl.BlockSpec(shape, lambda idx, table: (table[HERE, 0] * blocks + idx,) + rest)


def limits(megabytes):
    return pltpu.CompilerParams(vmem_limit_bytes=megabytes * MIB)


def cost(flops, bytes_accessed):
    return pl.CostEstimate(
        flops=flops // SHRINK, bytes_accessed=bytes_accessed // SHRINK, transcendentals=0
    )


def pack(row, sources, targets, copies, smalls, name):
    vmem = pl.BlockSpec(memory_space=pltpu.VMEM)
    return pl.pallas_call(
        functools.partial(pack_kernel, copies, len(sources), len(smalls)),
        in_specs=[SMEM] + [vmem] * (len(sources) + len(smalls)),
        out_specs=[vmem] * len(targets),
        out_shape=[Shape(shape, BF) for shape in targets],
        scratch_shapes=[pltpu.VMEM((16, LANES), F32)],
        compiler_params=limits(60),
        name=name,
    )(row, *sources, *smalls)


def finish(parts, shapes):
    vmem = pl.BlockSpec(memory_space=pltpu.VMEM)
    return pl.pallas_call(
        finish_kernel,
        in_specs=[vmem] * len(parts),
        out_specs=[vmem] * 7,
        out_shape=[Shape(shape, F32) for shape in shapes],
        compiler_params=limits(60),
        name="finish",
    )(*parts)


def add_pairs(pairs, outs, name):
    vmem = pl.BlockSpec(memory_space=pltpu.VMEM)
    return pl.pallas_call(
        functools.partial(add_kernel, len(pairs), tuple(parts for _, parts in outs)),
        in_specs=[vmem] * (2 * len(pairs)),
        out_specs=[vmem] * len(outs),
        out_shape=[Shape(shape, BF) for shape, _ in outs],
        compiler_params=limits(60),
        name=name,
    )(*[item for pair in pairs for item in pair])


def put_back(table, full, come, part, axis):
    blocks = full.shape[0] // 2 // come.shape[0]

    def target(idx, table):
        place = [(1 - table[HERE, 0]) * blocks, 0, 0]
        place[axis] = place[axis] + part
        return tuple(place)

    return pl.pallas_call(
        place_kernel,
        grid_spec=pltpu.PrefetchScalarGridSpec(
            num_scalar_prefetch=1,
            grid=(1,),
            in_specs=[ANY, whole(come.shape)],
            out_specs=pl.BlockSpec(come.shape, target),
        ),
        out_shape=Shape(full.shape, BF),
        input_output_aliases={1: 0},
        compiler_params=limits(60),
        name="put_back",
    )(table, full, come)


def unpack(place, pieces, model, width):
    slabs, rows = place.shape[0], pieces[0].shape[1]
    vmem = pl.BlockSpec(memory_space=pltpu.VMEM)
    return pl.pallas_call(
        unpack_kernel,
        in_specs=[vmem] + [ANY] * len(pieces),
        out_specs=[vmem] * 4,
        out_shape=[Shape((4, model), F32)] * 2 + [Shape((1, width), F32)] * 2,
        scratch_shapes=[pltpu.VMEM((slabs, rows, LANES), BF), pltpu.SemaphoreType.DMA],
        compiler_params=limits(60),
        name="unpack",
    )(place, *pieces)


class Weight:
    def __init__(self, shape, segments):
        self.shape = shape
        self.segments = segments


def call(kernel, name, table, groups, weights, static, inputs, outputs, scratch, grid, flops, traffic, first):
    names = []
    for weight in weights:
        for segment in weight.segments:
            if segment[0] not in names:
                names.append(segment[0])
    specs = tuple(
        tuple((names.index(segment[0]),) + tuple(segment[1:]) for segment in weight.segments)
        for weight in weights
    )
    pieces = [tuple(groups[item]) for item in names] + [tuple(first)]
    counts = tuple(len(item) for item in pieces)
    pieces = [item for group in pieces for item in group]
    return pl.pallas_call(
        functools.partial(kernel, specs, counts, *static),
        grid_spec=pltpu.PrefetchScalarGridSpec(
            num_scalar_prefetch=1,
            grid=(grid,),
            in_specs=[ANY] * len(pieces) + [spec for _, spec in inputs],
            out_specs=[spec for _, spec in outputs],
            scratch_shapes=[pltpu.VMEM(weight.shape, BF) for weight in weights]
            + scratch
            + [pltpu.SemaphoreType.DMA((len(weights),))],
        ),
        out_shape=[shape for shape, _ in outputs],
        compiler_params=limits(60),
        cost_estimate=cost(flops, traffic),
        name=name,
    )(table, *pieces, *[value for value, _ in inputs])


def spatial_forward(table, groups, weights, own, other, vec, first=()):
    frames, half, model = other.shape
    patches = 2 * half
    each = min(2, frames)
    grid = frames // each
    joined = model // JOINED
    spread = patches * (JOINED * HEADS // model)

    def out(*shape, dtype=BF):
        return Shape((frames,) + shape, dtype), leading((each,) + shape)

    return call(
        spatial_forward_kernel,
        "spatial_forward",
        table,
        groups,
        weights,
        (),
        [
            (own, mine((each, half, model), grid)),
            (other, leading((each, half, model))),
            (vec, whole(vec.shape)),
        ],
        [
            out(patches, model, dtype=F32),
            out(patches, model),
            out(patches, 3 * model),
            out(patches, model),
            out(joined, patches, spread),
        ],
        [],
        grid,
        2 * frames * patches * model * (4 * model + 2 * patches),
        frames * patches * model * 24,
        first,
    )


def feed_forward(table, groups, weights, middle, vec, b_in, first=()):
    tokens, model = middle.shape
    width = b_in.shape[1]
    block = min(512, tokens)
    return call(
        feed_forward_kernel,
        "feed_forward",
        table,
        groups,
        weights,
        (),
        [
            (middle, leading((block, model))),
            (vec, whole(vec.shape)),
            (b_in, whole(b_in.shape)),
        ],
        [
            (Shape((tokens, model), F32), leading((block, model))),
            (Shape((tokens, model), BF), leading((block, model))),
            (Shape((tokens, width), BF), leading((block, width))),
            (Shape((tokens, width), BF), leading((block, width))),
        ],
        [],
        tokens // block,
        4 * tokens * model * width,
        tokens * (8 * model + 4 * width),
        first,
    )


def feed_backward(table, groups, weights, grad, middle, slope, vec, first=()):
    tokens, model = middle.shape
    width = slope.shape[1]
    block = min(512, tokens)
    small = (8, 2 * model + width)
    return call(
        feed_backward_kernel,
        "feed_backward",
        table,
        groups,
        weights,
        (),
        [
            (grad, leading((block, model))),
            (middle, leading((block, model))),
            (slope, leading((block, width))),
            (vec, whole(vec.shape)),
        ],
        [
            (Shape((tokens, model), F32), leading((block, model))),
            (Shape((tokens, model), BF), leading((block, model))),
            (Shape((tokens, model), BF), leading((block, model))),
            (Shape((tokens, width), BF), leading((block, width))),
            (Shape(small, F32), whole(small)),
        ],
        [],
        tokens // block,
        4 * tokens * model * width,
        tokens * (14 * model + 4 * width),
        first,
    )


def spatial_backward(table, groups, weights, grad, own, other, mixed, prob, vec, first=()):
    frames, half, model = other.shape
    patches = 2 * half
    each = min(2, frames)
    small = (8, 2 * model)
    blocks = frames // each
    early = (blocks + 1) // 2
    late = max(1, blocks - early)
    block = (each, half, model)
    return call(
        spatial_backward_kernel,
        "spatial_backward",
        table,
        groups,
        weights,
        (),
        [
            (grad, leading((each, patches, model))),
            (own, mine((each, half, model), frames // each)),
            (other, leading((each, half, model))),
            (mixed, leading((each, patches, 3 * model))),
            (prob, leading((each,) + prob.shape[1:])),
            (vec, whole(vec.shape)),
        ],
        [
            (Shape(own.shape, BF), mine((each, half, model), frames // each)),
            (
                Shape((early * each, half, model), BF),
                pl.BlockSpec(block, lambda idx, _: (jnp.minimum(idx, early - 1), 0, 0)),
            ),
            (
                Shape((late * each, half, model), BF),
                pl.BlockSpec(block, lambda idx, _: (jnp.maximum(idx - early, 0), 0, 0)),
            ),
            (Shape((frames, patches, 3 * model), BF), leading((each, patches, 3 * model))),
            (Shape(small, F32), whole(small)),
        ],
        [pltpu.VMEM((each * patches, model), BF)],
        frames // each,
        2 * frames * patches * model * (4 * model + 4 * patches),
        frames * patches * model * 30,
        first,
    )


def temporal_block(table, groups, weights, rows, own, other, vec, b_in, clips, first=()):
    steps, patches, model = rows.shape
    width = b_in.shape[1]
    half = other.shape[1]
    each = min(64, half)
    tile = min(16, each)
    halves = half // each
    last = halves - 1
    count = steps * each
    total = steps * patches
    small = (8, 4 * model + width)
    block = (steps, each, model)
    spread = steps * tile * (JOINED * HEADS // model)
    mine_part = pl.BlockSpec(
        block, lambda idx, table: (table[HERE, 0], jnp.minimum(idx, last), 0)
    )
    other_part = pl.BlockSpec(block, lambda idx, _: (0, jnp.maximum(idx - halves, 0), 0))
    return call(
        temporal_kernel,
        "temporal_block",
        table,
        groups,
        weights,
        (tile, clips, halves),
        [
            (rows, pl.BlockSpec(block, lambda idx, _: (0, idx, 0))),
            (own, mine_part),
            (other, other_part),
            (vec, whole(vec.shape)),
            (b_in, whole(b_in.shape)),
        ],
        [
            (Shape(own.shape, BF), mine_part),
            *[(Shape(block, BF), whole(block))] * halves,
            (Shape((steps, patches, model), F32), pl.BlockSpec(block, lambda idx, _: (0, idx, 0))),
            (Shape(small, F32), whole(small)),
            (Shape((total, model), BF), leading((count, model))),
            (Shape((total, model), BF), leading((count, model))),
            (Shape((total, model), BF), leading((count, model))),
            (Shape((total, width), BF), leading((count, width))),
            (Shape((total, model), BF), leading((count, model))),
            (Shape((total, width), BF), leading((count, width))),
            (Shape((total, model), BF), leading((count, model))),
            (Shape((total, 3 * model), BF), leading((count, 3 * model))),
        ],
        [
            pltpu.VMEM((count, 3 * model), BF),
            pltpu.VMEM((each // tile, model // JOINED, steps * tile, spread), BF),
            pltpu.VMEM((count, width), BF),
            pltpu.VMEM((count, model), BF),
        ],
        2 * halves,
        4 * total * model * (4 * model + 2 * width),
        total * (40 * model + 4 * width),
        first,
    )


def weight_grads(table, which, n_out, slabs, jobs, name, small=None, first=()):
    tile, most = 512, 1024
    tokens = jobs[0][0].shape[0]
    plans, operands = [], []
    col, flops, rows = 0, 0, 0
    for left, right, by_rows in jobs:
        length = (left if by_rows else right).shape[1]
        tiles = tuple(min(most, length - begin) for begin in range(0, length, most))
        plans.append((len(operands), len(operands) + 1, by_rows, col, tiles))
        operands += [left, right]
        if not by_rows:
            rows = left.shape[1] // slabs
        col += length
        flops += 2 * tokens * left.shape[1] * right.shape[1]
    extra = []
    if small is not None:
        place = jnp.broadcast_to(table[TO_A][:, None], (slabs, LANES))
        extra = [place, *small]
        col += LANES
    vmem = pl.BlockSpec(memory_space=pltpu.VMEM)
    return pl.pallas_call(
        functools.partial(
            weight_grad_kernel,
            tuple(plans),
            which,
            slabs,
            len(operands),
            n_out,
            int(small is not None),
        ),
        in_specs=[SMEM] + [ANY] * len(operands) + [vmem] * len(extra) + [ANY] * len(first),
        out_specs=[ANY] * n_out + [vmem],
        out_shape=[Shape((slabs // n_out, rows, col), BF)] * n_out + [Shape((8, LANES), F32)],
        scratch_shapes=[
            pltpu.VMEM((2, tokens, tile), BF),
            pltpu.VMEM((2, tokens, most), BF),
            pltpu.VMEM((slabs, rows, col), BF),
            pltpu.SemaphoreType.DMA((2, 2)),
            pltpu.SemaphoreType.DMA,
        ],
        compiler_params=limits(60),
        cost_estimate=cost(flops, flops // 512),
        name=name,
    )(table, *operands, *extra, *first)


def plain_grad(left, right):
    grad = dot(left, right, 0, 0)
    return lax.psum_scatter(grad, AXES, scatter_dimension=0, tiled=True)


class Plan:
    def __init__(self, mesh):
        self.dp = mesh.shape["dp"]
        self.seq = mesh.shape["seq"]
        self.count = self.dp * self.seq
        self.cube = self.dp == 16 and self.seq == 2

    def swap(self, value, mask):
        pairs = [(idx, idx ^ mask) for idx in range(self.count)]
        return lax.ppermute(value, AXES, pairs)

    def me(self):
        return lax.axis_index("dp") * self.seq + lax.axis_index("seq")


ROW, CORE, COLUMN, Z_LOW, Z_HIGH = 1, 2, 4, 8, 16


def gather_masks(order):
    masks = [0]
    for stage in order:
        masks = masks + [mask ^ bit for bit in stage for mask in masks]
    return masks


STAGE_Z = (Z_LOW, Z_HIGH, Z_LOW | Z_HIGH)
GATHER_A = (STAGE_Z, (COLUMN,), (ROW,), (CORE,))
GATHER_B = (STAGE_Z, (ROW,), (COLUMN,), (CORE,))
GATHER_C = ((ROW,), STAGE_Z, (COLUMN,), (CORE,))


def join(*values, axis=0):
    total = sum(value.shape[axis] for value in values)
    low = jnp.array(-jnp.inf, values[0].dtype)
    joined, first = None, 0
    for value in values:
        count = value.shape[axis]
        sides = [(0, 0, 0)] * value.ndim
        sides[axis] = (first, total - first - count, 0)
        padded = lax.pad(value, low, sides)
        joined = padded if joined is None else jnp.maximum(joined, padded)
        first += count
    return joined


SUM_A = (CORE, COLUMN, ROW, Z_HIGH, Z_LOW)


def sum_masks(order):
    masks = [0]
    for bit in reversed(order):
        masks = masks + [mask ^ bit for mask in masks]
    return masks


def inverse_masks(masks, order):
    place = jnp.zeros_like(masks)
    for idx, bit in enumerate(reversed(order)):
        place = place + jnp.where((masks & bit) != 0, 1 << idx, 0)
    return place


def add_up(*values):
    total = values[0].astype(F32)
    for value in values[1:]:
        total = total + value.astype(F32)
    return total


class Sum:
    def __init__(self, plan, keep, send, cut):
        self.plan = plan
        self.keep, self.away = keep, send
        cols = keep.shape[2]
        parts = ((0, cut, 0), (cut, cols - cut, 1))
        self.parts = [part for part in parts if part[1]]

    def send_core(self):
        return self.plan.swap(self.away, CORE)

    def add_core(self, come):
        rows, cols = self.keep.shape[1:]
        shape = (2, 2, 4, rows, cols)
        every = slice(None)
        outs = []
        for first, size, index in self.parts:
            for half in range(2):
                lead = (half, every) if index == 0 else (every, half)
                part = (0, lead + (every, every), first, size, 0)
                outs.append(((2, 4, rows, size), (part,)))
        sums = add_pairs([(self.keep.reshape(shape), come.reshape(shape))], outs, "add_core")
        self.keep, self.away = sums[::2], sums[1::2]

    def send_first(self):
        bits = [(COLUMN, ROW)[index] for _, _, index in self.parts]
        return [self.plan.swap(item, bit) for item, bit in zip(self.away, bits)]

    def add_first(self, come):
        pairs = list(zip(self.keep, come))
        every = slice(None)
        outs = []
        for pair, (keep, _) in enumerate(pairs):
            for half in range(2):
                part = (pair, (half, every, every), 0, keep.shape[3], 0)
                outs.append((keep.shape[1:], (part,)))
        sums = add_pairs(pairs, outs, "add_first")
        self.keep, self.away = sums[::2], sums[1::2]

    def send_second(self):
        bits = [(ROW, COLUMN)[index] for _, _, index in self.parts]
        return [self.plan.swap(item, bit) for item, bit in zip(self.away, bits)]

    def add_second(self, come):
        pairs = list(zip(self.keep, come))
        every = slice(None)
        rows = self.keep[0].shape[1]
        total = sum(size for _, size, _ in self.parts)
        outs = []
        for idx in range(4):
            lead = (slice(idx, idx + 1), every)
            parts = tuple(
                (pair, lead, 0, size, first) for pair, (first, size, _) in enumerate(self.parts)
            )
            outs.append(((1, rows, total), parts))
        sums = add_pairs(pairs, outs, "add_second")
        self.keep, self.away = sums[0], sums[1:]

    def send_last(self):
        one, two, both = self.away
        swap = self.plan.swap
        return [swap(one, Z_LOW), swap(two, Z_HIGH), swap(both, Z_LOW | Z_HIGH)]


def together(*values):
    return lax.optimization_barrier(values)


def to_frames(plan, values):
    full = lax.all_to_all(values, "seq", split_axis=0, concat_axis=1, tiled=True)
    half = full.shape[1] // 2
    return full[:, :half], full[:, half:]


def from_frames(plan, own, other):
    full = jnp.concatenate([own, other], 1)
    return lax.all_to_all(full, "seq", split_axis=1, concat_axis=0, tiled=True)


def regroup(plan, values, split_axis, concat_axis):
    members = plan.seq // MICRO
    if members == 1:
        return values
    row = lax.axis_index("seq")
    rank = row % members
    size = values.shape[split_axis] // members
    span = values.shape[concat_axis]
    shape = list(values.shape)
    shape[split_axis] = size
    shape[concat_axis] = span * members
    result = jnp.zeros(shape, values.dtype)
    for shift in range(members):
        target = (rank + shift) % members
        part = lax.dynamic_slice_in_dim(values, target * size, size, split_axis)
        if shift:
            pairs = [
                (idx, idx - idx % members + (idx + shift) % members) for idx in range(plan.seq)
            ]
            part = lax.ppermute(part, "seq", pairs)
        source = (rank - shift) % members
        result = lax.dynamic_update_slice_in_dim(result, part, source * span, concat_axis)
    return result


def plain_weights(plan, weights, small):
    groups, blocks = {}, []
    for idx in range(2):
        block = []
        for name, value in zip(("qkv", "proj", "in", "out"), weights):
            key = name + str(idx)
            whole_value = lax.all_gather(value[idx], AXES, axis=0, tiled=True)
            groups[key] = [whole_value[None]]
            block.append(Weight(whole_value.shape, ((key, AS_IS, 0, value.shape[2], 0, 1, 0),)))
        blocks.append(block)
    return groups, blocks, lax.all_gather(small, AXES, axis=0).astype(F32)


def cube_weights(shapes, fold):
    (model, triple), _, (_, width), _ = shapes
    start = triple + model + width
    first = [
        Weight(shapes[0], (("att0", FROM_C, 0, triple, 0, 1, 0),)),
        Weight(shapes[1], (("att0", FROM_C, triple, model, 0, 1, 0),)),
        Weight(shapes[2], (("in0", FROM_A, 0, width, 0, 1, 0),)),
        Weight(
            shapes[3],
            tuple(("out0", FROM_B, idx * model, model, idx, fold, 0) for idx in range(fold)),
        ),
    ]
    last = [
        Weight(shapes[0], (("last", AS_IS, 0, triple, 0, 1, 0),)),
        Weight(shapes[1], (("last", AS_IS, triple, model, 0, 1, 0),)),
        Weight(shapes[2], (("last", AS_IS, triple + model, width, 0, 1, 0),)),
        Weight(
            shapes[3],
            tuple(("last", AS_IS, start + idx * model, model, idx, fold, 0) for idx in range(fold)),
        ),
    ]
    return [first, last]


def cube_packs(plan, row, tokens, weights, smalls):
    w_qkv, w_proj, w_in, w_out = weights
    rows, triple = w_qkv.shape[1:]
    model, width = w_proj.shape[2], w_in.shape[2]
    fold = w_out.shape[1] // rows
    start = triple + model + width
    steps, here = tokens.shape[1:3]
    count = steps // 2

    def cols(first, size):
        return (slice(None), pl.ds(first, size))

    copies = [
        (0, (0,), 0, cols(0, triple)),
        (1, (0,), 0, cols(triple, model)),
        (4, (0, lambda me: pl.ds((1 - me) * count, count)), 3, (slice(None),)),
        (2, (0,), 1, cols(0, width)),
        (0, (1,), 2, cols(0, triple)),
        (1, (1,), 2, cols(triple, model)),
        (2, (1,), 2, cols(triple + model, width)),
    ]
    for idx in range(fold):
        part = pl.ds(idx * rows, rows)
        copies.append((3, (0, part), 1, cols(width + idx * model, model)))
        copies.append((3, (1, part), 2, cols(start + idx * model, model)))
    targets = [
        (rows, triple + model + LANES),
        (rows, width + fold * model),
        (rows, start + fold * model),
        (count, here, model),
    ]
    return pack(row, [*weights, tokens], targets, copies, smalls, "pack")


def on_device(plan, tokens, lengths, cotangent, norm_gain, norm_bias, w_qkv, w_proj, w_in, b_in, w_out):
    steps_all, here, model = tokens.shape[1:]
    steps = steps_all // MICRO
    width = b_in.shape[1] * plan.count
    row = lax.axis_index("seq")
    micro = row * MICRO // plan.seq
    own_lengths = lax.dynamic_index_in_dim(lengths[0], micro, 0, keepdims=False)
    clips = own_lengths.shape[0]

    weights = (w_qkv, w_proj, w_in, w_out)
    shapes = ((model, 3 * model), (model, model), (model, width), (width, model))
    wide = model // plan.count
    cut = 4 * wide
    slabs = plan.count
    waits = ()
    if plan.cube:
        me = plan.me()
        orders = [gather_masks(GATHER_A), gather_masks(GATHER_B), gather_masks(GATHER_C), sum_masks(SUM_A)]
        table = jnp.concatenate(
            [
                me ^ jnp.array(orders, jnp.int32),
                inverse_masks(me ^ jnp.arange(plan.count, dtype=jnp.int32), SUM_A)[None],
                jnp.arange(plan.count, dtype=jnp.int32)[None],
                jnp.broadcast_to(row, (1, plan.count)).astype(jnp.int32),
                jnp.pad(own_lengths, (0, plan.count - clips))[None],
            ]
        )
        row_index = jnp.reshape(row, (1,)).astype(jnp.int32)
        own = tokens[0]
        att, feed_0, last, away = cube_packs(
            plan, row_index, tokens, weights, (norm_gain, norm_bias, b_in)
        )
        last = lax.all_gather(last, AXES, axis=0, tiled=True)
        groups = {"last": [last.reshape(plan.count, -1, last.shape[1])]}
        att, feed_0 = att[None], feed_0[None]
        att = join(att, plan.swap(att, ROW))
        *come, feed_0, cotangent = together(
            *[plan.swap(att, bit) for bit in STAGE_Z], feed_0, cotangent
        )
        att = join(att, *come)
        ct_own = cotangent[0]
        (ct_away,) = pack(
            row_index,
            [cotangent],
            [away.shape],
            [(0, (0, lambda me: pl.ds((1 - me) * steps, steps)), 0, (slice(None),))],
            (),
            "pack_cotangent",
        )
        come, other, *feed_come, ct_away = together(
            plan.swap(att, COLUMN),
            plan.swap(away, ROW),
            *[plan.swap(feed_0, bit) for bit in STAGE_Z],
            ct_away,
        )
        ct_other = plan.swap(ct_away, ROW)
        att = join(att, come)
        parts = [feed_0] + feed_come
        part_a = join(*[item[:, :, :width] for item in parts])
        part_b = join(*[item[:, :, width:] for item in parts])
        att_come, *come = together(
            plan.swap(att, CORE), plan.swap(part_a, COLUMN), plan.swap(part_b, ROW)
        )
        groups["att0"] = [att, att_come]
        part_a, part_b = join(part_a, come[0]), join(part_b, come[1])
        moving = [plan.swap(part_a, ROW), plan.swap(part_b, COLUMN)]
        waits = (part_a, part_b)
        place = jnp.broadcast_to(table[FROM_C][:, None], (slabs, LANES))
        unpacked = unpack(place, groups["att0"], model, width)
        vecs, biases = unpacked[:2], unpacked[2:]
        blocks = cube_weights(shapes, w_out.shape[1] // w_in.shape[1])
    else:
        own, other = to_frames(plan, tokens[0])
        table = jnp.zeros((8, clips), jnp.int32).at[CLIP_LENGTHS].set(own_lengths)
        small = jnp.concatenate([norm_gain.reshape(-1), norm_bias.reshape(-1), b_in.reshape(-1)])
        groups, blocks, small_all = plain_weights(plan, weights, small)
        gains = small_all[:, :cut].reshape(plan.count, 2, 2, wide)
        shifts = small_all[:, cut : 2 * cut].reshape(plan.count, 2, 2, wide)
        gains = gains.transpose(1, 2, 0, 3).reshape(2, 2, model)
        shifts = shifts.transpose(1, 2, 0, 3).reshape(2, 2, model)
        vecs = jnp.stack([gains, shifts], 2).reshape(2, 4, model)
        biases = small_all[:, 2 * cut :]
        biases = biases.reshape(plan.count, 2, -1).transpose(1, 0, 2).reshape(2, 1, width)

    middle, normed_0, mixed, attended, prob = spatial_forward(
        table, groups, blocks[0][:2], own, other, vecs[0], waits
    )
    frames, patches = middle.shape[:2]
    count = frames * patches
    middle = middle.reshape(count, model)
    if plan.cube:
        *moving, middle = together(*moving, middle)
        part_a, part_b = join(part_a, moving[0]), join(part_b, moving[1])
        groups["in0"] = [part_a, plan.swap(part_a, CORE)]
        groups["out0"] = [part_b, plan.swap(part_b, CORE)]
    result, second_0, hidden, slope = feed_forward(
        table, groups, blocks[0][2:], middle, vecs[0], biases[0]
    )
    if plan.cube:
        ct_other, result = together(ct_other, result)
    else:
        ct_own, ct_other = to_frames(plan, cotangent[0])
    rows = regroup(plan, result.reshape(frames, patches, model), 1, 0)
    if plan.seq != 2:
        full = regroup(plan, jnp.concatenate([ct_own, ct_other], 1), 1, 0)
        cut_at = full.shape[1] // 2
        ct_own, ct_other = full[:, :cut_at], full[:, cut_at:]
    (
        active_own,
        *active_other,
        grad,
        small_1,
        normed_1,
        attended_1,
        second_1,
        hidden_1,
        branch_1,
        grad_pre_1,
        proj_in_1,
        grad_mixed_1,
    ) = temporal_block(
        table, groups, blocks[1], rows, ct_own, ct_other, vecs[1], biases[1], clips
    )
    grad = regroup(plan, grad, 0, 1).reshape(count, model)

    def flat(values):
        return values.reshape(count, values.shape[-1])

    pairs_1 = [
        (normed_1, grad_mixed_1, False),
        (attended_1, proj_in_1, False),
        (second_1, grad_pre_1, False),
        (hidden_1, branch_1, True),
    ]
    waits = ()
    if plan.cube:
        g_last, over = weight_grads(table, AS_IS, 1, slabs, pairs_1, "grads_last")
        s_last = lax.psum_scatter(
            g_last.reshape(model, -1), AXES, scatter_dimension=0, tiled=True
        )
        active_come = [plan.swap(item, ROW) for item in active_other]
        waits = (over,)

    grad_middle, proj_in_0, branch_0, grad_pre_0, small_0 = feed_backward(
        table, groups, blocks[0][2:], grad, middle, slope, vecs[0], waits
    )
    pairs_0 = [
        (flat(attended), proj_in_0, False),
        (second_0, grad_pre_0, False),
        (hidden, branch_0, True),
    ]
    waits = ()
    if plan.cube:
        active_come[0], branch_0 = together(active_come[0], branch_0)
        pairs_0[2] = (hidden, branch_0, True)
        keep, send, _ = weight_grads(table, PLACE, 2, slabs, pairs_0, "grads_feed")
        active_come[1], send = together(active_come[1], send)
        s_feed = Sum(plan, keep, send, (model + 2 * width) // 2)
        s_feed.add_core(s_feed.send_core())
        feed_come = s_feed.send_first()
        activations = put_back(table, active_own, active_come[0], 0, 1)
        activations = put_back(table, activations, active_come[1], 1, 1)
        waits = (*s_feed.keep, activations)
    grad_own, grad_early, grad_late, grad_mixed_0, tiny_0 = spatial_backward(
        table,
        groups,
        blocks[0][:2],
        grad_middle.reshape(frames, patches, model),
        own,
        other,
        mixed,
        prob,
        vecs[0],
        waits,
    )
    pairs_2 = [(flat(normed_0), flat(grad_mixed_0), False)]
    if plan.cube:
        *feed_come, grad_early = together(*feed_come, grad_early)
        s_feed.add_first(feed_come)
        tokens_come = [plan.swap(grad_early, ROW)]
        feed_come = s_feed.send_second()
        keep, send, _ = weight_grads(
            table,
            PLACE,
            2,
            slabs,
            pairs_2,
            "grads_attention",
            (tiny_0, small_0, small_1),
            s_feed.keep,
        )
        *feed_come, tokens_come[0], grad_late, send = together(
            *feed_come, *tokens_come, grad_late, send
        )
        s_att = Sum(plan, keep, send, 3 * model // 2)
        tokens_come.append(plan.swap(grad_late, ROW))
        s_att.add_core(s_att.send_core())
        att_come = s_att.send_first()
        s_feed.add_second(feed_come)
        feed_come = s_feed.send_last()
        grad_tokens = put_back(table, grad_own, tokens_come[0], 0, 0)
        *att_come, grad_tokens = together(*att_come, grad_tokens)
        s_att.add_first(att_come)
        att_come = s_att.send_second()
        *feed_come, att_come[0], att_come[1] = together(*feed_come, *att_come)
        s_att.add_second(att_come)
        *att_come, tokens_come[1], s_last = together(
            *s_att.send_last(), tokens_come[1], s_last
        )
        outs = finish(
            [
                s_att.keep,
                *att_come,
                s_feed.keep,
                *feed_come,
                s_last,
            ],
            [
                norm_gain.shape,
                norm_bias.shape,
                w_qkv.shape,
                w_proj.shape,
                w_in.shape,
                b_in.shape,
                w_out.shape,
            ],
        )
        grad_tokens = put_back(table, grad_tokens, tokens_come[1], 1, 0)
        return (activations[None], grad_tokens[None], *outs)

    active = regroup(plan, jnp.concatenate([active_own[:steps], *active_other], 1), 0, 1)
    half = active.shape[1] // 2
    activations = from_frames(plan, active[:, :half], active[:, half:])
    grad_other = jnp.concatenate([grad_early, grad_late], 0)[:frames]
    grad_tokens = from_frames(plan, grad_own, grad_other)
    each = [(pairs_2 + pairs_0), pairs_1]
    sums = [
        tuple(plain_grad(*each[block][item][:2]) for block in range(2)) for item in range(4)
    ]
    tiny_0, small_0, small_1 = [jnp.sum(item, 0) for item in (tiny_0, small_0, small_1)]
    far = 2 * model + width
    columns = [
        tiny_0[:model],
        small_0[:model],
        small_1[far : far + model],
        small_1[:model],
        tiny_0[model:],
        small_0[model : 2 * model],
        small_1[far + model :],
        small_1[model : 2 * model],
        small_0[2 * model :],
        small_1[2 * model : far],
    ]
    smalls = jnp.concatenate([item.reshape(plan.count, -1) for item in columns], 1)
    mine = lax.psum_scatter(smalls, AXES, scatter_dimension=0, tiled=True).reshape(-1)
    grad_gain = mine[:cut].reshape(2, 2, wide)
    grad_shift = mine[cut : 2 * cut].reshape(2, 2, wide)
    grad_b_in = mine[2 * cut :].reshape(2, -1)
    return (
        activations[None],
        grad_tokens[None],
        grad_gain,
        grad_shift,
        jnp.stack(sums[0]),
        jnp.stack(sums[1]),
        jnp.stack(sums[2]),
        grad_b_in,
        jnp.stack(sums[3]),
    )


def solution(mesh):
    in_specs = (
        P("dp", None, "seq", None),
        P("dp", None, None),
        P("dp", None, "seq", None),
        P(None, None, AXES),
        P(None, None, AXES),
        P(None, AXES, None),
        P(None, AXES, None),
        P(None, AXES, None),
        P(None, AXES),
        P(None, AXES, None),
    )
    out_specs = (
        P("dp", None, "seq", None),
        P("dp", None, "seq", None),
        P(None, None, AXES),
        P(None, None, AXES),
        P(None, AXES, None),
        P(None, AXES, None),
        P(None, AXES, None),
        P(None, AXES),
        P(None, AXES, None),
    )
    return jax.shard_map(
        functools.partial(on_device, Plan(mesh)),
        mesh=mesh,
        in_specs=in_specs,
        out_specs=out_specs,
        check_vma=False,
    )
```

```python
import functools

import jax
import jax.numpy as jnp
from jax import lax
from jax.experimental import pallas as pl
from jax.experimental.pallas import tpu as pltpu
from jax.sharding import PartitionSpec as P

HEADS = 8
MICRO = 2
LANES = 128
JOINED = 256
AXES = ("dp", "seq")
BF = jnp.bfloat16
F32 = jnp.float32
MIB = 1 << 20
SHRINK = 1000
FROM_A, FROM_B, FROM_C, TO_A, PLACE, AS_IS, HERE, CLIP_LENGTHS = range(8)


def dot(left, right, left_dim, right_dim):
    return lax.dot_general(
        left, right, (((left_dim,), (right_dim,)), ((), ())), preferred_element_type=F32
    )


def norm_stats(values):
    centre = values - jnp.mean(values, -1, keepdims=True)
    variance = jnp.mean(centre * centre, -1, keepdims=True)
    inverse = lax.rsqrt(variance + 1e-05)
    return centre * inverse, inverse


def norm_back(grad_scaled, unit_rows, inverse):
    mean_grad = jnp.mean(grad_scaled, -1, keepdims=True)
    mean_cross = jnp.mean(grad_scaled * unit_rows, -1, keepdims=True)
    return inverse * (grad_scaled - mean_grad - unit_rows * mean_cross)


def fold_rows(values):
    return jnp.sum(values.reshape(-1, 8, values.shape[-1]), 0)


def gelu_pair(values):
    cumulative = 0.5 * (1.0 + lax.erf(values * 0.7071067811865476))
    slope = cumulative + values * jnp.exp(-0.5 * values * values) * 0.3989422804014327
    return values * cumulative, slope


def start_weight(segments, groups, table_ref, held, sem):
    for group, which, first_col, cols, block, blocks, to_col in segments:
        slab = 0
        for piece in groups[group]:
            rows = piece.shape[1]
            for idx in range(piece.shape[0]):
                first = table_ref[which, slab] * (rows * blocks) + block * rows
                pltpu.make_async_copy(
                    piece.at[idx, :, pl.ds(first_col, cols)],
                    held.at[pl.ds(pl.multiple_of(first, rows), rows), pl.ds(to_col, cols)],
                    sem,
                ).start()
                slab += 1


def wait_weight(held, sem):
    pltpu.make_async_copy(held, held, sem).wait()


def split_refs(refs, counts):
    groups = []
    for count in counts:
        groups.append(refs[:count])
        refs = refs[count:]
    return groups, refs


def spread_heads(values, width, scale):
    lane = lax.broadcasted_iota(jnp.int32, (1, values.shape[-1]), 1)
    parts = []
    for head in range(values.shape[-1] // width):
        inside = (lane >= head * width) & (lane < (head + 1) * width)
        parts.append(values * jnp.where(inside, scale, 0.0).astype(BF))
    return jnp.concatenate(parts, 0)


def merge_heads(values, width):
    lane = lax.broadcasted_iota(jnp.int32, (1, values.shape[-1]), 1)
    count = values.shape[-1] // width
    rows = values.shape[0] // count
    merged = values[(count - 1) * rows :]
    for head in range(count - 2, -1, -1):
        merged = jnp.where(
            lane < (head + 1) * width, values[head * rows : (head + 1) * rows], merged
        )
    return merged


def attend_forward(sets, model, load, store, keep, bias):
    width = model // HEADS
    scale = width ** (-0.5)
    units = [(item, part) for item in range(sets) for part in range(model // JOINED)]

    def before(item, part):
        first = part * JOINED
        queries = spread_heads(load(item, first), width, scale)
        scores = dot(load(item, model + first), queries, 1, 1)
        return scores if bias is None else scores + bias

    scores = before(*units[0])
    for number, (item, part) in enumerate(units):
        following = before(*units[number + 1]) if number + 1 < len(units) else None
        first = part * JOINED
        exponent = jnp.exp(scores - jnp.max(scores, 0, keepdims=True))
        prob = (exponent * (1.0 / jnp.sum(exponent, 0, keepdims=True))).astype(BF)
        keep(item, part, prob)
        result = merge_heads(dot(prob, load(item, 2 * model + first), 0, 0), width)
        store(item, first, result.astype(BF))
        scores = following


def attend_backward(sets, model, load, load_grad, load_prob, store, late):
    width = model // HEADS
    scale = width ** (-0.5)
    units = [(item, part) for item in range(sets) for part in range(model // JOINED)]

    def before(item, part):
        first = part * JOINED
        spread_grad = spread_heads(load_grad(item, first), width, 1.0)
        return spread_grad, dot(load(item, 2 * model + first), spread_grad, 1, 1)

    def finish(item, part, spread_grad, grad_scores):
        first = part * JOINED
        spread_query = spread_heads(load(item, first), width, scale)
        prob = load_prob(item, part)
        store(item, 2 * model + first, dot(prob, spread_grad, 1, 0).astype(BF))
        store(item, model + first, dot(grad_scores, spread_query, 1, 0).astype(BF))
        scaled_key = load(item, model + first) * jnp.asarray(scale, BF)
        result = merge_heads(dot(grad_scores, scaled_key, 0, 0), width)
        store(item, first, result.astype(BF))

    started = before(*units[0]) if late else None
    waiting = None
    for number, (item, part) in enumerate(units):
        following = None
        if late and number + 1 < len(units):
            following = before(*units[number + 1])
        spread_grad, grad_prob = started if late else before(item, part)
        prob = load_prob(item, part).astype(F32)
        total = jnp.sum(prob * grad_prob, 0, keepdims=True)
        grad_scores = (prob * (grad_prob - total)).astype(BF)
        if late:
            if waiting is not None:
                finish(*waiting)
            waiting = (item, part, spread_grad, grad_scores)
            started = following
        else:
            finish(item, part, spread_grad, grad_scores)
    if late:
        finish(*waiting)


def spatial_forward_kernel(specs, counts, table_ref, *refs):
    groups, refs = split_refs(refs, counts)
    (
        own_ref,
        other_ref,
        vec_ref,
        middle_ref,
        normed_ref,
        qkv_ref,
        attended_ref,
        prob_ref,
        w_qkv,
        w_proj,
        sems,
    ) = refs
    frames, half, model = own_ref.shape

    @pl.when(pl.program_id(0) == 0)
    def _():
        start_weight(specs[0], groups, table_ref, w_qkv, sems.at[0])
        start_weight(specs[1], groups, table_ref, w_proj, sems.at[1])
        wait_weight(w_qkv, sems.at[0])
        wait_weight(w_proj, sems.at[1])

    rows = jnp.concatenate([own_ref[...], other_ref[...]], 1).astype(F32)
    rows = rows.reshape(frames * 2 * half, model)
    unit, _ = norm_stats(rows)
    normed = (unit * vec_ref[0:1] + vec_ref[1:2]).astype(BF)
    normed_ref[...] = normed.reshape(normed_ref.shape)
    qkv_ref[...] = dot(normed, w_qkv[...], 1, 0).astype(BF).reshape(qkv_ref.shape)

    def load(frame, first):
        return qkv_ref[frame, :, first : first + JOINED]

    def store(frame, first, value):
        attended_ref[frame, :, first : first + JOINED] = value

    def keep(frame, part, value):
        prob_ref[frame, part] = value

    attend_forward(frames, model, load, store, keep, None)
    attended = attended_ref[...].reshape(rows.shape)
    middle = rows + dot(attended, w_proj[...], 1, 0)
    middle_ref[...] = middle.reshape(middle_ref.shape)


def feed_forward_kernel(specs, counts, table_ref, *refs):
    groups, refs = split_refs(refs, counts)
    (
        middle_ref,
        vec_ref,
        b_in_ref,
        result_ref,
        normed_ref,
        hidden_ref,
        slope_ref,
        w_in,
        w_out,
        sems,
    ) = refs

    @pl.when(pl.program_id(0) == 0)
    def _():
        start_weight(specs[0], groups, table_ref, w_in, sems.at[0])
        start_weight(specs[1], groups, table_ref, w_out, sems.at[1])
        wait_weight(w_in, sems.at[0])
        wait_weight(w_out, sems.at[1])

    middle = middle_ref[...]
    unit, _ = norm_stats(middle)
    normed = (unit * vec_ref[2:3] + vec_ref[3:4]).astype(BF)
    normed_ref[...] = normed
    result_ref[...] = middle + ff_through(normed, b_in_ref, w_in, w_out, hidden_ref, slope_ref)


def ff_through(normed, b_in_ref, w_in, w_out, hidden_ref, slope_ref):
    width = w_in.shape[1]
    chunk = min(512, width)
    starts = range(0, width, chunk)

    def before(first):
        cols = slice(first, first + chunk)
        return dot(normed, w_in[:, cols], 1, 0) + b_in_ref[:, cols]

    total, waiting, pre_act = None, None, before(0)
    for first in starts:
        following = before(first + chunk) if first + chunk < width else None
        cols = slice(first, first + chunk)
        hidden, slope = gelu_pair(pre_act)
        hidden = hidden.astype(BF)
        hidden_ref[:, cols] = hidden
        slope_ref[:, cols] = slope.astype(BF)
        if waiting is not None:
            term = dot(waiting, w_out[first - chunk : first, :], 1, 0)
            total = term if total is None else total + term
        waiting, pre_act = hidden, following
    term = dot(waiting, w_out[width - chunk :, :], 1, 0)
    return term if total is None else total + term


def ff_back(grad_out, branch, unit, inverse, gain, w_in, w_out, slope_ref, grad_pre_ref, small_ref):
    model, width = w_in.shape
    chunk = min(512, width)

    def before(first):
        return dot(branch, w_out[first : first + chunk, :], 1, 1)

    grad_second, waiting, grad_hidden = None, None, before(0)
    for first in range(0, width, chunk):
        following = before(first + chunk) if first + chunk < width else None
        cols = slice(first, first + chunk)
        grad_pre = (grad_hidden * slope_ref[:, cols].astype(F32)).astype(BF)
        grad_pre_ref[:, cols] = grad_pre
        small_ref[:, 2 * model + first : 2 * model + first + chunk] += fold_rows(
            grad_pre.astype(F32)
        )
        if waiting is not None:
            term = dot(waiting, w_in[:, first - chunk : first], 1, 1)
            grad_second = term if grad_second is None else grad_second + term
        waiting, grad_hidden = grad_pre, following
    term = dot(waiting, w_in[:, width - chunk :], 1, 1)
    grad_second = term if grad_second is None else grad_second + term
    small_ref[:, :model] += fold_rows(grad_second * unit)
    small_ref[:, model : 2 * model] += fold_rows(grad_second)
    return grad_out + norm_back(grad_second * gain, unit, inverse)


def feed_backward_kernel(specs, counts, table_ref, *refs):
    groups, refs = split_refs(refs, counts)
    (
        grad_ref,
        middle_ref,
        slope_ref,
        vec_ref,
        grad_middle_ref,
        proj_in_ref,
        branch_ref,
        grad_pre_ref,
        small_ref,
        w_in,
        w_out,
        sems,
    ) = refs

    @pl.when(pl.program_id(0) == 0)
    def _():
        start_weight(specs[0], groups, table_ref, w_in, sems.at[0])
        start_weight(specs[1], groups, table_ref, w_out, sems.at[1])
        small_ref[...] = jnp.zeros_like(small_ref)
        wait_weight(w_in, sems.at[0])
        wait_weight(w_out, sems.at[1])

    unit, inverse = norm_stats(middle_ref[...])
    branch = grad_ref[...].astype(BF)
    branch_ref[...] = branch
    grad_middle = ff_back(
        grad_ref[...],
        branch,
        unit,
        inverse,
        vec_ref[2:3],
        w_in,
        w_out,
        slope_ref,
        grad_pre_ref,
        small_ref,
    )
    grad_middle_ref[...] = grad_middle
    proj_in_ref[...] = grad_middle.astype(BF)


def spatial_backward_kernel(specs, counts, table_ref, *refs):
    groups, refs = split_refs(refs, counts)
    (
        grad_ref,
        own_ref,
        other_ref,
        qkv_ref,
        prob_ref,
        vec_ref,
        grad_own_ref,
        grad_early_ref,
        grad_late_ref,
        grad_mixed_ref,
        small_ref,
        w_qkv,
        w_proj,
        grad_att,
        sems,
    ) = refs
    frames, half, model = own_ref.shape

    @pl.when(pl.program_id(0) == 0)
    def _():
        start_weight(specs[0], groups, table_ref, w_qkv, sems.at[0])
        start_weight(specs[1], groups, table_ref, w_proj, sems.at[1])
        small_ref[...] = jnp.zeros_like(small_ref)
        wait_weight(w_qkv, sems.at[0])
        wait_weight(w_proj, sems.at[1])

    rows = jnp.concatenate([own_ref[...], other_ref[...]], 1).astype(F32)
    rows = rows.reshape(frames * 2 * half, model)
    unit, inverse = norm_stats(rows)
    grad_middle = grad_ref[...].reshape(rows.shape)
    grad_att[...] = dot(grad_middle.astype(BF), w_proj[...], 1, 1).astype(BF)

    def load(frame, first):
        return qkv_ref[frame, :, first : first + JOINED]

    def load_grad(frame, first):
        return grad_att[frame * 2 * half : (frame + 1) * 2 * half, first : first + JOINED]

    def load_prob(frame, part):
        return prob_ref[frame, part]

    def store(frame, first, value):
        grad_mixed_ref[frame, :, first : first + JOINED] = value

    attend_backward(frames, model, load, load_grad, load_prob, store, 0)
    grad_mixed = grad_mixed_ref[...].reshape(rows.shape[0], 3 * model)
    grad_first = dot(grad_mixed, w_qkv[...], 1, 1)
    small_ref[:, :model] += fold_rows(grad_first * unit)
    small_ref[:, model : 2 * model] += fold_rows(grad_first)
    grad_rows = grad_middle + norm_back(grad_first * vec_ref[0:1], unit, inverse)
    grad_rows = grad_rows.astype(BF).reshape(frames, 2 * half, model)
    grad_own_ref[...] = grad_rows[:, :half]
    early = pl.program_id(0) < (pl.num_programs(0) + 1) // 2

    @pl.when(early)
    def _():
        grad_early_ref[...] = grad_rows[:, half:]

    @pl.when(jnp.logical_not(early))
    def _():
        grad_late_ref[...] = grad_rows[:, half:]


def temporal_kernel(specs, counts, tile, clips, halves, table_ref, *refs):
    groups, refs = split_refs(refs, counts)
    (
        rows_ref,
        own_ref,
        other_ref,
        vec_ref,
        b_in_ref,
        active_own_ref,
        *refs,
    ) = refs
    active_other_refs, refs = refs[:halves], refs[halves:]
    (
        grad_ref,
        small_ref,
        normed_one_ref,
        attended_ref,
        normed_two_ref,
        hidden_ref,
        branch_ref,
        grad_pre_ref,
        proj_in_ref,
        grad_mixed_ref,
        w_qkv,
        w_proj,
        w_in,
        w_out,
        mixed,
        probs,
        slope,
        grad_att,
        sems,
    ) = refs
    steps, patches, model = rows_ref.shape
    tiles = patches // tile
    held = (w_qkv, w_proj, w_in, w_out)

    @pl.when(pl.program_id(0) == 0)
    def _():
        for idx in range(4):
            start_weight(specs[idx], groups, table_ref, held[idx], sems.at[idx])
        small_ref[...] = jnp.zeros_like(small_ref)
        wait_weight(held[0], sems.at[0])

    def gather_rows(ref):
        parts = [
            ref[:, idx * tile : (idx + 1) * tile, :].reshape(steps * tile, model)
            for idx in range(tiles)
        ]
        return jnp.concatenate(parts, 0)

    def spread_rows(ref, values):
        for idx in range(tiles):
            part = values[idx * steps * tile : (idx + 1) * steps * tile]
            ref[:, idx * tile : (idx + 1) * tile, :] = part.reshape(steps, tile, model).astype(
                ref.dtype
            )

    rows = gather_rows(rows_ref)
    unit_one, inverse_one = norm_stats(rows)
    normed_one = (unit_one * vec_ref[0:1] + vec_ref[1:2]).astype(BF)
    normed_one_ref[...] = normed_one
    mixed[...] = dot(normed_one, w_qkv[...], 1, 0).astype(BF)
    span = steps * tile
    key_row = lax.broadcasted_iota(jnp.int32, (span, span), 0)
    query_row = lax.broadcasted_iota(jnp.int32, (span, span), 1)
    key_step, query_step = key_row // tile, query_row // tile
    key_clip, query_clip, end = jnp.zeros_like(key_row), jnp.zeros_like(key_row), 0
    for clip in range(clips):
        end = end + table_ref[CLIP_LENGTHS, clip]
        key_clip = key_clip + jnp.where(key_step >= end, 1, 0)
        query_clip = query_clip + jnp.where(query_step >= end, 1, 0)
    seen = (key_clip == query_clip) & (key_step <= query_step) & (key_row % tile == query_row % tile)
    bias = jnp.where(seen, 0.0, -1000000000.0)
    bias = jnp.concatenate([bias] * (JOINED // (model // HEADS)), 1)

    def load(idx, first):
        return mixed[idx * span : (idx + 1) * span, first : first + JOINED]

    def store(idx, first, value):
        attended_ref[idx * span : (idx + 1) * span, first : first + JOINED] = value

    def keep(idx, part, value):
        probs[idx, part] = value

    attend_forward(tiles, model, load, store, keep, bias)

    @pl.when(pl.program_id(0) == 0)
    def _():
        for idx in range(1, 4):
            wait_weight(held[idx], sems.at[idx])

    middle = rows + dot(attended_ref[...], w_proj[...], 1, 0)
    unit_two, inverse_two = norm_stats(middle)
    normed_two = (unit_two * vec_ref[2:3] + vec_ref[3:4]).astype(BF)
    normed_two_ref[...] = normed_two
    result = middle + ff_through(normed_two, b_in_ref, w_in, w_out, hidden_ref, slope)
    from_own = pl.program_id(0) < halves

    @pl.when(from_own)
    def _():
        spread_rows(active_own_ref, result)

    for idx, active_other_ref in enumerate(active_other_refs):

        @pl.when(pl.program_id(0) == halves + idx)
        def _():
            spread_rows(active_other_ref, result)

    branch = gather_rows(jnp.where(from_own, own_ref[...], other_ref[...]))
    branch_ref[...] = branch
    grad_middle = ff_back(
        branch.astype(F32),
        branch,
        unit_two,
        inverse_two,
        vec_ref[2:3],
        w_in,
        w_out,
        slope,
        grad_pre_ref,
        small_ref,
    )
    proj_in = grad_middle.astype(BF)
    proj_in_ref[...] = proj_in
    grad_att[...] = dot(proj_in, w_proj[...], 1, 1).astype(BF)

    def load_grad(idx, first):
        return grad_att[idx * span : (idx + 1) * span, first : first + JOINED]

    def load_prob(idx, part):
        return probs[idx, part]

    def store_grad(idx, first, value):
        grad_mixed_ref[idx * span : (idx + 1) * span, first : first + JOINED] = value

    attend_backward(tiles, model, load, load_grad, load_prob, store_grad, 1)
    grad_first = dot(grad_mixed_ref[...], w_qkv[...], 1, 1)
    offset = 2 * model + w_in.shape[1]
    small_ref[:, offset : offset + model] += fold_rows(grad_first * unit_one)
    small_ref[:, offset + model : offset + 2 * model] += fold_rows(grad_first)
    spread_rows(
        grad_ref, grad_middle + norm_back(grad_first * vec_ref[0:1], unit_one, inverse_one)
    )


def weight_grad_kernel(jobs, which, slabs, n_in, n_out, has_small, table_ref, *refs):
    ins, refs = refs[:n_in], refs[n_in:]
    over, fixed, moving, staged, in_sems, sem = refs[-6:]
    outs = refs[-6 - n_out : -6]
    each = slabs // n_out
    rows = staged.shape[1]
    steps, loads = [], []
    for number, (left, right, by_rows, first_col, tiles) in enumerate(jobs):
        begin = 0
        for item, size in enumerate(tiles):
            needs = []
            if item == 0:
                still = right if by_rows else left
                needs.append((still, 0, ins[still].shape[1], fixed, number % 2, 0))
            slot = len(steps) % 2
            needs.append((left if by_rows else right, begin, size, moving, slot, 1))
            loads.append(needs)
            steps.append((by_rows, number % 2, slot, begin, size, first_col))
            begin += size

    def copies(step):
        return [
            pltpu.make_async_copy(
                ins[array].at[:, pl.ds(first, size)],
                buffer.at[slot, :, pl.ds(0, size)],
                in_sems.at[kind, slot],
            )
            for array, first, size, buffer, slot, kind in loads[step]
        ]

    def send_out(first_col, cols):
        for half, out in enumerate(outs):
            pltpu.make_async_copy(
                staged.at[pl.ds(half * each, each), :, pl.ds(first_col, cols)],
                out.at[:, :, pl.ds(first_col, cols)],
                sem,
            ).start()

    for copy in copies(0):
        copy.start()
    for step, (by_rows, still, slot, begin, size, first_col) in enumerate(steps):
        if step + 1 < len(steps):
            for copy in copies(step + 1):
                copy.start()
        for copy in copies(step):
            copy.wait()
        if by_rows:
            cols = fixed.shape[2]
            value = dot(moving[slot, :, :size], fixed[still], 0, 0).astype(BF)
            fold = ins[jobs[-1][0]].shape[1] // (slabs * rows)
            for idx in range(size // (fold * rows)):
                place = table_ref[which, begin // (fold * rows) + idx]
                for part in range(fold):
                    source = (idx * fold + part) * rows
                    to_col = first_col + part * cols
                    staged[place, :, to_col : to_col + cols] = value[source : source + rows]
            if step + 1 == len(steps):
                send_out(first_col, fold * cols)
        else:
            value = dot(fixed[still], moving[slot, :, :size], 0, 0).astype(BF)
            to_col = first_col + begin
            for idx in range(slabs):
                place = table_ref[which, idx]
                staged[place, :, to_col : to_col + size] = value[idx * rows : (idx + 1) * rows]
            send_out(to_col, size)
    if has_small:
        width = staged.shape[2] - LANES
        staged[:, :, width:] = small_slabs(refs[0], refs[1:4])
        send_out(width, LANES)
    for out in outs:
        pltpu.make_async_copy(out, out, sem).wait()
    over[...] = jnp.zeros_like(over)


def small_slabs(place_ref, sums):
    tiny_0, small_0, small_1 = [jnp.sum(ref[...], 0, keepdims=True) for ref in sums]
    model = tiny_0.shape[1] // 2
    width = small_0.shape[1] - 2 * model
    far = 2 * model + width
    place = place_ref[...][:, :1]
    slabs = place.shape[0]

    def table(items):
        total = jnp.zeros((slabs, LANES), F32)
        offset = 0
        for values in items:
            length = values.shape[1]
            each = length // slabs
            lane = lax.broadcasted_iota(jnp.int32, (1, length), 1)
            mine = jnp.where(lane // each == place, values, 0.0).astype(BF)
            source = lax.broadcasted_iota(jnp.int32, (length, LANES), 0)
            target = lax.broadcasted_iota(jnp.int32, (length, LANES), 1)
            choose = jnp.where(source % each + offset == target, 1.0, 0.0).astype(BF)
            total = total + dot(mine, choose, 1, 0)
            offset += each
        return total

    norms = table(
        [
            tiny_0[:, :model],
            small_0[:, :model],
            small_1[:, far : far + model],
            small_1[:, :model],
            tiny_0[:, model:],
            small_0[:, model : 2 * model],
            small_1[:, far + model :],
            small_1[:, model : 2 * model],
        ]
    )
    biases = table([small_0[:, 2 * model :], small_1[:, 2 * model : far]])
    row = lax.broadcasted_iota(jnp.int32, (slabs, 16, LANES), 1)
    both = jnp.where(row == 0, norms[:, None, :], jnp.where(row == 1, biases[:, None, :], 0.0))
    return both.astype(BF)


def pack_kernel(copies, n_in, n_small, row_ref, *refs):
    ins, refs = refs[:n_in], refs[n_in:]
    smalls, refs = refs[:n_small], refs[n_small:]
    outs, wide = refs[:-1], refs[-1]
    for source, source_index, target, target_index in copies:
        index = tuple(item(row_ref[0]) if callable(item) else item for item in source_index)
        outs[target][target_index] = ins[source][index]
    if n_small:
        gain_ref, shift_ref, bias_ref = smalls
        wide[...] = jnp.zeros_like(wide)
        for block in range(2):
            wide[2 * block : 2 * block + 2, : gain_ref.shape[2]] = gain_ref[block].astype(F32)
            wide[4 + 2 * block : 6 + 2 * block, : gain_ref.shape[2]] = shift_ref[block].astype(F32)
        wide[8:10, : bias_ref.shape[1]] = bias_ref[...].astype(F32)
        width = outs[0].shape[1] - LANES
        outs[0][:, width:] = wide[...].astype(BF)


def unpack_kernel(place_ref, *refs):
    pieces, vec_refs, bias_refs, (held, sem) = refs[:-6], refs[-6:-4], refs[-4:-2], refs[-2:]
    first = 0
    for piece in pieces:
        count = piece.shape[0]
        width = piece.shape[2] - LANES
        pltpu.make_async_copy(
            piece.at[:, :, pl.ds(width, LANES)], held.at[pl.ds(first, count)], sem
        ).start()
        first += count
    pltpu.make_async_copy(held, held, sem).wait()
    values = held[...].astype(F32)
    place = place_ref[...][:, :1]
    slabs = place.shape[0]

    def row(idx, length):
        each = length // slabs
        lane = lax.broadcasted_iota(jnp.int32, (LANES, length), 1)
        source = lax.broadcasted_iota(jnp.int32, (LANES, length), 0)
        choose = jnp.where(lane % each == source, 1.0, 0.0).astype(BF)
        wide = dot(values[:, idx, :].astype(BF), choose, 1, 0)
        mine = lax.broadcasted_iota(jnp.int32, (1, length), 1) // each == place
        return jnp.sum(jnp.where(mine, wide, 0.0), 0, keepdims=True)

    model, width = vec_refs[0].shape[1], bias_refs[0].shape[1]
    for block in range(2):
        for norm in range(2):
            vec_refs[block][2 * norm : 2 * norm + 1] = row(2 * block + norm, model)
            vec_refs[block][2 * norm + 1 : 2 * norm + 2] = row(4 + 2 * block + norm, model)
        bias_refs[block][...] = row(8 + block, width)


def finish_kernel(*refs):
    parts = [refs[:4], refs[4:8]]
    last_ref = refs[8]
    gain_ref, shift_ref, qkv_ref, proj_ref, in_ref, b_in_ref, out_ref = refs[9:]

    def total(idx, first, cols):
        if idx == 2:
            return last_ref[:, first : first + cols].astype(F32)
        return add_up(*[ref[0, :, first : first + cols] for ref in parts[idx]])

    model, width = proj_ref.shape[2], in_ref.shape[2]
    triple, rows = 3 * model, proj_ref.shape[1]
    start = triple + model
    qkv_ref[0] = total(0, 0, triple)
    qkv_ref[1] = total(2, 0, triple)
    proj_ref[0] = total(1, 0, model)
    proj_ref[1] = total(2, triple, model)
    in_ref[0] = total(1, model, width)
    in_ref[1] = total(2, start, width)
    for idx in range(width // model):
        to_rows = slice(idx * rows, (idx + 1) * rows)
        out_ref[0, to_rows] = total(1, model + width + idx * model, model)
        out_ref[1, to_rows] = total(2, start + width + idx * model, model)
    small = total(0, triple, LANES)
    wide = gain_ref.shape[2]
    for block in range(2):
        for norm in range(2):
            first = (2 * block + norm) * wide
            gain_ref[block, norm : norm + 1] = small[0:1, first : first + wide]
            first += 4 * wide
            shift_ref[block, norm : norm + 1] = small[0:1, first : first + wide]
        cols = b_in_ref.shape[1]
        b_in_ref[block : block + 1] = small[1:2, block * cols : (block + 1) * cols]


def add_kernel(count, plans, *refs):
    outs = refs[2 * count :]
    for out, parts in zip(outs, plans):
        for pair, index, first, cols, to_col in parts:
            place = index + (slice(first, first + cols),)
            value = add_up(refs[2 * pair][place], refs[2 * pair + 1][place])
            out[..., to_col : to_col + cols] = value.astype(out.dtype)


def place_kernel(axis, table_ref, _, *refs):
    first = 0
    for come_ref in refs[:-1]:
        size = come_ref.shape[axis]
        place = [slice(None)] * 3
        place[axis] = slice(first, first + size)
        refs[-1][tuple(place)] = come_ref[...]
        first += size


ANY = pl.BlockSpec(memory_space=pl.ANY)
SMEM = pl.BlockSpec(memory_space=pltpu.SMEM)
Shape = jax.ShapeDtypeStruct


def whole(shape):
    return pl.BlockSpec(shape, lambda idx, *_: (0,) * len(shape))


def leading(shape):
    return pl.BlockSpec(shape, lambda idx, *_: (idx,) + (0,) * (len(shape) - 1))


def mine(shape, blocks):
    rest = (0,) * (len(shape) - 1)
    return pl.BlockSpec(shape, lambda idx, table: (table[HERE, 0] * blocks + idx,) + rest)


def limits(megabytes):
    return pltpu.CompilerParams(vmem_limit_bytes=megabytes * MIB)


def cost(flops, bytes_accessed):
    return pl.CostEstimate(
        flops=flops // SHRINK, bytes_accessed=bytes_accessed // SHRINK, transcendentals=0
    )


def pack(row, sources, targets, copies, smalls, name):
    vmem = pl.BlockSpec(memory_space=pltpu.VMEM)
    return pl.pallas_call(
        functools.partial(pack_kernel, copies, len(sources), len(smalls)),
        in_specs=[SMEM] + [vmem] * (len(sources) + len(smalls)),
        out_specs=[vmem] * len(targets),
        out_shape=[Shape(shape, BF) for shape in targets],
        scratch_shapes=[pltpu.VMEM((16, LANES), F32)],
        compiler_params=limits(60),
        name=name,
    )(row, *sources, *smalls)


def finish(parts, shapes):
    vmem = pl.BlockSpec(memory_space=pltpu.VMEM)
    return pl.pallas_call(
        finish_kernel,
        in_specs=[vmem] * len(parts),
        out_specs=[vmem] * 7,
        out_shape=[Shape(shape, F32) for shape in shapes],
        compiler_params=limits(60),
        name="finish",
    )(*parts)


def add_pairs(pairs, outs, name):
    vmem = pl.BlockSpec(memory_space=pltpu.VMEM)
    return pl.pallas_call(
        functools.partial(add_kernel, len(pairs), tuple(parts for _, parts in outs)),
        in_specs=[vmem] * (2 * len(pairs)),
        out_specs=[vmem] * len(outs),
        out_shape=[Shape(shape, BF) for shape, _ in outs],
        compiler_params=limits(60),
        name=name,
    )(*[item for pair in pairs for item in pair])


def put_back(table, full, come, axis):
    half = (full.shape[0] // 2,) + full.shape[1:]
    return pl.pallas_call(
        functools.partial(place_kernel, axis),
        grid_spec=pltpu.PrefetchScalarGridSpec(
            num_scalar_prefetch=1,
            grid=(1,),
            in_specs=[ANY] + [whole(item.shape) for item in come],
            out_specs=pl.BlockSpec(half, lambda idx, table: (1 - table[HERE, 0], 0, 0)),
        ),
        out_shape=Shape(full.shape, BF),
        input_output_aliases={1: 0},
        compiler_params=limits(60),
        name="put_back",
    )(table, full, *come)


def unpack(place, pieces, model, width):
    slabs, rows = place.shape[0], pieces[0].shape[1]
    vmem = pl.BlockSpec(memory_space=pltpu.VMEM)
    return pl.pallas_call(
        unpack_kernel,
        in_specs=[vmem] + [ANY] * len(pieces),
        out_specs=[vmem] * 4,
        out_shape=[Shape((4, model), F32)] * 2 + [Shape((1, width), F32)] * 2,
        scratch_shapes=[pltpu.VMEM((slabs, rows, LANES), BF), pltpu.SemaphoreType.DMA],
        compiler_params=limits(60),
        name="unpack",
    )(place, *pieces)


class Weight:
    def __init__(self, shape, segments):
        self.shape = shape
        self.segments = segments


def call(kernel, name, table, groups, weights, static, inputs, outputs, scratch, grid, flops, traffic, first):
    names = []
    for weight in weights:
        for segment in weight.segments:
            if segment[0] not in names:
                names.append(segment[0])
    specs = tuple(
        tuple((names.index(segment[0]),) + tuple(segment[1:]) for segment in weight.segments)
        for weight in weights
    )
    pieces = [tuple(groups[item]) for item in names] + [tuple(first)]
    counts = tuple(len(item) for item in pieces)
    pieces = [item for group in pieces for item in group]
    return pl.pallas_call(
        functools.partial(kernel, specs, counts, *static),
        grid_spec=pltpu.PrefetchScalarGridSpec(
            num_scalar_prefetch=1,
            grid=(grid,),
            in_specs=[ANY] * len(pieces) + [spec for _, spec in inputs],
            out_specs=[spec for _, spec in outputs],
            scratch_shapes=[pltpu.VMEM(weight.shape, BF) for weight in weights]
            + scratch
            + [pltpu.SemaphoreType.DMA((len(weights),))],
        ),
        out_shape=[shape for shape, _ in outputs],
        compiler_params=limits(60),
        cost_estimate=cost(flops, traffic),
        name=name,
    )(table, *pieces, *[value for value, _ in inputs])


def spatial_forward(table, groups, weights, own, other, vec, first=()):
    frames, half, model = other.shape
    patches = 2 * half
    each = min(2, frames)
    grid = frames // each
    joined = model // JOINED
    spread = patches * (JOINED * HEADS // model)

    def out(*shape, dtype=BF):
        return Shape((frames,) + shape, dtype), leading((each,) + shape)

    return call(
        spatial_forward_kernel,
        "spatial_forward",
        table,
        groups,
        weights,
        (),
        [
            (own, mine((each, half, model), grid)),
            (other, leading((each, half, model))),
            (vec, whole(vec.shape)),
        ],
        [
            out(patches, model, dtype=F32),
            out(patches, model),
            out(patches, 3 * model),
            out(patches, model),
            out(joined, patches, spread),
        ],
        [],
        grid,
        2 * frames * patches * model * (4 * model + 2 * patches),
        frames * patches * model * 24,
        first,
    )


def feed_forward(table, groups, weights, middle, vec, b_in, first=()):
    tokens, model = middle.shape
    width = b_in.shape[1]
    block = min(512, tokens)
    return call(
        feed_forward_kernel,
        "feed_forward",
        table,
        groups,
        weights,
        (),
        [
            (middle, leading((block, model))),
            (vec, whole(vec.shape)),
            (b_in, whole(b_in.shape)),
        ],
        [
            (Shape((tokens, model), F32), leading((block, model))),
            (Shape((tokens, model), BF), leading((block, model))),
            (Shape((tokens, width), BF), leading((block, width))),
            (Shape((tokens, width), BF), leading((block, width))),
        ],
        [],
        tokens // block,
        4 * tokens * model * width,
        tokens * (8 * model + 4 * width),
        first,
    )


def feed_backward(table, groups, weights, grad, middle, slope, vec, first=()):
    tokens, model = middle.shape
    width = slope.shape[1]
    block = min(512, tokens)
    small = (8, 2 * model + width)
    return call(
        feed_backward_kernel,
        "feed_backward",
        table,
        groups,
        weights,
        (),
        [
            (grad, leading((block, model))),
            (middle, leading((block, model))),
            (slope, leading((block, width))),
            (vec, whole(vec.shape)),
        ],
        [
            (Shape((tokens, model), F32), leading((block, model))),
            (Shape((tokens, model), BF), leading((block, model))),
            (Shape((tokens, model), BF), leading((block, model))),
            (Shape((tokens, width), BF), leading((block, width))),
            (Shape(small, F32), whole(small)),
        ],
        [],
        tokens // block,
        4 * tokens * model * width,
        tokens * (14 * model + 4 * width),
        first,
    )


def spatial_backward(table, groups, weights, grad, own, other, mixed, prob, vec, first=()):
    frames, half, model = other.shape
    patches = 2 * half
    each = min(2, frames)
    small = (8, 2 * model)
    blocks = frames // each
    early = (blocks + 1) // 2
    late = max(1, blocks - early)
    block = (each, half, model)
    return call(
        spatial_backward_kernel,
        "spatial_backward",
        table,
        groups,
        weights,
        (),
        [
            (grad, leading((each, patches, model))),
            (own, mine((each, half, model), frames // each)),
            (other, leading((each, half, model))),
            (mixed, leading((each, patches, 3 * model))),
            (prob, leading((each,) + prob.shape[1:])),
            (vec, whole(vec.shape)),
        ],
        [
            (Shape(own.shape, BF), mine((each, half, model), frames // each)),
            (
                Shape((early * each, half, model), BF),
                pl.BlockSpec(block, lambda idx, _: (jnp.minimum(idx, early - 1), 0, 0)),
            ),
            (
                Shape((late * each, half, model), BF),
                pl.BlockSpec(block, lambda idx, _: (jnp.maximum(idx - early, 0), 0, 0)),
            ),
            (Shape((frames, patches, 3 * model), BF), leading((each, patches, 3 * model))),
            (Shape(small, F32), whole(small)),
        ],
        [pltpu.VMEM((each * patches, model), BF)],
        frames // each,
        2 * frames * patches * model * (4 * model + 4 * patches),
        frames * patches * model * 30,
        first,
    )


def temporal_block(table, groups, weights, rows, own, other, vec, b_in, clips, first=()):
    steps, patches, model = rows.shape
    width = b_in.shape[1]
    half = other.shape[1]
    each = min(64, half)
    tile = min(16, each)
    halves = half // each
    last = halves - 1
    count = steps * each
    total = steps * patches
    small = (8, 4 * model + width)
    block = (steps, each, model)
    spread = steps * tile * (JOINED * HEADS // model)
    mine_part = pl.BlockSpec(
        block, lambda idx, table: (table[HERE, 0], jnp.minimum(idx, last), 0)
    )
    other_part = pl.BlockSpec(block, lambda idx, _: (0, jnp.maximum(idx - halves, 0), 0))
    return call(
        temporal_kernel,
        "temporal_block",
        table,
        groups,
        weights,
        (tile, clips, halves),
        [
            (rows, pl.BlockSpec(block, lambda idx, _: (0, idx, 0))),
            (own, mine_part),
            (other, other_part),
            (vec, whole(vec.shape)),
            (b_in, whole(b_in.shape)),
        ],
        [
            (Shape(own.shape, BF), mine_part),
            *[(Shape(block, BF), whole(block))] * halves,
            (Shape((steps, patches, model), F32), pl.BlockSpec(block, lambda idx, _: (0, idx, 0))),
            (Shape(small, F32), whole(small)),
            (Shape((total, model), BF), leading((count, model))),
            (Shape((total, model), BF), leading((count, model))),
            (Shape((total, model), BF), leading((count, model))),
            (Shape((total, width), BF), leading((count, width))),
            (Shape((total, model), BF), leading((count, model))),
            (Shape((total, width), BF), leading((count, width))),
            (Shape((total, model), BF), leading((count, model))),
            (Shape((total, 3 * model), BF), leading((count, 3 * model))),
        ],
        [
            pltpu.VMEM((count, 3 * model), BF),
            pltpu.VMEM((each // tile, model // JOINED, steps * tile, spread), BF),
            pltpu.VMEM((count, width), BF),
            pltpu.VMEM((count, model), BF),
        ],
        2 * halves,
        4 * total * model * (4 * model + 2 * width),
        total * (40 * model + 4 * width),
        first,
    )


def weight_grads(table, which, n_out, slabs, jobs, name, small=None, first=()):
    tile, most = 512, 1024
    tokens = jobs[0][0].shape[0]
    plans, operands = [], []
    col, flops, rows = 0, 0, 0
    for left, right, by_rows in jobs:
        length = (left if by_rows else right).shape[1]
        tiles = tuple(min(most, length - begin) for begin in range(0, length, most))
        plans.append((len(operands), len(operands) + 1, by_rows, col, tiles))
        operands += [left, right]
        if not by_rows:
            rows = left.shape[1] // slabs
        col += length
        flops += 2 * tokens * left.shape[1] * right.shape[1]
    extra = []
    if small is not None:
        place = jnp.broadcast_to(table[TO_A][:, None], (slabs, LANES))
        extra = [place, *small]
        col += LANES
    vmem = pl.BlockSpec(memory_space=pltpu.VMEM)
    return pl.pallas_call(
        functools.partial(
            weight_grad_kernel,
            tuple(plans),
            which,
            slabs,
            len(operands),
            n_out,
            int(small is not None),
        ),
        in_specs=[SMEM] + [ANY] * len(operands) + [vmem] * len(extra) + [ANY] * len(first),
        out_specs=[ANY] * n_out + [vmem],
        out_shape=[Shape((slabs // n_out, rows, col), BF)] * n_out + [Shape((8, LANES), F32)],
        scratch_shapes=[
            pltpu.VMEM((2, tokens, tile), BF),
            pltpu.VMEM((2, tokens, most), BF),
            pltpu.VMEM((slabs, rows, col), BF),
            pltpu.SemaphoreType.DMA((2, 2)),
            pltpu.SemaphoreType.DMA,
        ],
        compiler_params=limits(60),
        cost_estimate=cost(flops, flops // 512),
        name=name,
    )(table, *operands, *extra, *first)


def plain_grad(left, right):
    grad = dot(left, right, 0, 0)
    return lax.psum_scatter(grad, AXES, scatter_dimension=0, tiled=True)


class Plan:
    def __init__(self, mesh):
        self.dp = mesh.shape["dp"]
        self.seq = mesh.shape["seq"]
        self.count = self.dp * self.seq
        self.cube = self.dp == 16 and self.seq == 2

    def swap(self, value, mask):
        pairs = [(idx, idx ^ mask) for idx in range(self.count)]
        return lax.ppermute(value, AXES, pairs)

    def me(self):
        return lax.axis_index("dp") * self.seq + lax.axis_index("seq")


ROW, CORE, COLUMN, Z_LOW, Z_HIGH = 1, 2, 4, 8, 16


def gather_masks(order):
    masks = [0]
    for stage in order:
        masks = masks + [mask ^ bit for bit in stage for mask in masks]
    return masks


STAGE_Z = (Z_LOW, Z_HIGH, Z_LOW | Z_HIGH)
GATHER_A = (STAGE_Z, (COLUMN,), (ROW,), (CORE,))
GATHER_B = (STAGE_Z, (ROW,), (COLUMN,), (CORE,))
GATHER_C = ((ROW,), STAGE_Z, (COLUMN,), (CORE,))


def join(*values, axis=0):
    total = sum(value.shape[axis] for value in values)
    low = jnp.array(-jnp.inf, values[0].dtype)
    joined, first = None, 0
    for value in values:
        count = value.shape[axis]
        sides = [(0, 0, 0)] * value.ndim
        sides[axis] = (first, total - first - count, 0)
        padded = lax.pad(value, low, sides)
        joined = padded if joined is None else jnp.maximum(joined, padded)
        first += count
    return joined


SUM_A = (CORE, COLUMN, ROW, Z_HIGH, Z_LOW)


def sum_masks(order):
    masks = [0]
    for bit in reversed(order):
        masks = masks + [mask ^ bit for mask in masks]
    return masks


def inverse_masks(masks, order):
    place = jnp.zeros_like(masks)
    for idx, bit in enumerate(reversed(order)):
        place = place + jnp.where((masks & bit) != 0, 1 << idx, 0)
    return place


def add_up(*values):
    total = values[0].astype(F32)
    for value in values[1:]:
        total = total + value.astype(F32)
    return total


class Sum:
    def __init__(self, plan, keep, send, cut):
        self.plan = plan
        self.keep, self.away = keep, send
        cols = keep.shape[2]
        parts = ((0, cut, 0), (cut, cols - cut, 1))
        self.parts = [part for part in parts if part[1]]

    def send_core(self):
        return self.plan.swap(self.away, CORE)

    def add_core(self, come):
        rows, cols = self.keep.shape[1:]
        shape = (2, 2, 4, rows, cols)
        every = slice(None)
        outs = []
        for first, size, index in self.parts:
            for half in range(2):
                lead = (half, every) if index == 0 else (every, half)
                part = (0, lead + (every, every), first, size, 0)
                outs.append(((2, 4, rows, size), (part,)))
        sums = add_pairs([(self.keep.reshape(shape), come.reshape(shape))], outs, "add_core")
        self.keep, self.away = list(sums[::2]), list(sums[1::2])

    def send_first(self):
        bits = [(COLUMN, ROW)[index] for _, _, index in self.parts]
        return [self.plan.swap(item, bit) for item, bit in zip(self.away, bits)]

    def add_first(self, come):
        pairs = list(zip(self.keep, come))
        every = slice(None)
        outs = []
        for pair, (keep, _) in enumerate(pairs):
            for half in range(2):
                part = (pair, (half, every, every), 0, keep.shape[3], 0)
                outs.append((keep.shape[1:], (part,)))
        sums = add_pairs(pairs, outs, "add_first")
        self.keep, self.away = list(sums[::2]), list(sums[1::2])

    def send_second(self):
        bits = [(ROW, COLUMN)[index] for _, _, index in self.parts]
        return [self.plan.swap(item, bit) for item, bit in zip(self.away, bits)]

    def add_second(self, come):
        pairs = list(zip(self.keep, come))
        every = slice(None)
        rows = self.keep[0].shape[1]
        total = sum(size for _, size, _ in self.parts)
        outs = []
        for idx in range(4):
            lead = (slice(idx, idx + 1), every)
            parts = tuple(
                (pair, lead, 0, size, first) for pair, (first, size, _) in enumerate(self.parts)
            )
            outs.append(((1, rows, total), parts))
        sums = add_pairs(pairs, outs, "add_second")
        self.keep, self.away = sums[0], sums[1:]

    def send_last(self):
        one, two, both = self.away
        swap = self.plan.swap
        return [swap(one, Z_LOW), swap(two, Z_HIGH), swap(both, Z_LOW | Z_HIGH)]


def together(*values):
    return lax.optimization_barrier(values)


def to_frames(plan, values):
    full = lax.all_to_all(values, "seq", split_axis=0, concat_axis=1, tiled=True)
    half = full.shape[1] // 2
    return full[:, :half], full[:, half:]


def from_frames(plan, own, other):
    full = jnp.concatenate([own, other], 1)
    return lax.all_to_all(full, "seq", split_axis=1, concat_axis=0, tiled=True)


def regroup(plan, values, split_axis, concat_axis):
    members = plan.seq // MICRO
    if members == 1:
        return values
    row = lax.axis_index("seq")
    rank = row % members
    size = values.shape[split_axis] // members
    span = values.shape[concat_axis]
    shape = list(values.shape)
    shape[split_axis] = size
    shape[concat_axis] = span * members
    result = jnp.zeros(shape, values.dtype)
    for shift in range(members):
        target = (rank + shift) % members
        part = lax.dynamic_slice_in_dim(values, target * size, size, split_axis)
        if shift:
            pairs = [
                (idx, idx - idx % members + (idx + shift) % members) for idx in range(plan.seq)
            ]
            part = lax.ppermute(part, "seq", pairs)
        source = (rank - shift) % members
        result = lax.dynamic_update_slice_in_dim(result, part, source * span, concat_axis)
    return result


def plain_weights(plan, weights, small):
    groups, blocks = {}, []
    for idx in range(2):
        block = []
        for name, value in zip(("qkv", "proj", "in", "out"), weights):
            key = name + str(idx)
            whole_value = lax.all_gather(value[idx], AXES, axis=0, tiled=True)
            groups[key] = [whole_value[None]]
            block.append(Weight(whole_value.shape, ((key, AS_IS, 0, value.shape[2], 0, 1, 0),)))
        blocks.append(block)
    return groups, blocks, lax.all_gather(small, AXES, axis=0).astype(F32)


def cube_weights(shapes, fold):
    (model, triple), _, (_, width), _ = shapes
    start = triple + model + width
    first = [
        Weight(shapes[0], (("att0", FROM_C, 0, triple, 0, 1, 0),)),
        Weight(shapes[1], (("att0", FROM_C, triple, model, 0, 1, 0),)),
        Weight(shapes[2], (("in0", FROM_A, 0, width, 0, 1, 0),)),
        Weight(
            shapes[3],
            tuple(("out0", FROM_B, idx * model, model, idx, fold, 0) for idx in range(fold)),
        ),
    ]
    last = [
        Weight(shapes[0], (("last", AS_IS, 0, triple, 0, 1, 0),)),
        Weight(shapes[1], (("last", AS_IS, triple, model, 0, 1, 0),)),
        Weight(shapes[2], (("last", AS_IS, triple + model, width, 0, 1, 0),)),
        Weight(
            shapes[3],
            tuple(("last", AS_IS, start + idx * model, model, idx, fold, 0) for idx in range(fold)),
        ),
    ]
    return [first, last]


def cube_packs(plan, row, tokens, weights, smalls):
    w_qkv, w_proj, w_in, w_out = weights
    rows, triple = w_qkv.shape[1:]
    model, width = w_proj.shape[2], w_in.shape[2]
    fold = w_out.shape[1] // rows
    start = triple + model + width
    steps, here = tokens.shape[1:3]
    count = steps // 2

    def cols(first, size):
        return (slice(None), pl.ds(first, size))

    copies = [
        (0, (0,), 0, cols(0, triple)),
        (1, (0,), 0, cols(triple, model)),
        (4, (0, lambda me: pl.ds((1 - me) * count, count)), 3, (slice(None),)),
        (2, (0,), 1, cols(0, width)),
        (0, (1,), 2, cols(0, triple)),
        (1, (1,), 2, cols(triple, model)),
        (2, (1,), 2, cols(triple + model, width)),
    ]
    for idx in range(fold):
        part = pl.ds(idx * rows, rows)
        copies.append((3, (0, part), 1, cols(width + idx * model, model)))
        copies.append((3, (1, part), 2, cols(start + idx * model, model)))
    targets = [
        (rows, triple + model + LANES),
        (rows, width + fold * model),
        (rows, start + fold * model),
        (count, here, model),
    ]
    return pack(row, [*weights, tokens], targets, copies, smalls, "pack")


def on_device(plan, tokens, lengths, cotangent, norm_gain, norm_bias, w_qkv, w_proj, w_in, b_in, w_out):
    steps_all, here, model = tokens.shape[1:]
    steps = steps_all // MICRO
    width = b_in.shape[1] * plan.count
    row = lax.axis_index("seq")
    micro = row * MICRO // plan.seq
    own_lengths = lax.dynamic_index_in_dim(lengths[0], micro, 0, keepdims=False)
    clips = own_lengths.shape[0]

    weights = (w_qkv, w_proj, w_in, w_out)
    shapes = ((model, 3 * model), (model, model), (model, width), (width, model))
    wide = model // plan.count
    cut = 4 * wide
    slabs = plan.count
    waits = ()
    if plan.cube:
        me = plan.me()
        orders = [gather_masks(GATHER_A), gather_masks(GATHER_B), gather_masks(GATHER_C), sum_masks(SUM_A)]
        table = jnp.concatenate(
            [
                me ^ jnp.array(orders, jnp.int32),
                inverse_masks(me ^ jnp.arange(plan.count, dtype=jnp.int32), SUM_A)[None],
                jnp.arange(plan.count, dtype=jnp.int32)[None],
                jnp.broadcast_to(row, (1, plan.count)).astype(jnp.int32),
                jnp.pad(own_lengths, (0, plan.count - clips))[None],
            ]
        )
        row_index = jnp.reshape(row, (1,)).astype(jnp.int32)
        own = tokens[0]
        att, feed_0, last, away = cube_packs(
            plan, row_index, tokens, weights, (norm_gain, norm_bias, b_in)
        )
        last = lax.all_gather(last, AXES, axis=0, tiled=True)
        groups = {"last": [last.reshape(plan.count, -1, last.shape[1])]}
        att, feed_0 = att[None], feed_0[None]
        att = join(att, plan.swap(att, ROW))
        *come, feed_0, cotangent = together(
            *[plan.swap(att, bit) for bit in STAGE_Z], feed_0, cotangent
        )
        att = join(att, *come)
        ct_own = cotangent[0]
        (ct_away,) = pack(
            row_index,
            [cotangent],
            [away.shape],
            [(0, (0, lambda me: pl.ds((1 - me) * steps, steps)), 0, (slice(None),))],
            (),
            "pack_cotangent",
        )
        come, other, *feed_come, ct_away = together(
            plan.swap(att, COLUMN),
            plan.swap(away, ROW),
            *[plan.swap(feed_0, bit) for bit in STAGE_Z],
            ct_away,
        )
        ct_other = plan.swap(ct_away, ROW)
        att = join(att, come)
        parts = [feed_0] + feed_come
        part_a = join(*[item[:, :, :width] for item in parts])
        part_b = join(*[item[:, :, width:] for item in parts])
        att_come, *come = together(
            plan.swap(att, CORE), plan.swap(part_a, COLUMN), plan.swap(part_b, ROW)
        )
        groups["att0"] = [att, att_come]
        part_a, part_b = join(part_a, come[0]), join(part_b, come[1])
        moving = [plan.swap(part_a, ROW), plan.swap(part_b, COLUMN)]
        waits = (part_a, part_b)
        place = jnp.broadcast_to(table[FROM_C][:, None], (slabs, LANES))
        unpacked = unpack(place, groups["att0"], model, width)
        vecs, biases = unpacked[:2], unpacked[2:]
        blocks = cube_weights(shapes, w_out.shape[1] // w_in.shape[1])
    else:
        own, other = to_frames(plan, tokens[0])
        table = jnp.zeros((8, clips), jnp.int32).at[CLIP_LENGTHS].set(own_lengths)
        small = jnp.concatenate([norm_gain.reshape(-1), norm_bias.reshape(-1), b_in.reshape(-1)])
        groups, blocks, small_all = plain_weights(plan, weights, small)
        gains = small_all[:, :cut].reshape(plan.count, 2, 2, wide)
        shifts = small_all[:, cut : 2 * cut].reshape(plan.count, 2, 2, wide)
        gains = gains.transpose(1, 2, 0, 3).reshape(2, 2, model)
        shifts = shifts.transpose(1, 2, 0, 3).reshape(2, 2, model)
        vecs = jnp.stack([gains, shifts], 2).reshape(2, 4, model)
        biases = small_all[:, 2 * cut :]
        biases = biases.reshape(plan.count, 2, -1).transpose(1, 0, 2).reshape(2, 1, width)

    middle, normed_0, mixed, attended, prob = spatial_forward(
        table, groups, blocks[0][:2], own, other, vecs[0], waits
    )
    frames, patches = middle.shape[:2]
    count = frames * patches
    middle = middle.reshape(count, model)
    if plan.cube:
        *moving, middle = together(*moving, middle)
        part_a, part_b = join(part_a, moving[0]), join(part_b, moving[1])
        groups["in0"] = [part_a, plan.swap(part_a, CORE)]
        groups["out0"] = [part_b, plan.swap(part_b, CORE)]
    result, second_0, hidden, slope = feed_forward(
        table, groups, blocks[0][2:], middle, vecs[0], biases[0]
    )
    if plan.cube:
        ct_other, result = together(ct_other, result)
    else:
        ct_own, ct_other = to_frames(plan, cotangent[0])
    rows = regroup(plan, result.reshape(frames, patches, model), 1, 0)
    if plan.seq != 2:
        full = regroup(plan, jnp.concatenate([ct_own, ct_other], 1), 1, 0)
        cut_at = full.shape[1] // 2
        ct_own, ct_other = full[:, :cut_at], full[:, cut_at:]
    (
        active_own,
        *active_other,
        grad,
        small_1,
        normed_1,
        attended_1,
        second_1,
        hidden_1,
        branch_1,
        grad_pre_1,
        proj_in_1,
        grad_mixed_1,
    ) = temporal_block(
        table, groups, blocks[1], rows, ct_own, ct_other, vecs[1], biases[1], clips
    )
    grad = regroup(plan, grad, 0, 1).reshape(count, model)

    def flat(values):
        return values.reshape(count, values.shape[-1])

    pairs_1 = [
        (normed_1, grad_mixed_1, False),
        (attended_1, proj_in_1, False),
        (second_1, grad_pre_1, False),
        (hidden_1, branch_1, True),
    ]
    waits = ()
    if plan.cube:
        g_last, over = weight_grads(table, AS_IS, 1, slabs, pairs_1, "grads_last")
        s_last = lax.psum_scatter(
            g_last.reshape(model, -1), AXES, scatter_dimension=0, tiled=True
        )
        active_come = [plan.swap(item, ROW) for item in active_other]
        waits = (over,)

    grad_middle, proj_in_0, branch_0, grad_pre_0, small_0 = feed_backward(
        table, groups, blocks[0][2:], grad, middle, slope, vecs[0], waits
    )
    pairs_0 = [
        (flat(attended), proj_in_0, False),
        (second_0, grad_pre_0, False),
        (hidden, branch_0, True),
    ]
    waits = ()
    if plan.cube:
        active_come[0], branch_0 = together(active_come[0], branch_0)
        pairs_0[2] = (hidden, branch_0, True)
        keep, send, _ = weight_grads(table, PLACE, 2, slabs, pairs_0, "grads_feed")
        active_come[1], send = together(active_come[1], send)
        s_feed = Sum(plan, keep, send, (model + 2 * width) // 3)
        s_feed.add_core(s_feed.send_core())
        feed_come = s_feed.send_first()
        activations = put_back(table, active_own, active_come, 1)
        waits = (*s_feed.keep, activations)
    grad_own, grad_early, grad_late, grad_mixed_0, tiny_0 = spatial_backward(
        table,
        groups,
        blocks[0][:2],
        grad_middle.reshape(frames, patches, model),
        own,
        other,
        mixed,
        prob,
        vecs[0],
        waits,
    )
    pairs_2 = [(flat(normed_0), flat(grad_mixed_0), False)]
    if plan.cube:
        *feed_come, grad_early = together(*feed_come, grad_early)
        s_feed.add_first(feed_come)
        tokens_come = [plan.swap(grad_early, ROW)]
        feed_come = s_feed.send_second()
        keep, send, _ = weight_grads(
            table,
            PLACE,
            2,
            slabs,
            pairs_2,
            "grads_attention",
            (tiny_0, small_0, small_1),
            s_feed.keep,
        )
        *feed_come, tokens_come[0], grad_late, send = together(
            *feed_come, *tokens_come, grad_late, send
        )
        s_att = Sum(plan, keep, send, 3 * model // 2)
        tokens_come.append(plan.swap(grad_late, ROW))
        s_att.add_core(s_att.send_core())
        att_come = s_att.send_first()
        s_feed.add_second(feed_come)
        feed_come = s_feed.send_last()
        s_att.add_first(together(*att_come))
        att_come = s_att.send_second()
        feed_come[0], feed_come[1], *att_come = together(feed_come[0], feed_come[1], *att_come)
        s_att.add_second(att_come)
        grad_tokens = put_back(table, grad_own, tokens_come, 0)
        *att_come, feed_come[2], grad_tokens, s_last = together(
            *s_att.send_last(), feed_come[2], grad_tokens, s_last
        )
        outs = finish(
            [
                s_att.keep,
                *att_come,
                s_feed.keep,
                *feed_come,
                s_last,
            ],
            [
                norm_gain.shape,
                norm_bias.shape,
                w_qkv.shape,
                w_proj.shape,
                w_in.shape,
                b_in.shape,
                w_out.shape,
            ],
        )
        return (activations[None], grad_tokens[None], *outs)

    active = regroup(plan, jnp.concatenate([active_own[:steps], *active_other], 1), 0, 1)
    half = active.shape[1] // 2
    activations = from_frames(plan, active[:, :half], active[:, half:])
    grad_other = jnp.concatenate([grad_early, grad_late], 0)[:frames]
    grad_tokens = from_frames(plan, grad_own, grad_other)
    each = [(pairs_2 + pairs_0), pairs_1]
    sums = [
        tuple(plain_grad(*each[block][item][:2]) for block in range(2)) for item in range(4)
    ]
    tiny_0, small_0, small_1 = [jnp.sum(item, 0) for item in (tiny_0, small_0, small_1)]
    far = 2 * model + width
    columns = [
        tiny_0[:model],
        small_0[:model],
        small_1[far : far + model],
        small_1[:model],
        tiny_0[model:],
        small_0[model : 2 * model],
        small_1[far + model :],
        small_1[model : 2 * model],
        small_0[2 * model :],
        small_1[2 * model : far],
    ]
    smalls = jnp.concatenate([item.reshape(plan.count, -1) for item in columns], 1)
    mine = lax.psum_scatter(smalls, AXES, scatter_dimension=0, tiled=True).reshape(-1)
    grad_gain = mine[:cut].reshape(2, 2, wide)
    grad_shift = mine[cut : 2 * cut].reshape(2, 2, wide)
    grad_b_in = mine[2 * cut :].reshape(2, -1)
    return (
        activations[None],
        grad_tokens[None],
        grad_gain,
        grad_shift,
        jnp.stack(sums[0]),
        jnp.stack(sums[1]),
        jnp.stack(sums[2]),
        grad_b_in,
        jnp.stack(sums[3]),
    )


def solution(mesh):
    in_specs = (
        P("dp", None, "seq", None),
        P("dp", None, None),
        P("dp", None, "seq", None),
        P(None, None, AXES),
        P(None, None, AXES),
        P(None, AXES, None),
        P(None, AXES, None),
        P(None, AXES, None),
        P(None, AXES),
        P(None, AXES, None),
    )
    out_specs = (
        P("dp", None, "seq", None),
        P("dp", None, "seq", None),
        P(None, None, AXES),
        P(None, None, AXES),
        P(None, AXES, None),
        P(None, AXES, None),
        P(None, AXES, None),
        P(None, AXES),
        P(None, AXES, None),
    )
    return jax.shard_map(
        functools.partial(on_device, Plan(mesh)),
        mesh=mesh,
        in_specs=in_specs,
        out_specs=out_specs,
        check_vma=False,
    )
```

```python
import functools

import jax
import jax.numpy as jnp
from jax import lax
from jax.experimental import pallas as pl
from jax.experimental.pallas import tpu as pltpu
from jax.sharding import PartitionSpec as P

HEADS = 8
MICRO = 2
LANES = 128
JOINED = 256
AXES = ("dp", "seq")
BF = jnp.bfloat16
F32 = jnp.float32
MIB = 1 << 20
SHRINK = 1000
FROM_A, FROM_B, FROM_C, TO_A, PLACE, AS_IS, HERE, CLIP_LENGTHS = range(8)


def dot(left, right, left_dim, right_dim):
    return lax.dot_general(
        left, right, (((left_dim,), (right_dim,)), ((), ())), preferred_element_type=F32
    )


def norm_stats(values):
    centre = values - jnp.mean(values, -1, keepdims=True)
    variance = jnp.mean(centre * centre, -1, keepdims=True)
    inverse = lax.rsqrt(variance + 1e-05)
    return centre * inverse, inverse


def norm_back(grad_scaled, unit_rows, inverse):
    mean_grad = jnp.mean(grad_scaled, -1, keepdims=True)
    mean_cross = jnp.mean(grad_scaled * unit_rows, -1, keepdims=True)
    return inverse * (grad_scaled - mean_grad - unit_rows * mean_cross)


def fold_rows(values):
    return jnp.sum(values.reshape(-1, 8, values.shape[-1]), 0)


def gelu_pair(values):
    cumulative = 0.5 * (1.0 + lax.erf(values * 0.7071067811865476))
    slope = cumulative + values * jnp.exp(-0.5 * values * values) * 0.3989422804014327
    return values * cumulative, slope


def start_weight(segments, groups, table_ref, held, sem):
    for group, which, first_col, cols, block, blocks, to_col in segments:
        slab = 0
        for piece in groups[group]:
            rows = piece.shape[1]
            for idx in range(piece.shape[0]):
                first = table_ref[which, slab] * (rows * blocks) + block * rows
                pltpu.make_async_copy(
                    piece.at[idx, :, pl.ds(first_col, cols)],
                    held.at[pl.ds(pl.multiple_of(first, rows), rows), pl.ds(to_col, cols)],
                    sem,
                ).start()
                slab += 1


def wait_weight(held, sem):
    pltpu.make_async_copy(held, held, sem).wait()


def split_refs(refs, counts):
    groups = []
    for count in counts:
        groups.append(refs[:count])
        refs = refs[count:]
    return groups, refs


def spread_heads(values, width, scale):
    lane = lax.broadcasted_iota(jnp.int32, (1, values.shape[-1]), 1)
    parts = []
    for head in range(values.shape[-1] // width):
        inside = (lane >= head * width) & (lane < (head + 1) * width)
        parts.append(values * jnp.where(inside, scale, 0.0).astype(BF))
    return jnp.concatenate(parts, 0)


def merge_heads(values, width):
    lane = lax.broadcasted_iota(jnp.int32, (1, values.shape[-1]), 1)
    count = values.shape[-1] // width
    rows = values.shape[0] // count
    merged = values[(count - 1) * rows :]
    for head in range(count - 2, -1, -1):
        merged = jnp.where(
            lane < (head + 1) * width, values[head * rows : (head + 1) * rows], merged
        )
    return merged


def attend_forward(sets, model, load, store, keep, bias):
    width = model // HEADS
    scale = width ** (-0.5)
    units = [(item, part) for item in range(sets) for part in range(model // JOINED)]

    def before(item, part):
        first = part * JOINED
        queries = spread_heads(load(item, first), width, scale)
        scores = dot(load(item, model + first), queries, 1, 1)
        return scores if bias is None else scores + bias

    scores = before(*units[0])
    for number, (item, part) in enumerate(units):
        following = before(*units[number + 1]) if number + 1 < len(units) else None
        first = part * JOINED
        exponent = jnp.exp(scores - jnp.max(scores, 0, keepdims=True))
        prob = (exponent * (1.0 / jnp.sum(exponent, 0, keepdims=True))).astype(BF)
        keep(item, part, prob)
        result = merge_heads(dot(prob, load(item, 2 * model + first), 0, 0), width)
        store(item, first, result.astype(BF))
        scores = following


def attend_backward(sets, model, load, load_grad, load_prob, store, late):
    width = model // HEADS
    scale = width ** (-0.5)
    units = [(item, part) for item in range(sets) for part in range(model // JOINED)]

    def before(item, part):
        first = part * JOINED
        spread_grad = spread_heads(load_grad(item, first), width, 1.0)
        return spread_grad, dot(load(item, 2 * model + first), spread_grad, 1, 1)

    def finish(item, part, spread_grad, grad_scores):
        first = part * JOINED
        spread_query = spread_heads(load(item, first), width, scale)
        prob = load_prob(item, part)
        store(item, 2 * model + first, dot(prob, spread_grad, 1, 0).astype(BF))
        store(item, model + first, dot(grad_scores, spread_query, 1, 0).astype(BF))
        scaled_key = load(item, model + first) * jnp.asarray(scale, BF)
        result = merge_heads(dot(grad_scores, scaled_key, 0, 0), width)
        store(item, first, result.astype(BF))

    started = before(*units[0]) if late else None
    waiting = None
    for number, (item, part) in enumerate(units):
        following = None
        if late and number + 1 < len(units):
            following = before(*units[number + 1])
        spread_grad, grad_prob = started if late else before(item, part)
        prob = load_prob(item, part).astype(F32)
        total = jnp.sum(prob * grad_prob, 0, keepdims=True)
        grad_scores = (prob * (grad_prob - total)).astype(BF)
        if late:
            if waiting is not None:
                finish(*waiting)
            waiting = (item, part, spread_grad, grad_scores)
            started = following
        else:
            finish(item, part, spread_grad, grad_scores)
    if late:
        finish(*waiting)


def spatial_forward_kernel(specs, counts, table_ref, *refs):
    groups, refs = split_refs(refs, counts)
    (
        own_ref,
        other_ref,
        vec_ref,
        middle_ref,
        normed_ref,
        qkv_ref,
        attended_ref,
        prob_ref,
        w_qkv,
        w_proj,
        sems,
    ) = refs
    frames, half, model = own_ref.shape

    @pl.when(pl.program_id(0) == 0)
    def _():
        start_weight(specs[0], groups, table_ref, w_qkv, sems.at[0])
        start_weight(specs[1], groups, table_ref, w_proj, sems.at[1])

    rows = jnp.concatenate([own_ref[...], other_ref[...]], 1).astype(F32)
    rows = rows.reshape(frames * 2 * half, model)
    unit, _ = norm_stats(rows)
    normed = (unit * vec_ref[0:1] + vec_ref[1:2]).astype(BF)
    normed_ref[...] = normed.reshape(normed_ref.shape)

    @pl.when(pl.program_id(0) == 0)
    def _():
        wait_weight(w_qkv, sems.at[0])
        wait_weight(w_proj, sems.at[1])

    qkv_ref[...] = dot(normed, w_qkv[...], 1, 0).astype(BF).reshape(qkv_ref.shape)

    def load(frame, first):
        return qkv_ref[frame, :, first : first + JOINED]

    def store(frame, first, value):
        attended_ref[frame, :, first : first + JOINED] = value

    def keep(frame, part, value):
        prob_ref[frame, part] = value

    attend_forward(frames, model, load, store, keep, None)
    attended = attended_ref[...].reshape(rows.shape)
    middle = rows + dot(attended, w_proj[...], 1, 0)
    middle_ref[...] = middle.reshape(middle_ref.shape)


def feed_forward_kernel(specs, counts, table_ref, *refs):
    groups, refs = split_refs(refs, counts)
    (
        middle_ref,
        vec_ref,
        b_in_ref,
        result_ref,
        normed_ref,
        hidden_ref,
        slope_ref,
        w_in,
        w_out,
        sems,
    ) = refs

    @pl.when(pl.program_id(0) == 0)
    def _():
        start_weight(specs[0], groups, table_ref, w_in, sems.at[0])
        start_weight(specs[1], groups, table_ref, w_out, sems.at[1])

    middle = middle_ref[...]
    unit, _ = norm_stats(middle)
    normed = (unit * vec_ref[2:3] + vec_ref[3:4]).astype(BF)
    normed_ref[...] = normed

    @pl.when(pl.program_id(0) == 0)
    def _():
        wait_weight(w_in, sems.at[0])
        wait_weight(w_out, sems.at[1])

    result_ref[...] = middle + ff_through(normed, b_in_ref, w_in, w_out, hidden_ref, slope_ref)


def ff_through(normed, b_in_ref, w_in, w_out, hidden_ref, slope_ref):
    width = w_in.shape[1]
    chunk = min(512, width)
    starts = range(0, width, chunk)

    def before(first):
        cols = slice(first, first + chunk)
        return dot(normed, w_in[:, cols], 1, 0) + b_in_ref[:, cols]

    total, waiting, pre_act = None, None, before(0)
    for first in starts:
        following = before(first + chunk) if first + chunk < width else None
        cols = slice(first, first + chunk)
        hidden, slope = gelu_pair(pre_act)
        hidden = hidden.astype(BF)
        hidden_ref[:, cols] = hidden
        slope_ref[:, cols] = slope.astype(BF)
        if waiting is not None:
            term = dot(waiting, w_out[first - chunk : first, :], 1, 0)
            total = term if total is None else total + term
        waiting, pre_act = hidden, following
    term = dot(waiting, w_out[width - chunk :, :], 1, 0)
    return term if total is None else total + term


def ff_back(grad_out, branch, unit, inverse, gain, w_in, w_out, slope_ref, grad_pre_ref, small_ref):
    model, width = w_in.shape
    chunk = min(512, width)

    def before(first):
        return dot(branch, w_out[first : first + chunk, :], 1, 1)

    grad_second, waiting, grad_hidden = None, None, before(0)
    for first in range(0, width, chunk):
        following = before(first + chunk) if first + chunk < width else None
        cols = slice(first, first + chunk)
        grad_pre = (grad_hidden * slope_ref[:, cols].astype(F32)).astype(BF)
        grad_pre_ref[:, cols] = grad_pre
        small_ref[:, 2 * model + first : 2 * model + first + chunk] += fold_rows(
            grad_pre.astype(F32)
        )
        if waiting is not None:
            term = dot(waiting, w_in[:, first - chunk : first], 1, 1)
            grad_second = term if grad_second is None else grad_second + term
        waiting, grad_hidden = grad_pre, following
    term = dot(waiting, w_in[:, width - chunk :], 1, 1)
    grad_second = term if grad_second is None else grad_second + term
    small_ref[:, :model] += fold_rows(grad_second * unit)
    small_ref[:, model : 2 * model] += fold_rows(grad_second)
    return grad_out + norm_back(grad_second * gain, unit, inverse)


def feed_backward_kernel(specs, counts, table_ref, *refs):
    groups, refs = split_refs(refs, counts)
    (
        grad_ref,
        middle_ref,
        slope_ref,
        vec_ref,
        grad_middle_ref,
        proj_in_ref,
        branch_ref,
        grad_pre_ref,
        small_ref,
        w_in,
        w_out,
        sems,
    ) = refs

    @pl.when(pl.program_id(0) == 0)
    def _():
        start_weight(specs[0], groups, table_ref, w_in, sems.at[0])
        start_weight(specs[1], groups, table_ref, w_out, sems.at[1])
        small_ref[...] = jnp.zeros_like(small_ref)

    unit, inverse = norm_stats(middle_ref[...])
    branch = grad_ref[...].astype(BF)
    branch_ref[...] = branch

    @pl.when(pl.program_id(0) == 0)
    def _():
        wait_weight(w_in, sems.at[0])
        wait_weight(w_out, sems.at[1])

    grad_middle = ff_back(
        grad_ref[...],
        branch,
        unit,
        inverse,
        vec_ref[2:3],
        w_in,
        w_out,
        slope_ref,
        grad_pre_ref,
        small_ref,
    )
    grad_middle_ref[...] = grad_middle
    proj_in_ref[...] = grad_middle.astype(BF)


def spatial_backward_kernel(specs, counts, table_ref, *refs):
    groups, refs = split_refs(refs, counts)
    (
        grad_ref,
        own_ref,
        other_ref,
        qkv_ref,
        prob_ref,
        vec_ref,
        grad_own_ref,
        grad_early_ref,
        grad_late_ref,
        grad_mixed_ref,
        small_ref,
        w_qkv,
        w_proj,
        grad_att,
        sems,
    ) = refs
    frames, half, model = own_ref.shape

    @pl.when(pl.program_id(0) == 0)
    def _():
        start_weight(specs[0], groups, table_ref, w_qkv, sems.at[0])
        start_weight(specs[1], groups, table_ref, w_proj, sems.at[1])
        small_ref[...] = jnp.zeros_like(small_ref)

    rows = jnp.concatenate([own_ref[...], other_ref[...]], 1).astype(F32)
    rows = rows.reshape(frames * 2 * half, model)
    unit, inverse = norm_stats(rows)
    grad_middle = grad_ref[...].reshape(rows.shape)

    @pl.when(pl.program_id(0) == 0)
    def _():
        wait_weight(w_qkv, sems.at[0])
        wait_weight(w_proj, sems.at[1])

    grad_att[...] = dot(grad_middle.astype(BF), w_proj[...], 1, 1).astype(BF)

    def load(frame, first):
        return qkv_ref[frame, :, first : first + JOINED]

    def load_grad(frame, first):
        return grad_att[frame * 2 * half : (frame + 1) * 2 * half, first : first + JOINED]

    def load_prob(frame, part):
        return prob_ref[frame, part]

    def store(frame, first, value):
        grad_mixed_ref[frame, :, first : first + JOINED] = value

    attend_backward(frames, model, load, load_grad, load_prob, store, 0)
    grad_mixed = grad_mixed_ref[...].reshape(rows.shape[0], 3 * model)
    grad_first = dot(grad_mixed, w_qkv[...], 1, 1)
    small_ref[:, :model] += fold_rows(grad_first * unit)
    small_ref[:, model : 2 * model] += fold_rows(grad_first)
    grad_rows = grad_middle + norm_back(grad_first * vec_ref[0:1], unit, inverse)
    grad_rows = grad_rows.astype(BF).reshape(frames, 2 * half, model)
    grad_own_ref[...] = grad_rows[:, :half]
    early = pl.program_id(0) < (pl.num_programs(0) + 1) // 2

    @pl.when(early)
    def _():
        grad_early_ref[...] = grad_rows[:, half:]

    @pl.when(jnp.logical_not(early))
    def _():
        grad_late_ref[...] = grad_rows[:, half:]


def temporal_kernel(specs, counts, tile, clips, halves, table_ref, *refs):
    groups, refs = split_refs(refs, counts)
    (
        rows_ref,
        own_ref,
        other_ref,
        vec_ref,
        b_in_ref,
        active_own_ref,
        *refs,
    ) = refs
    active_other_refs, refs = refs[:halves], refs[halves:]
    (
        grad_ref,
        small_ref,
        normed_one_ref,
        attended_ref,
        normed_two_ref,
        hidden_ref,
        branch_ref,
        grad_pre_ref,
        proj_in_ref,
        grad_mixed_ref,
        w_qkv,
        w_proj,
        w_in,
        w_out,
        mixed,
        probs,
        slope,
        grad_att,
        sems,
    ) = refs
    steps, patches, model = rows_ref.shape
    tiles = patches // tile
    held = (w_qkv, w_proj, w_in, w_out)

    @pl.when(pl.program_id(0) == 0)
    def _():
        for idx in range(4):
            start_weight(specs[idx], groups, table_ref, held[idx], sems.at[idx])
        small_ref[...] = jnp.zeros_like(small_ref)

    def gather_rows(ref):
        parts = [
            ref[:, idx * tile : (idx + 1) * tile, :].reshape(steps * tile, model)
            for idx in range(tiles)
        ]
        return jnp.concatenate(parts, 0)

    def spread_rows(ref, values):
        for idx in range(tiles):
            part = values[idx * steps * tile : (idx + 1) * steps * tile]
            ref[:, idx * tile : (idx + 1) * tile, :] = part.reshape(steps, tile, model).astype(
                ref.dtype
            )

    rows = gather_rows(rows_ref)
    unit_one, inverse_one = norm_stats(rows)
    normed_one = (unit_one * vec_ref[0:1] + vec_ref[1:2]).astype(BF)
    normed_one_ref[...] = normed_one

    @pl.when(pl.program_id(0) == 0)
    def _():
        wait_weight(held[0], sems.at[0])

    mixed[...] = dot(normed_one, w_qkv[...], 1, 0).astype(BF)
    span = steps * tile
    key_row = lax.broadcasted_iota(jnp.int32, (span, span), 0)
    query_row = lax.broadcasted_iota(jnp.int32, (span, span), 1)
    key_step, query_step = key_row // tile, query_row // tile
    key_clip, query_clip, end = jnp.zeros_like(key_row), jnp.zeros_like(key_row), 0
    for clip in range(clips):
        end = end + table_ref[CLIP_LENGTHS, clip]
        key_clip = key_clip + jnp.where(key_step >= end, 1, 0)
        query_clip = query_clip + jnp.where(query_step >= end, 1, 0)
    seen = (key_clip == query_clip) & (key_step <= query_step) & (key_row % tile == query_row % tile)
    bias = jnp.where(seen, 0.0, -1000000000.0)
    bias = jnp.concatenate([bias] * (JOINED // (model // HEADS)), 1)

    def load(idx, first):
        return mixed[idx * span : (idx + 1) * span, first : first + JOINED]

    def store(idx, first, value):
        attended_ref[idx * span : (idx + 1) * span, first : first + JOINED] = value

    def keep(idx, part, value):
        probs[idx, part] = value

    attend_forward(tiles, model, load, store, keep, bias)

    @pl.when(pl.program_id(0) == 0)
    def _():
        for idx in range(1, 4):
            wait_weight(held[idx], sems.at[idx])

    middle = rows + dot(attended_ref[...], w_proj[...], 1, 0)
    unit_two, inverse_two = norm_stats(middle)
    normed_two = (unit_two * vec_ref[2:3] + vec_ref[3:4]).astype(BF)
    normed_two_ref[...] = normed_two
    result = middle + ff_through(normed_two, b_in_ref, w_in, w_out, hidden_ref, slope)
    from_own = pl.program_id(0) < halves

    @pl.when(from_own)
    def _():
        spread_rows(active_own_ref, result)

    for idx, active_other_ref in enumerate(active_other_refs):

        @pl.when(pl.program_id(0) == halves + idx)
        def _():
            spread_rows(active_other_ref, result)

    branch = gather_rows(jnp.where(from_own, own_ref[...], other_ref[...]))
    branch_ref[...] = branch
    grad_middle = ff_back(
        branch.astype(F32),
        branch,
        unit_two,
        inverse_two,
        vec_ref[2:3],
        w_in,
        w_out,
        slope,
        grad_pre_ref,
        small_ref,
    )
    proj_in = grad_middle.astype(BF)
    proj_in_ref[...] = proj_in
    grad_att[...] = dot(proj_in, w_proj[...], 1, 1).astype(BF)

    def load_grad(idx, first):
        return grad_att[idx * span : (idx + 1) * span, first : first + JOINED]

    def load_prob(idx, part):
        return probs[idx, part]

    def store_grad(idx, first, value):
        grad_mixed_ref[idx * span : (idx + 1) * span, first : first + JOINED] = value

    attend_backward(tiles, model, load, load_grad, load_prob, store_grad, 1)
    grad_first = dot(grad_mixed_ref[...], w_qkv[...], 1, 1)
    offset = 2 * model + w_in.shape[1]
    small_ref[:, offset : offset + model] += fold_rows(grad_first * unit_one)
    small_ref[:, offset + model : offset + 2 * model] += fold_rows(grad_first)
    spread_rows(
        grad_ref, grad_middle + norm_back(grad_first * vec_ref[0:1], unit_one, inverse_one)
    )


def weight_grad_kernel(jobs, which, slabs, n_in, n_out, has_small, table_ref, *refs):
    ins, refs = refs[:n_in], refs[n_in:]
    over, fixed, moving, staged, in_sems, sem = refs[-6:]
    outs = refs[-6 - n_out : -6]
    each = slabs // n_out
    rows = staged.shape[1]
    steps, loads = [], []
    for number, (left, right, by_rows, first_col, tiles) in enumerate(jobs):
        begin = 0
        for item, size in enumerate(tiles):
            needs = []
            if item == 0:
                still = right if by_rows else left
                needs.append((still, 0, ins[still].shape[1], fixed, number % 2, 0))
            slot = len(steps) % 2
            needs.append((left if by_rows else right, begin, size, moving, slot, 1))
            loads.append(needs)
            steps.append((by_rows, number % 2, slot, begin, size, first_col))
            begin += size

    def copies(step):
        return [
            pltpu.make_async_copy(
                ins[array].at[:, pl.ds(first, size)],
                buffer.at[slot, :, pl.ds(0, size)],
                in_sems.at[kind, slot],
            )
            for array, first, size, buffer, slot, kind in loads[step]
        ]

    def send_out(first_col, cols):
        for half, out in enumerate(outs):
            pltpu.make_async_copy(
                staged.at[pl.ds(half * each, each), :, pl.ds(first_col, cols)],
                out.at[:, :, pl.ds(first_col, cols)],
                sem,
            ).start()

    for copy in copies(0):
        copy.start()
    for step, (by_rows, still, slot, begin, size, first_col) in enumerate(steps):
        if step + 1 < len(steps):
            for copy in copies(step + 1):
                copy.start()
        for copy in copies(step):
            copy.wait()
        if by_rows:
            cols = fixed.shape[2]
            value = dot(moving[slot, :, :size], fixed[still], 0, 0).astype(BF)
            fold = ins[jobs[-1][0]].shape[1] // (slabs * rows)
            for idx in range(size // (fold * rows)):
                place = table_ref[which, begin // (fold * rows) + idx]
                for part in range(fold):
                    source = (idx * fold + part) * rows
                    to_col = first_col + part * cols
                    staged[place, :, to_col : to_col + cols] = value[source : source + rows]
            if step + 1 == len(steps):
                send_out(first_col, fold * cols)
        else:
            value = dot(fixed[still], moving[slot, :, :size], 0, 0).astype(BF)
            to_col = first_col + begin
            for idx in range(slabs):
                place = table_ref[which, idx]
                staged[place, :, to_col : to_col + size] = value[idx * rows : (idx + 1) * rows]
            send_out(to_col, size)
    if has_small:
        width = staged.shape[2] - LANES
        staged[:, :, width:] = small_slabs(refs[0], refs[1:4])
        send_out(width, LANES)
    for out in outs:
        pltpu.make_async_copy(out, out, sem).wait()
    over[...] = jnp.zeros_like(over)


def small_slabs(place_ref, sums):
    tiny_0, small_0, small_1 = [jnp.sum(ref[...], 0, keepdims=True) for ref in sums]
    model = tiny_0.shape[1] // 2
    width = small_0.shape[1] - 2 * model
    far = 2 * model + width
    place = place_ref[...][:, :1]
    slabs = place.shape[0]

    def table(items):
        total = jnp.zeros((slabs, LANES), F32)
        offset = 0
        for values in items:
            length = values.shape[1]
            each = length // slabs
            lane = lax.broadcasted_iota(jnp.int32, (1, length), 1)
            mine = jnp.where(lane // each == place, values, 0.0).astype(BF)
            source = lax.broadcasted_iota(jnp.int32, (length, LANES), 0)
            target = lax.broadcasted_iota(jnp.int32, (length, LANES), 1)
            choose = jnp.where(source % each + offset == target, 1.0, 0.0).astype(BF)
            total = total + dot(mine, choose, 1, 0)
            offset += each
        return total

    norms = table(
        [
            tiny_0[:, :model],
            small_0[:, :model],
            small_1[:, far : far + model],
            small_1[:, :model],
            tiny_0[:, model:],
            small_0[:, model : 2 * model],
            small_1[:, far + model :],
            small_1[:, model : 2 * model],
        ]
    )
    biases = table([small_0[:, 2 * model :], small_1[:, 2 * model : far]])
    row = lax.broadcasted_iota(jnp.int32, (slabs, 16, LANES), 1)
    both = jnp.where(row == 0, norms[:, None, :], jnp.where(row == 1, biases[:, None, :], 0.0))
    return both.astype(BF)


def pack_kernel(copies, n_in, n_small, row_ref, *refs):
    ins, refs = refs[:n_in], refs[n_in:]
    smalls, refs = refs[:n_small], refs[n_small:]
    outs, wide = refs[:-1], refs[-1]
    for source, source_index, target, target_index in copies:
        index = tuple(item(row_ref[0]) if callable(item) else item for item in source_index)
        outs[target][target_index] = ins[source][index]
    if n_small:
        gain_ref, shift_ref, bias_ref = smalls
        wide[...] = jnp.zeros_like(wide)
        for block in range(2):
            wide[2 * block : 2 * block + 2, : gain_ref.shape[2]] = gain_ref[block].astype(F32)
            wide[4 + 2 * block : 6 + 2 * block, : gain_ref.shape[2]] = shift_ref[block].astype(F32)
        wide[8:10, : bias_ref.shape[1]] = bias_ref[...].astype(F32)
        width = outs[0].shape[1] - LANES
        outs[0][:, width:] = wide[...].astype(BF)


def unpack_kernel(place_ref, *refs):
    pieces, vec_refs, bias_refs, (held, sem) = refs[:-6], refs[-6:-4], refs[-4:-2], refs[-2:]
    first = 0
    for piece in pieces:
        count = piece.shape[0]
        width = piece.shape[2] - LANES
        pltpu.make_async_copy(
            piece.at[:, :, pl.ds(width, LANES)], held.at[pl.ds(first, count)], sem
        ).start()
        first += count
    pltpu.make_async_copy(held, held, sem).wait()
    values = held[...].astype(F32)
    place = place_ref[...][:, :1]
    slabs = place.shape[0]

    def row(idx, length):
        each = length // slabs
        lane = lax.broadcasted_iota(jnp.int32, (LANES, length), 1)
        source = lax.broadcasted_iota(jnp.int32, (LANES, length), 0)
        choose = jnp.where(lane % each == source, 1.0, 0.0).astype(BF)
        wide = dot(values[:, idx, :].astype(BF), choose, 1, 0)
        mine = lax.broadcasted_iota(jnp.int32, (1, length), 1) // each == place
        return jnp.sum(jnp.where(mine, wide, 0.0), 0, keepdims=True)

    model, width = vec_refs[0].shape[1], bias_refs[0].shape[1]
    for block in range(2):
        for norm in range(2):
            vec_refs[block][2 * norm : 2 * norm + 1] = row(2 * block + norm, model)
            vec_refs[block][2 * norm + 1 : 2 * norm + 2] = row(4 + 2 * block + norm, model)
        bias_refs[block][...] = row(8 + block, width)


def finish_kernel(*refs):
    parts = [refs[:4], refs[4:8]]
    last_ref = refs[8]
    gain_ref, shift_ref, qkv_ref, proj_ref, in_ref, b_in_ref, out_ref = refs[9:]

    def total(idx, first, cols):
        if idx == 2:
            return last_ref[:, first : first + cols].astype(F32)
        return add_up(*[ref[0, :, first : first + cols] for ref in parts[idx]])

    model, width = proj_ref.shape[2], in_ref.shape[2]
    triple, rows = 3 * model, proj_ref.shape[1]
    start = triple + model
    qkv_ref[0] = total(0, 0, triple)
    qkv_ref[1] = total(2, 0, triple)
    proj_ref[0] = total(1, 0, model)
    proj_ref[1] = total(2, triple, model)
    in_ref[0] = total(1, model, width)
    in_ref[1] = total(2, start, width)
    for idx in range(width // model):
        to_rows = slice(idx * rows, (idx + 1) * rows)
        out_ref[0, to_rows] = total(1, model + width + idx * model, model)
        out_ref[1, to_rows] = total(2, start + width + idx * model, model)
    small = total(0, triple, LANES)
    wide = gain_ref.shape[2]
    for block in range(2):
        for norm in range(2):
            first = (2 * block + norm) * wide
            gain_ref[block, norm : norm + 1] = small[0:1, first : first + wide]
            first += 4 * wide
            shift_ref[block, norm : norm + 1] = small[0:1, first : first + wide]
        cols = b_in_ref.shape[1]
        b_in_ref[block : block + 1] = small[1:2, block * cols : (block + 1) * cols]


def add_kernel(count, plans, *refs):
    outs = refs[2 * count :]
    for out, parts in zip(outs, plans):
        for pair, index, first, cols, to_col in parts:
            place = index + (slice(first, first + cols),)
            value = add_up(refs[2 * pair][place], refs[2 * pair + 1][place])
            out[..., to_col : to_col + cols] = value.astype(out.dtype)


def place_kernel(axis, table_ref, _, *refs):
    first = 0
    for come_ref in refs[:-1]:
        size = come_ref.shape[axis]
        place = [slice(None)] * 3
        place[axis] = slice(first, first + size)
        refs[-1][tuple(place)] = come_ref[...]
        first += size


ANY = pl.BlockSpec(memory_space=pl.ANY)
SMEM = pl.BlockSpec(memory_space=pltpu.SMEM)
Shape = jax.ShapeDtypeStruct


def whole(shape):
    return pl.BlockSpec(shape, lambda idx, *_: (0,) * len(shape))


def leading(shape):
    return pl.BlockSpec(shape, lambda idx, *_: (idx,) + (0,) * (len(shape) - 1))


def mine(shape, blocks):
    rest = (0,) * (len(shape) - 1)
    return pl.BlockSpec(shape, lambda idx, table: (table[HERE, 0] * blocks + idx,) + rest)


def limits(megabytes):
    return pltpu.CompilerParams(vmem_limit_bytes=megabytes * MIB)


def cost(flops, bytes_accessed):
    return pl.CostEstimate(
        flops=flops // SHRINK, bytes_accessed=bytes_accessed // SHRINK, transcendentals=0
    )


def pack(row, sources, targets, copies, smalls, name):
    vmem = pl.BlockSpec(memory_space=pltpu.VMEM)
    return pl.pallas_call(
        functools.partial(pack_kernel, copies, len(sources), len(smalls)),
        in_specs=[SMEM] + [vmem] * (len(sources) + len(smalls)),
        out_specs=[vmem] * len(targets),
        out_shape=[Shape(shape, BF) for shape in targets],
        scratch_shapes=[pltpu.VMEM((16, LANES), F32)],
        compiler_params=limits(60),
        name=name,
    )(row, *sources, *smalls)


def finish(parts, shapes):
    vmem = pl.BlockSpec(memory_space=pltpu.VMEM)
    return pl.pallas_call(
        finish_kernel,
        in_specs=[vmem] * len(parts),
        out_specs=[vmem] * 7,
        out_shape=[Shape(shape, F32) for shape in shapes],
        compiler_params=limits(60),
        name="finish",
    )(*parts)


def add_pairs(pairs, outs, name):
    vmem = pl.BlockSpec(memory_space=pltpu.VMEM)
    return pl.pallas_call(
        functools.partial(add_kernel, len(pairs), tuple(parts for _, parts in outs)),
        in_specs=[vmem] * (2 * len(pairs)),
        out_specs=[vmem] * len(outs),
        out_shape=[Shape(shape, BF) for shape, _ in outs],
        compiler_params=limits(60),
        name=name,
    )(*[item for pair in pairs for item in pair])


def put_back(table, full, come, axis):
    half = (full.shape[0] // 2,) + full.shape[1:]
    return pl.pallas_call(
        functools.partial(place_kernel, axis),
        grid_spec=pltpu.PrefetchScalarGridSpec(
            num_scalar_prefetch=1,
            grid=(1,),
            in_specs=[ANY] + [whole(item.shape) for item in come],
            out_specs=pl.BlockSpec(half, lambda idx, table: (1 - table[HERE, 0], 0, 0)),
        ),
        out_shape=Shape(full.shape, BF),
        input_output_aliases={1: 0},
        compiler_params=limits(60),
        name="put_back",
    )(table, full, *come)


def unpack(place, pieces, model, width):
    slabs, rows = place.shape[0], pieces[0].shape[1]
    vmem = pl.BlockSpec(memory_space=pltpu.VMEM)
    return pl.pallas_call(
        unpack_kernel,
        in_specs=[vmem] + [ANY] * len(pieces),
        out_specs=[vmem] * 4,
        out_shape=[Shape((4, model), F32)] * 2 + [Shape((1, width), F32)] * 2,
        scratch_shapes=[pltpu.VMEM((slabs, rows, LANES), BF), pltpu.SemaphoreType.DMA],
        compiler_params=limits(60),
        name="unpack",
    )(place, *pieces)


class Weight:
    def __init__(self, shape, segments):
        self.shape = shape
        self.segments = segments


def call(kernel, name, table, groups, weights, static, inputs, outputs, scratch, grid, flops, traffic, first):
    names = []
    for weight in weights:
        for segment in weight.segments:
            if segment[0] not in names:
                names.append(segment[0])
    specs = tuple(
        tuple((names.index(segment[0]),) + tuple(segment[1:]) for segment in weight.segments)
        for weight in weights
    )
    pieces = [tuple(groups[item]) for item in names] + [tuple(first)]
    counts = tuple(len(item) for item in pieces)
    pieces = [item for group in pieces for item in group]
    return pl.pallas_call(
        functools.partial(kernel, specs, counts, *static),
        grid_spec=pltpu.PrefetchScalarGridSpec(
            num_scalar_prefetch=1,
            grid=(grid,),
            in_specs=[ANY] * len(pieces) + [spec for _, spec in inputs],
            out_specs=[spec for _, spec in outputs],
            scratch_shapes=[pltpu.VMEM(weight.shape, BF) for weight in weights]
            + scratch
            + [pltpu.SemaphoreType.DMA((len(weights),))],
        ),
        out_shape=[shape for shape, _ in outputs],
        compiler_params=limits(60),
        cost_estimate=cost(flops, traffic),
        name=name,
    )(table, *pieces, *[value for value, _ in inputs])


def spatial_forward(table, groups, weights, own, other, vec, first=()):
    frames, half, model = other.shape
    patches = 2 * half
    each = min(2, frames)
    grid = frames // each
    joined = model // JOINED
    spread = patches * (JOINED * HEADS // model)

    def out(*shape, dtype=BF):
        return Shape((frames,) + shape, dtype), leading((each,) + shape)

    return call(
        spatial_forward_kernel,
        "spatial_forward",
        table,
        groups,
        weights,
        (),
        [
            (own, mine((each, half, model), grid)),
            (other, leading((each, half, model))),
            (vec, whole(vec.shape)),
        ],
        [
            out(patches, model, dtype=F32),
            out(patches, model),
            out(patches, 3 * model),
            out(patches, model),
            out(joined, patches, spread),
        ],
        [],
        grid,
        2 * frames * patches * model * (4 * model + 2 * patches),
        frames * patches * model * 24,
        first,
    )


def feed_forward(table, groups, weights, middle, vec, b_in, first=()):
    tokens, model = middle.shape
    width = b_in.shape[1]
    block = min(512, tokens)
    return call(
        feed_forward_kernel,
        "feed_forward",
        table,
        groups,
        weights,
        (),
        [
            (middle, leading((block, model))),
            (vec, whole(vec.shape)),
            (b_in, whole(b_in.shape)),
        ],
        [
            (Shape((tokens, model), F32), leading((block, model))),
            (Shape((tokens, model), BF), leading((block, model))),
            (Shape((tokens, width), BF), leading((block, width))),
            (Shape((tokens, width), BF), leading((block, width))),
        ],
        [],
        tokens // block,
        4 * tokens * model * width,
        tokens * (8 * model + 4 * width),
        first,
    )


def feed_backward(table, groups, weights, grad, middle, slope, vec, first=()):
    tokens, model = middle.shape
    width = slope.shape[1]
    block = min(512, tokens)
    small = (8, 2 * model + width)
    return call(
        feed_backward_kernel,
        "feed_backward",
        table,
        groups,
        weights,
        (),
        [
            (grad, leading((block, model))),
            (middle, leading((block, model))),
            (slope, leading((block, width))),
            (vec, whole(vec.shape)),
        ],
        [
            (Shape((tokens, model), F32), leading((block, model))),
            (Shape((tokens, model), BF), leading((block, model))),
            (Shape((tokens, model), BF), leading((block, model))),
            (Shape((tokens, width), BF), leading((block, width))),
            (Shape(small, F32), whole(small)),
        ],
        [],
        tokens // block,
        4 * tokens * model * width,
        tokens * (14 * model + 4 * width),
        first,
    )


def spatial_backward(table, groups, weights, grad, own, other, mixed, prob, vec, first=()):
    frames, half, model = other.shape
    patches = 2 * half
    each = min(2, frames)
    small = (8, 2 * model)
    blocks = frames // each
    early = (blocks + 1) // 2
    late = max(1, blocks - early)
    block = (each, half, model)
    return call(
        spatial_backward_kernel,
        "spatial_backward",
        table,
        groups,
        weights,
        (),
        [
            (grad, leading((each, patches, model))),
            (own, mine((each, half, model), frames // each)),
            (other, leading((each, half, model))),
            (mixed, leading((each, patches, 3 * model))),
            (prob, leading((each,) + prob.shape[1:])),
            (vec, whole(vec.shape)),
        ],
        [
            (Shape(own.shape, BF), mine((each, half, model), frames // each)),
            (
                Shape((early * each, half, model), BF),
                pl.BlockSpec(block, lambda idx, _: (jnp.minimum(idx, early - 1), 0, 0)),
            ),
            (
                Shape((late * each, half, model), BF),
                pl.BlockSpec(block, lambda idx, _: (jnp.maximum(idx - early, 0), 0, 0)),
            ),
            (Shape((frames, patches, 3 * model), BF), leading((each, patches, 3 * model))),
            (Shape(small, F32), whole(small)),
        ],
        [pltpu.VMEM((each * patches, model), BF)],
        frames // each,
        2 * frames * patches * model * (4 * model + 4 * patches),
        frames * patches * model * 30,
        first,
    )


def temporal_block(table, groups, weights, rows, own, other, vec, b_in, clips, first=()):
    steps, patches, model = rows.shape
    width = b_in.shape[1]
    half = other.shape[1]
    each = min(64, half)
    tile = min(16, each)
    halves = half // each
    last = halves - 1
    count = steps * each
    total = steps * patches
    small = (8, 4 * model + width)
    block = (steps, each, model)
    spread = steps * tile * (JOINED * HEADS // model)
    mine_part = pl.BlockSpec(
        block, lambda idx, table: (table[HERE, 0], jnp.minimum(idx, last), 0)
    )
    other_part = pl.BlockSpec(block, lambda idx, _: (0, jnp.maximum(idx - halves, 0), 0))
    return call(
        temporal_kernel,
        "temporal_block",
        table,
        groups,
        weights,
        (tile, clips, halves),
        [
            (rows, pl.BlockSpec(block, lambda idx, _: (0, idx, 0))),
            (own, mine_part),
            (other, other_part),
            (vec, whole(vec.shape)),
            (b_in, whole(b_in.shape)),
        ],
        [
            (Shape(own.shape, BF), mine_part),
            *[(Shape(block, BF), whole(block))] * halves,
            (Shape((steps, patches, model), F32), pl.BlockSpec(block, lambda idx, _: (0, idx, 0))),
            (Shape(small, F32), whole(small)),
            (Shape((total, model), BF), leading((count, model))),
            (Shape((total, model), BF), leading((count, model))),
            (Shape((total, model), BF), leading((count, model))),
            (Shape((total, width), BF), leading((count, width))),
            (Shape((total, model), BF), leading((count, model))),
            (Shape((total, width), BF), leading((count, width))),
            (Shape((total, model), BF), leading((count, model))),
            (Shape((total, 3 * model), BF), leading((count, 3 * model))),
        ],
        [
            pltpu.VMEM((count, 3 * model), BF),
            pltpu.VMEM((each // tile, model // JOINED, steps * tile, spread), BF),
            pltpu.VMEM((count, width), BF),
            pltpu.VMEM((count, model), BF),
        ],
        2 * halves,
        4 * total * model * (4 * model + 2 * width),
        total * (40 * model + 4 * width),
        first,
    )


def weight_grads(table, which, n_out, slabs, jobs, name, small=None, first=()):
    tile, most = 512, 1024
    tokens = jobs[0][0].shape[0]
    plans, operands = [], []
    col, flops, rows = 0, 0, 0
    for left, right, by_rows in jobs:
        length = (left if by_rows else right).shape[1]
        tiles = tuple(sorted(min(most, length - begin) for begin in range(0, length, most)))
        plans.append((len(operands), len(operands) + 1, by_rows, col, tiles))
        operands += [left, right]
        if not by_rows:
            rows = left.shape[1] // slabs
        col += length
        flops += 2 * tokens * left.shape[1] * right.shape[1]
    extra = []
    if small is not None:
        place = jnp.broadcast_to(table[TO_A][:, None], (slabs, LANES))
        extra = [place, *small]
        col += LANES
    vmem = pl.BlockSpec(memory_space=pltpu.VMEM)
    return pl.pallas_call(
        functools.partial(
            weight_grad_kernel,
            tuple(plans),
            which,
            slabs,
            len(operands),
            n_out,
            int(small is not None),
        ),
        in_specs=[SMEM] + [ANY] * len(operands) + [vmem] * len(extra) + [ANY] * len(first),
        out_specs=[ANY] * n_out + [vmem],
        out_shape=[Shape((slabs // n_out, rows, col), BF)] * n_out + [Shape((8, LANES), F32)],
        scratch_shapes=[
            pltpu.VMEM((2, tokens, tile), BF),
            pltpu.VMEM((2, tokens, most), BF),
            pltpu.VMEM((slabs, rows, col), BF),
            pltpu.SemaphoreType.DMA((2, 2)),
            pltpu.SemaphoreType.DMA,
        ],
        compiler_params=limits(60),
        cost_estimate=cost(flops, flops // 512),
        name=name,
    )(table, *operands, *extra, *first)


def plain_grad(left, right):
    grad = dot(left, right, 0, 0)
    return lax.psum_scatter(grad, AXES, scatter_dimension=0, tiled=True)


class Plan:
    def __init__(self, mesh):
        self.dp = mesh.shape["dp"]
        self.seq = mesh.shape["seq"]
        self.count = self.dp * self.seq
        self.cube = self.dp == 16 and self.seq == 2

    def swap(self, value, mask):
        pairs = [(idx, idx ^ mask) for idx in range(self.count)]
        return lax.ppermute(value, AXES, pairs)

    def me(self):
        return lax.axis_index("dp") * self.seq + lax.axis_index("seq")


ROW, CORE, COLUMN, Z_LOW, Z_HIGH = 1, 2, 4, 8, 16


def gather_masks(order):
    masks = [0]
    for stage in order:
        masks = masks + [mask ^ bit for bit in stage for mask in masks]
    return masks


STAGE_Z = (Z_LOW, Z_HIGH, Z_LOW | Z_HIGH)
GATHER_A = (STAGE_Z, (COLUMN,), (ROW,), (CORE,))
GATHER_B = (STAGE_Z, (ROW,), (COLUMN,), (CORE,))
GATHER_C = ((ROW,), STAGE_Z, (COLUMN,), (CORE,))


def join(*values, axis=0):
    total = sum(value.shape[axis] for value in values)
    low = jnp.array(-jnp.inf, values[0].dtype)
    joined, first = None, 0
    for value in values:
        count = value.shape[axis]
        sides = [(0, 0, 0)] * value.ndim
        sides[axis] = (first, total - first - count, 0)
        padded = lax.pad(value, low, sides)
        joined = padded if joined is None else jnp.maximum(joined, padded)
        first += count
    return joined


SUM_A = (CORE, COLUMN, ROW, Z_HIGH, Z_LOW)


def sum_masks(order):
    masks = [0]
    for bit in reversed(order):
        masks = masks + [mask ^ bit for mask in masks]
    return masks


def inverse_masks(masks, order):
    place = jnp.zeros_like(masks)
    for idx, bit in enumerate(reversed(order)):
        place = place + jnp.where((masks & bit) != 0, 1 << idx, 0)
    return place


def add_up(*values):
    total = values[0].astype(F32)
    for value in values[1:]:
        total = total + value.astype(F32)
    return total


class Sum:
    def __init__(self, plan, keep, send, cut):
        self.plan = plan
        self.keep, self.away = keep, send
        cols = keep.shape[2]
        parts = ((0, cut, 0), (cut, cols - cut, 1))
        self.parts = [part for part in parts if part[1]]

    def send_core(self):
        return self.plan.swap(self.away, CORE)

    def add_core(self, come):
        rows, cols = self.keep.shape[1:]
        shape = (2, 2, 4, rows, cols)
        every = slice(None)
        outs = []
        for first, size, index in self.parts:
            for half in range(2):
                lead = (half, every) if index == 0 else (every, half)
                part = (0, lead + (every, every), first, size, 0)
                outs.append(((2, 4, rows, size), (part,)))
        sums = add_pairs([(self.keep.reshape(shape), come.reshape(shape))], outs, "add_core")
        self.keep, self.away = list(sums[::2]), list(sums[1::2])

    def send_first(self):
        bits = [(COLUMN, ROW)[index] for _, _, index in self.parts]
        return [self.plan.swap(item, bit) for item, bit in zip(self.away, bits)]

    def add_first(self, come):
        pairs = list(zip(self.keep, come))
        every = slice(None)
        outs = []
        for pair, (keep, _) in enumerate(pairs):
            for half in range(2):
                part = (pair, (half, every, every), 0, keep.shape[3], 0)
                outs.append((keep.shape[1:], (part,)))
        sums = add_pairs(pairs, outs, "add_first")
        self.keep, self.away = list(sums[::2]), list(sums[1::2])

    def send_second(self):
        bits = [(ROW, COLUMN)[index] for _, _, index in self.parts]
        return [self.plan.swap(item, bit) for item, bit in zip(self.away, bits)]

    def add_second(self, come):
        pairs = list(zip(self.keep, come))
        every = slice(None)
        rows = self.keep[0].shape[1]
        total = sum(size for _, size, _ in self.parts)
        outs = []
        for idx in range(4):
            lead = (slice(idx, idx + 1), every)
            parts = tuple(
                (pair, lead, 0, size, first) for pair, (first, size, _) in enumerate(self.parts)
            )
            outs.append(((1, rows, total), parts))
        sums = add_pairs(pairs, outs, "add_second")
        self.keep, self.away = sums[0], sums[1:]

    def send_last(self):
        one, two, both = self.away
        swap = self.plan.swap
        return [swap(one, Z_LOW), swap(two, Z_HIGH), swap(both, Z_LOW | Z_HIGH)]


def together(*values):
    return lax.optimization_barrier(values)


def to_frames(plan, values):
    full = lax.all_to_all(values, "seq", split_axis=0, concat_axis=1, tiled=True)
    half = full.shape[1] // 2
    return full[:, :half], full[:, half:]


def from_frames(plan, own, other):
    full = jnp.concatenate([own, other], 1)
    return lax.all_to_all(full, "seq", split_axis=1, concat_axis=0, tiled=True)


def regroup(plan, values, split_axis, concat_axis):
    members = plan.seq // MICRO
    if members == 1:
        return values
    row = lax.axis_index("seq")
    rank = row % members
    size = values.shape[split_axis] // members
    span = values.shape[concat_axis]
    shape = list(values.shape)
    shape[split_axis] = size
    shape[concat_axis] = span * members
    result = jnp.zeros(shape, values.dtype)
    for shift in range(members):
        target = (rank + shift) % members
        part = lax.dynamic_slice_in_dim(values, target * size, size, split_axis)
        if shift:
            pairs = [
                (idx, idx - idx % members + (idx + shift) % members) for idx in range(plan.seq)
            ]
            part = lax.ppermute(part, "seq", pairs)
        source = (rank - shift) % members
        result = lax.dynamic_update_slice_in_dim(result, part, source * span, concat_axis)
    return result


def plain_weights(plan, weights, small):
    groups, blocks = {}, []
    for idx in range(2):
        block = []
        for name, value in zip(("qkv", "proj", "in", "out"), weights):
            key = name + str(idx)
            whole_value = lax.all_gather(value[idx], AXES, axis=0, tiled=True)
            groups[key] = [whole_value[None]]
            block.append(Weight(whole_value.shape, ((key, AS_IS, 0, value.shape[2], 0, 1, 0),)))
        blocks.append(block)
    return groups, blocks, lax.all_gather(small, AXES, axis=0).astype(F32)


def cube_weights(shapes, fold):
    (model, triple), _, (_, width), _ = shapes
    start = triple + model + width
    first = [
        Weight(shapes[0], (("att0", FROM_C, 0, triple, 0, 1, 0),)),
        Weight(shapes[1], (("att0", FROM_C, triple, model, 0, 1, 0),)),
        Weight(shapes[2], (("in0", FROM_A, 0, width, 0, 1, 0),)),
        Weight(
            shapes[3],
            tuple(("out0", FROM_B, idx * model, model, idx, fold, 0) for idx in range(fold)),
        ),
    ]
    last = [
        Weight(shapes[0], (("last", AS_IS, 0, triple, 0, 1, 0),)),
        Weight(shapes[1], (("last", AS_IS, triple, model, 0, 1, 0),)),
        Weight(shapes[2], (("last", AS_IS, triple + model, width, 0, 1, 0),)),
        Weight(
            shapes[3],
            tuple(("last", AS_IS, start + idx * model, model, idx, fold, 0) for idx in range(fold)),
        ),
    ]
    return [first, last]


def cube_packs(plan, row, tokens, weights, smalls):
    w_qkv, w_proj, w_in, w_out = weights
    rows, triple = w_qkv.shape[1:]
    model, width = w_proj.shape[2], w_in.shape[2]
    fold = w_out.shape[1] // rows
    start = triple + model + width
    steps, here = tokens.shape[1:3]
    count = steps // 2

    def cols(first, size):
        return (slice(None), pl.ds(first, size))

    copies = [
        (0, (0,), 0, cols(0, triple)),
        (1, (0,), 0, cols(triple, model)),
        (4, (0, lambda me: pl.ds((1 - me) * count, count)), 3, (slice(None),)),
        (2, (0,), 1, cols(0, width)),
        (0, (1,), 2, cols(0, triple)),
        (1, (1,), 2, cols(triple, model)),
        (2, (1,), 2, cols(triple + model, width)),
    ]
    for idx in range(fold):
        part = pl.ds(idx * rows, rows)
        copies.append((3, (0, part), 1, cols(width + idx * model, model)))
        copies.append((3, (1, part), 2, cols(start + idx * model, model)))
    targets = [
        (rows, triple + model + LANES),
        (rows, width + fold * model),
        (rows, start + fold * model),
        (count, here, model),
    ]
    return pack(row, [*weights, tokens], targets, copies, smalls, "pack")


def on_device(plan, tokens, lengths, cotangent, norm_gain, norm_bias, w_qkv, w_proj, w_in, b_in, w_out):
    steps_all, here, model = tokens.shape[1:]
    steps = steps_all // MICRO
    width = b_in.shape[1] * plan.count
    row = lax.axis_index("seq")
    micro = row * MICRO // plan.seq
    own_lengths = lax.dynamic_index_in_dim(lengths[0], micro, 0, keepdims=False)
    clips = own_lengths.shape[0]

    weights = (w_qkv, w_proj, w_in, w_out)
    shapes = ((model, 3 * model), (model, model), (model, width), (width, model))
    wide = model // plan.count
    cut = 4 * wide
    slabs = plan.count
    waits = ()
    if plan.cube:
        me = plan.me()
        orders = [gather_masks(GATHER_A), gather_masks(GATHER_B), gather_masks(GATHER_C), sum_masks(SUM_A)]
        table = jnp.concatenate(
            [
                me ^ jnp.array(orders, jnp.int32),
                inverse_masks(me ^ jnp.arange(plan.count, dtype=jnp.int32), SUM_A)[None],
                jnp.arange(plan.count, dtype=jnp.int32)[None],
                jnp.broadcast_to(row, (1, plan.count)).astype(jnp.int32),
                jnp.pad(own_lengths, (0, plan.count - clips))[None],
            ]
        )
        row_index = jnp.reshape(row, (1,)).astype(jnp.int32)
        own = tokens[0]
        att, feed_0, last, away = cube_packs(
            plan, row_index, tokens, weights, (norm_gain, norm_bias, b_in)
        )
        last = lax.all_gather(last, AXES, axis=0, tiled=True)
        groups = {"last": [last.reshape(plan.count, -1, last.shape[1])]}
        att, feed_0 = att[None], feed_0[None]
        att = join(att, plan.swap(att, ROW))
        *come, feed_0, cotangent = together(
            *[plan.swap(att, bit) for bit in STAGE_Z], feed_0, cotangent
        )
        att = join(att, *come)
        ct_own = cotangent[0]
        (ct_away,) = pack(
            row_index,
            [cotangent],
            [away.shape],
            [(0, (0, lambda me: pl.ds((1 - me) * steps, steps)), 0, (slice(None),))],
            (),
            "pack_cotangent",
        )
        come, other, *feed_come, ct_away = together(
            plan.swap(att, COLUMN),
            plan.swap(away, ROW),
            *[plan.swap(feed_0, bit) for bit in STAGE_Z],
            ct_away,
        )
        ct_other = plan.swap(ct_away, ROW)
        att = join(att, come)
        parts = [feed_0] + feed_come
        part_a = join(*[item[:, :, :width] for item in parts])
        part_b = join(*[item[:, :, width:] for item in parts])
        att_come, *come = together(
            plan.swap(att, CORE), plan.swap(part_a, COLUMN), plan.swap(part_b, ROW)
        )
        groups["att0"] = [att, att_come]
        part_a, part_b = join(part_a, come[0]), join(part_b, come[1])
        moving = [plan.swap(part_a, ROW), plan.swap(part_b, COLUMN)]
        waits = (part_a, part_b)
        place = jnp.broadcast_to(table[FROM_C][:, None], (slabs, LANES))
        unpacked = unpack(place, groups["att0"], model, width)
        vecs, biases = unpacked[:2], unpacked[2:]
        blocks = cube_weights(shapes, w_out.shape[1] // w_in.shape[1])
    else:
        own, other = to_frames(plan, tokens[0])
        table = jnp.zeros((8, clips), jnp.int32).at[CLIP_LENGTHS].set(own_lengths)
        small = jnp.concatenate([norm_gain.reshape(-1), norm_bias.reshape(-1), b_in.reshape(-1)])
        groups, blocks, small_all = plain_weights(plan, weights, small)
        gains = small_all[:, :cut].reshape(plan.count, 2, 2, wide)
        shifts = small_all[:, cut : 2 * cut].reshape(plan.count, 2, 2, wide)
        gains = gains.transpose(1, 2, 0, 3).reshape(2, 2, model)
        shifts = shifts.transpose(1, 2, 0, 3).reshape(2, 2, model)
        vecs = jnp.stack([gains, shifts], 2).reshape(2, 4, model)
        biases = small_all[:, 2 * cut :]
        biases = biases.reshape(plan.count, 2, -1).transpose(1, 0, 2).reshape(2, 1, width)

    middle, normed_0, mixed, attended, prob = spatial_forward(
        table, groups, blocks[0][:2], own, other, vecs[0], waits
    )
    frames, patches = middle.shape[:2]
    count = frames * patches
    middle = middle.reshape(count, model)
    if plan.cube:
        *moving, middle = together(*moving, middle)
        part_a, part_b = join(part_a, moving[0]), join(part_b, moving[1])
        groups["in0"] = [part_a, plan.swap(part_a, CORE)]
        groups["out0"] = [part_b, plan.swap(part_b, CORE)]
    result, second_0, hidden, slope = feed_forward(
        table, groups, blocks[0][2:], middle, vecs[0], biases[0]
    )
    if plan.cube:
        ct_other, result = together(ct_other, result)
    else:
        ct_own, ct_other = to_frames(plan, cotangent[0])
    rows = regroup(plan, result.reshape(frames, patches, model), 1, 0)
    if plan.seq != 2:
        full = regroup(plan, jnp.concatenate([ct_own, ct_other], 1), 1, 0)
        cut_at = full.shape[1] // 2
        ct_own, ct_other = full[:, :cut_at], full[:, cut_at:]
    (
        active_own,
        *active_other,
        grad,
        small_1,
        normed_1,
        attended_1,
        second_1,
        hidden_1,
        branch_1,
        grad_pre_1,
        proj_in_1,
        grad_mixed_1,
    ) = temporal_block(
        table, groups, blocks[1], rows, ct_own, ct_other, vecs[1], biases[1], clips
    )
    grad = regroup(plan, grad, 0, 1).reshape(count, model)

    def flat(values):
        return values.reshape(count, values.shape[-1])

    pairs_1 = [
        (normed_1, grad_mixed_1, False),
        (attended_1, proj_in_1, False),
        (second_1, grad_pre_1, False),
        (hidden_1, branch_1, True),
    ]
    waits = ()
    if plan.cube:
        g_last, over = weight_grads(table, AS_IS, 1, slabs, pairs_1, "grads_last")
        s_last = lax.psum_scatter(
            g_last.reshape(model, -1), AXES, scatter_dimension=0, tiled=True
        )
        active_come = [plan.swap(item, ROW) for item in active_other]
        waits = (over,)

    grad_middle, proj_in_0, branch_0, grad_pre_0, small_0 = feed_backward(
        table, groups, blocks[0][2:], grad, middle, slope, vecs[0], waits
    )
    pairs_0 = [
        (flat(attended), proj_in_0, False),
        (second_0, grad_pre_0, False),
        (hidden, branch_0, True),
    ]
    waits = ()
    if plan.cube:
        active_come[0], branch_0 = together(active_come[0], branch_0)
        pairs_0[2] = (hidden, branch_0, True)
        keep, send, _ = weight_grads(table, PLACE, 2, slabs, pairs_0, "grads_feed")
        active_come[1], send = together(active_come[1], send)
        s_feed = Sum(plan, keep, send, (model + 2 * width) // 3)
        s_feed.add_core(s_feed.send_core())
        feed_come = s_feed.send_first()
        activations = put_back(table, active_own, active_come, 1)
        waits = (*s_feed.keep, activations)
    grad_own, grad_early, grad_late, grad_mixed_0, tiny_0 = spatial_backward(
        table,
        groups,
        blocks[0][:2],
        grad_middle.reshape(frames, patches, model),
        own,
        other,
        mixed,
        prob,
        vecs[0],
        waits,
    )
    pairs_2 = [(flat(normed_0), flat(grad_mixed_0), False)]
    if plan.cube:
        *feed_come, grad_early = together(*feed_come, grad_early)
        s_feed.add_first(feed_come)
        tokens_come = [plan.swap(grad_early, ROW)]
        feed_come = s_feed.send_second()
        keep, send, _ = weight_grads(
            table,
            PLACE,
            2,
            slabs,
            pairs_2,
            "grads_attention",
            (tiny_0, small_0, small_1),
            s_feed.keep,
        )
        *feed_come, tokens_come[0], grad_late, send = together(
            *feed_come, *tokens_come, grad_late, send
        )
        s_att = Sum(plan, keep, send, 2 * model)
        tokens_come.append(plan.swap(grad_late, ROW))
        s_att.add_core(s_att.send_core())
        att_come = s_att.send_first()
        s_feed.add_second(feed_come)
        feed_come = s_feed.send_last()
        s_att.add_first(together(*att_come))
        att_come = s_att.send_second()
        feed_come[0], feed_come[1], *att_come = together(feed_come[0], feed_come[1], *att_come)
        s_att.add_second(att_come)
        grad_tokens = put_back(table, grad_own, tokens_come, 0)
        *att_come, feed_come[2], grad_tokens, s_last = together(
            *s_att.send_last(), feed_come[2], grad_tokens, s_last
        )
        outs = finish(
            [
                s_att.keep,
                *att_come,
                s_feed.keep,
                *feed_come,
                s_last,
            ],
            [
                norm_gain.shape,
                norm_bias.shape,
                w_qkv.shape,
                w_proj.shape,
                w_in.shape,
                b_in.shape,
                w_out.shape,
            ],
        )
        return (activations[None], grad_tokens[None], *outs)

    active = regroup(plan, jnp.concatenate([active_own[:steps], *active_other], 1), 0, 1)
    half = active.shape[1] // 2
    activations = from_frames(plan, active[:, :half], active[:, half:])
    grad_other = jnp.concatenate([grad_early, grad_late], 0)[:frames]
    grad_tokens = from_frames(plan, grad_own, grad_other)
    each = [(pairs_2 + pairs_0), pairs_1]
    sums = [
        tuple(plain_grad(*each[block][item][:2]) for block in range(2)) for item in range(4)
    ]
    tiny_0, small_0, small_1 = [jnp.sum(item, 0) for item in (tiny_0, small_0, small_1)]
    far = 2 * model + width
    columns = [
        tiny_0[:model],
        small_0[:model],
        small_1[far : far + model],
        small_1[:model],
        tiny_0[model:],
        small_0[model : 2 * model],
        small_1[far + model :],
        small_1[model : 2 * model],
        small_0[2 * model :],
        small_1[2 * model : far],
    ]
    smalls = jnp.concatenate([item.reshape(plan.count, -1) for item in columns], 1)
    mine = lax.psum_scatter(smalls, AXES, scatter_dimension=0, tiled=True).reshape(-1)
    grad_gain = mine[:cut].reshape(2, 2, wide)
    grad_shift = mine[cut : 2 * cut].reshape(2, 2, wide)
    grad_b_in = mine[2 * cut :].reshape(2, -1)
    return (
        activations[None],
        grad_tokens[None],
        grad_gain,
        grad_shift,
        jnp.stack(sums[0]),
        jnp.stack(sums[1]),
        jnp.stack(sums[2]),
        grad_b_in,
        jnp.stack(sums[3]),
    )


def solution(mesh):
    in_specs = (
        P("dp", None, "seq", None),
        P("dp", None, None),
        P("dp", None, "seq", None),
        P(None, None, AXES),
        P(None, None, AXES),
        P(None, AXES, None),
        P(None, AXES, None),
        P(None, AXES, None),
        P(None, AXES),
        P(None, AXES, None),
    )
    out_specs = (
        P("dp", None, "seq", None),
        P("dp", None, "seq", None),
        P(None, None, AXES),
        P(None, None, AXES),
        P(None, AXES, None),
        P(None, AXES, None),
        P(None, AXES, None),
        P(None, AXES),
        P(None, AXES, None),
    )
    return jax.shard_map(
        functools.partial(on_device, Plan(mesh)),
        mesh=mesh,
        in_specs=in_specs,
        out_specs=out_specs,
        check_vma=False,
    )
```
